128 devices in a mesh: seq: 8 (over z, core), mp: 16 (over y, x).
Axes of the slice: x: 4, y: 4, z: 4, core: 2. Of those that a mesh axis runs over, the one named last changes fastest.
Arguments:
- tokens: float32 [2, 4096, 1536], P(None, 'seq'), may hold values from -6 to 6
- cotangent: float32 [2, 4096, 1536], P(None, 'seq'), may hold values from -6 to 6
- lengths: int32 [2], replicated, may hold values from 1024 to 4096, as said below
- adapter_ids: int32 [2], replicated, may hold values from 0 to 7
- mix_gain: float32 [2, 1536], replicated, may hold values from 0.5 to 1.5
- ffn_gain: float32 [2, 1536], replicated, may hold values from 0.5 to 1.5
- w_branch: bfloat16 [2, 1536, 2048], P(None, None, 'mp'), may hold values from -0.15625 to 0.15625
- input_weight: bfloat16 [2, 1536, 2048], P(None, None, 'mp'), may hold values from -0.3125 to 0.3125
- conv_weight: float32 [2, 4, 2048], P(None, None, 'mp'), may hold values from -6 to 6
- conv_bias: float32 [2, 2048], P(None, 'mp'), may hold values from -3 to 3
- gate_a_weight: bfloat16 [2, 16, 128, 128], P(None, 'mp'), may hold values from -0.5 to 0.5
- gate_a_bias: float32 [2, 2048], P(None, 'mp'), may hold values from -4 to 4
- gate_i_weight: bfloat16 [2, 16, 128, 128], P(None, 'mp'), may hold values from -0.5 to 0.5
- gate_i_bias: float32 [2, 2048], P(None, 'mp'), may hold values from -4 to 4
- decay_param: float32 [2, 2048], P(None, 'mp'), may hold values from -12 to -4.7
- w_out: bfloat16 [2, 2048, 1536], P(None, 'mp'), may hold values from -0.125 to 0.125
- w_gate: bfloat16 [2, 1536, 4608], P(None, None, 'mp'), may hold values from -0.15625 to 0.15625
- w_up: bfloat16 [2, 1536, 4608], P(None, None, 'mp'), may hold values from -0.15625 to 0.15625
- w_down: bfloat16 [2, 4608, 1536], P(None, 'mp'), may hold values from -0.09375 to 0.09375
- mix_down: bfloat16 [2, 8, 1536, 32], replicated, may hold values from -0.15625 to 0.15625
- mix_up: bfloat16 [2, 8, 2, 16, 2048], P(None, None, None, None, 'mp'), may hold values from -0.75 to 0.75
- out_down: bfloat16 [2, 8, 2048, 16], P(None, None, 'mp'), may hold values from -0.125 to 0.125
- out_up: bfloat16 [2, 8, 16, 1536], replicated, may hold values from -0.75 to 0.75
- ffn_down: bfloat16 [2, 8, 1536, 32], replicated, may hold values from -0.15625 to 0.15625
- ffn_up: bfloat16 [2, 8, 2, 16, 4608], P(None, None, None, None, 'mp'), may hold values from -0.75 to 0.75
- back_down: bfloat16 [2, 8, 4608, 16], P(None, None, 'mp'), may hold values from -0.09375 to 0.09375
- back_up: bfloat16 [2, 8, 16, 1536], replicated, may hold values from -0.75 to 0.75
Outputs:
- output: float32 [2, 4096, 1536], P(None, 'seq')
- grad_tokens: float32 [2, 4096, 1536], P(None, 'seq')
- grad_mix_down: float32 [2, 8, 1536, 32], replicated
- grad_mix_up: float32 [2, 8, 2, 16, 2048], replicated
- grad_out_down: float32 [2, 8, 2048, 16], replicated
- grad_out_up: float32 [2, 8, 16, 1536], replicated
- grad_ffn_down: float32 [2, 8, 1536, 32], replicated
- grad_ffn_up: float32 [2, 8, 2, 16, 4608], replicated
- grad_back_down: float32 [2, 8, 4608, 16], replicated
- grad_back_up: float32 [2, 8, 16, 1536], replicated
The draws below stay inside these ranges and needn't reach their ends.
Inputs may be any that keep to these rules, and one draw needn't show every extreme that they name: `lengths`: one sequence, drawn from the seed, has length 4096.
All inputs are finite; a program needn't handle non-finite values.
Results may differ from the reference program's by a relative error of at most 0.014.
Values may be sent and summed in bfloat16 or wider, within the bound.
No kernel may reach another device: no remote copies, remote signals or barrier semaphores. Data moves between devices by JAX's collectives and lax.ppermute only.
A program may use at most 448 MiB of HBM per device.

```python
import jax
import jax.numpy as jnp
from jax import lax

D = 1536
RW = 2048
FF = 4608
HEAD_DIM = 128
CONV = 4
RANK = 16
ADAPTERS = 8
LAYERS = 2
SEQS = 2
LEN = 4096
HEADS = 16
GROUP = 512


def draw_tokens(key, part):
    key = jax.random.fold_in(key, 37)
    noise_key, common_key = jax.random.split(key)
    noise = jax.random.normal(noise_key, (SEQS, LEN // GROUP, GROUP, D), jnp.float32)
    common = 2.0 * jax.random.normal(common_key, (SEQS, LEN // GROUP, 1, D), jnp.float32)
    values = (noise + common).reshape(SEQS, LEN, D)
    return jnp.clip(values, -6.0, 6.0).astype(jnp.float32)


def draw_lengths(key, part):
    key = jax.random.fold_in(key, 11)
    pick_key, others_key = jax.random.split(key)
    longest = jax.random.randint(pick_key, (), 0, SEQS)
    others = jax.random.randint(others_key, (SEQS,), LEN // 4, LEN + 1)
    return jnp.where(jnp.arange(SEQS) == longest, LEN, others).astype(jnp.int32)


def draw_decay_param(key, part):
    key = jax.random.fold_in(key, 23)
    first_key = jax.random.fold_in(key, 0)
    uniform_part = jax.random.uniform(first_key, (LAYERS, RW), jnp.float32)
    slowest = jnp.log(1.0 / (4.0 * LEN))
    fastest = jnp.log(1.0 / 30.0)
    forget_rate = jnp.exp(slowest + uniform_part * (fastest - slowest))
    return jnp.log(jnp.expm1(forget_rate / 4.0)).astype(jnp.float32)


def steps_of(rng, extent, pieces, low, high):
    level, own = 1.0, jax.random.fold_in(rng, 6)
    for dim, shards_of in pieces:
        heights = jnp.exp(jax.random.uniform(jax.random.fold_in(own, dim), (shards_of,), jnp.float32, low / len(pieces), high / len(pieces)))
        level = level * jnp.repeat(heights, extent[dim] // shards_of).reshape([-1 if axis == dim else 1 for axis in range(len(extent))])
    return level


def centred(rng, dims, width, reach, cuts=(), kind=jnp.bfloat16):
    entries = jax.random.normal(rng, dims, jnp.float32) * width
    if len(cuts) > 0:
        entries = steps_of(rng, dims, cuts, -0.22, 0.18) * entries
    return jnp.clip(entries, min=-reach, max=reach).astype(kind)


def setup_inputs(seed: int = 0) -> dict:
    streams_of = jax.random.split(jax.random.key(seed), 28)
    tokens = draw_tokens(jax.random.fold_in(streams_of[27], 71), 0)
    cotangent = centred(streams_of[1], (SEQS, LEN, D), 1.0, 6.0, ((1, 8),), jnp.float32)
    lengths = draw_lengths(jax.random.fold_in(streams_of[27], 71), 0)
    adapter_ids = jax.random.randint(streams_of[3], (SEQS,), 0, ADAPTERS).astype(jnp.int32)
    mix_gain = jnp.clip(1.0 + 0.1 * jax.random.normal(streams_of[4], (LAYERS, D), jnp.float32), 0.5, 1.5)
    ffn_gain = jnp.clip(1.0 + 0.1 * jax.random.normal(streams_of[5], (LAYERS, D), jnp.float32), 0.5, 1.5)
    w_branch = centred(streams_of[6], (LAYERS, D, RW), D ** -0.5, 0.15625, ((2, 16),))
    input_weight = centred(streams_of[7], (LAYERS, D, RW), (D // 4) ** -0.5, 0.3125, ((2, 16),))
    conv_weight = centred(streams_of[8], (LAYERS, CONV, RW), 1 ** -0.5, 6.0, ((2, 16),), jnp.float32)
    conv_bias = centred(streams_of[9], (LAYERS, RW), 0.5, 3.0, ((1, 16),), jnp.float32)
    gate_a_weight = centred(streams_of[10], (LAYERS, HEADS, HEAD_DIM, HEAD_DIM), HEAD_DIM ** -0.5, 0.5, ((1, 16),))
    gate_a_bias = centred(streams_of[11], (LAYERS, RW), 1.0, 4.0, ((1, 16),), jnp.float32)
    gate_i_weight = centred(streams_of[12], (LAYERS, HEADS, HEAD_DIM, HEAD_DIM), HEAD_DIM ** -0.5, 0.5, ((1, 16),))
    gate_i_bias = centred(streams_of[13], (LAYERS, RW), 1.0, 4.0, ((1, 16),), jnp.float32)
    decay_param = draw_decay_param(jax.random.fold_in(streams_of[27], 71), 0)
    w_out = centred(streams_of[15], (LAYERS, RW, D), RW ** -0.5, 0.125, ((1, 16),))
    w_gate = centred(streams_of[16], (LAYERS, D, FF), D ** -0.5, 0.15625, ((2, 16),))
    w_up = centred(streams_of[17], (LAYERS, D, FF), D ** -0.5, 0.15625, ((2, 16),))
    w_down = centred(streams_of[18], (LAYERS, FF, D), FF ** -0.5, 0.09375, ((1, 16),))
    mix_down = centred(streams_of[19], (LAYERS, ADAPTERS, D, 2 * RANK), D ** -0.5, 0.15625)
    mix_up = centred(streams_of[20], (LAYERS, ADAPTERS, 2, RANK, RW), (4 * RANK) ** -0.5, 0.75, ((4, 16),))
    out_down = centred(streams_of[21], (LAYERS, ADAPTERS, RW, RANK), RW ** -0.5, 0.125, ((2, 16),))
    out_up = centred(streams_of[22], (LAYERS, ADAPTERS, RANK, D), (4 * RANK) ** -0.5, 0.75)
    ffn_down = centred(streams_of[23], (LAYERS, ADAPTERS, D, 2 * RANK), D ** -0.5, 0.15625)
    ffn_up = centred(streams_of[24], (LAYERS, ADAPTERS, 2, RANK, FF), (4 * RANK) ** -0.5, 0.75, ((4, 16),))
    back_down = centred(streams_of[25], (LAYERS, ADAPTERS, FF, RANK), FF ** -0.5, 0.09375, ((2, 16),))
    back_up = centred(streams_of[26], (LAYERS, ADAPTERS, RANK, D), (4 * RANK) ** -0.5, 0.75)
    return dict(tokens=tokens, cotangent=cotangent, lengths=lengths, adapter_ids=adapter_ids, mix_gain=mix_gain, ffn_gain=ffn_gain, w_branch=w_branch, input_weight=input_weight, conv_weight=conv_weight, conv_bias=conv_bias, gate_a_weight=gate_a_weight, gate_a_bias=gate_a_bias, gate_i_weight=gate_i_weight, gate_i_bias=gate_i_bias, decay_param=decay_param, w_out=w_out, w_gate=w_gate, w_up=w_up, w_down=w_down, mix_down=mix_down, mix_up=mix_up, out_down=out_down, out_up=out_up, ffn_down=ffn_down, ffn_up=ffn_up, back_down=back_down, back_up=back_up)


@jax.custom_vjp
def low(v):
    return lax.optimization_barrier(v.astype(jnp.bfloat16)).astype(jnp.float32)

@jax.custom_vjp
def low_back(v):
    return v

def low_keep(v):
    return (low(v), None)

def low_pass(kept, grad):
    return (grad,)

def back_keep(v):
    return (v, None)

def back_low(kept, grad):
    return (low(grad),)
low.defvjp(low_keep, low_pass)
low_back.defvjp(back_keep, back_low)

def product(left_operand, right_operand):
    return jnp.dot(left_operand, right_operand, precision=lax.Precision.HIGHEST)

def batched(left_operand, right_operand):
    return jnp.einsum('hcr,hry->hcy', left_operand, right_operand, precision=lax.Precision.HIGHEST)

def choose(onehot, table):
    return jnp.einsum('sa,a...->s...', onehot, table, precision=lax.Precision.HIGHEST)

def rms_scale(values, gain_row):
    return values * lax.rsqrt(lax.optimization_barrier(jnp.mean(values * values, axis=-1, keepdims=True)) + 1e-06) * gain_row

def linear_pair(earlier, later):
    return (earlier[0] * later[0], later[0] * earlier[1] + later[1])

def causal_conv(inputs, weight, bias):
    summed = bias + weight[0] * inputs
    for offset in range(1, CONV):
        moved = jnp.pad(inputs, ((0, 0), (offset, 0), (0, 0)))[:, :LEN]
        summed = summed + weight[offset] * moved
    return summed

def block_gate(heads, weight, bias):
    joined = jnp.einsum('slhi,hij->slhj', heads, weight, precision=lax.Precision.HIGHEST)
    return jax.nn.sigmoid(low_back(joined.reshape(SEQS, LEN, RW) + bias))

def mixer_block(residual, onehot, frozen, tables, layer_index):
    down_mix = choose(onehot, tables[0][layer_index])
    up_mix = choose(onehot, tables[1][layer_index])
    down_out = choose(onehot, tables[2][layer_index])
    up_out = choose(onehot, tables[3][layer_index])
    normed = low(rms_scale(residual, frozen[0][layer_index]))
    latent = low(batched(normed, down_mix))
    branch = low_back(product(normed, frozen[2][layer_index]) + batched(latent[..., :RANK], up_mix[:, 0]))
    inputs = low_back(low(product(normed, frozen[3][layer_index]) + batched(latent[..., RANK:], up_mix[:, 1])))
    conv_out = causal_conv(inputs, frozen[4][layer_index], frozen[5][layer_index])
    heads = low(conv_out).reshape(SEQS, LEN, HEADS, HEAD_DIM)
    recurrence_gate = block_gate(heads, frozen[6][layer_index], frozen[7][layer_index])
    gate_i = block_gate(heads, frozen[8][layer_index], frozen[9][layer_index])
    decay_step = jnp.exp(-8.0 * recurrence_gate * jax.nn.softplus(frozen[10][layer_index]))
    first_token = (jnp.arange(LEN) == 0)[None, :, None]
    scale = jnp.where(first_token, 1.0, jnp.sqrt(1.0 - decay_step * decay_step + 0.01))
    driven = conv_out * gate_i * scale
    states = lax.associative_scan(linear_pair, (decay_step, driven), axis=1)[1]
    mixed = low_back(low(states * jax.nn.gelu(branch)))
    out_latent = batched(mixed, down_out)
    return residual + low_back(product(mixed, frozen[11][layer_index]) + batched(out_latent, up_out))

def ffn_block(residual, onehot, frozen, tables, layer_index):
    down_ffn = choose(onehot, tables[4][layer_index])
    up_ffn = choose(onehot, tables[5][layer_index])
    down_back = choose(onehot, tables[6][layer_index])
    up_back = choose(onehot, tables[7][layer_index])
    normed = low(rms_scale(residual, frozen[1][layer_index]))
    latent = low(batched(normed, down_ffn))
    gate_pre = low_back(product(normed, frozen[12][layer_index]) + batched(latent[..., :RANK], up_ffn[:, 0]))
    up_pre = low_back(product(normed, frozen[13][layer_index]) + batched(latent[..., RANK:], up_ffn[:, 1]))
    hidden = low_back(low(jax.nn.gelu(gate_pre) * up_pre))
    back_latent = batched(hidden, down_back)
    return residual + low_back(product(hidden, frozen[14][layer_index]) + batched(back_latent, up_back))

def reference(tokens, cotangent, lengths, adapter_ids, mix_gain, ffn_gain, w_branch, input_weight, conv_weight, conv_bias, gate_a_weight, gate_a_bias, gate_i_weight, gate_i_bias, decay_param, w_out, w_gate, w_up, w_down, mix_down, mix_up, out_down, out_up, ffn_down, ffn_up, back_down, back_up):
    frozen = tuple((member.astype(jnp.float32) for member in (mix_gain, ffn_gain, w_branch, input_weight, conv_weight, conv_bias, gate_a_weight, gate_a_bias, gate_i_weight, gate_i_bias, decay_param, w_out, w_gate, w_up, w_down)))
    tables = tuple((member.astype(jnp.float32) for member in (mix_down, mix_up, out_down, out_up, ffn_down, ffn_up, back_down, back_up)))
    onehot = (adapter_ids[:, None] == jnp.arange(ADAPTERS, dtype=jnp.int32)[None, :]).astype(jnp.float32)
    valid_mask = (jnp.arange(LEN, dtype=jnp.int32)[None, :] < lengths[:, None]).astype(jnp.float32)

    def forward_pass(start_tokens, adapter_tables):
        residual = start_tokens
        for layer_index in range(LAYERS):
            residual = mixer_block(residual, onehot, frozen, adapter_tables, layer_index)
            residual = ffn_block(residual, onehot, frozen, adapter_tables, layer_index)
        return residual * valid_mask[:, :, None]
    output, pullback = jax.vjp(forward_pass, tokens.astype(jnp.float32), tables)
    grad_tokens, grads = pullback(cotangent.astype(jnp.float32))
    return (output, grad_tokens, grads[0], grads[1], grads[2], grads[3], grads[4], grads[5], grads[6], grads[7])
```

```python
import functools

import jax
import jax.numpy as jnp
from jax import lax
from jax.experimental import pallas as pl
from jax.experimental.pallas import tpu as pltpu
from jax.sharding import Mesh
from jax.sharding import PartitionSpec as P

ALL = ("z", "core", "y", "x")
BF = jnp.bfloat16
F32 = jnp.float32
RANK = 16
HOME = 64
BLOCK = 256
GELU_C = 0.7978845608028654


def device_pairs(move):
    pairs = []
    for z in range(4):
        for c in range(2):
            for y in range(4):
                for x in range(4):
                    to = move(z, c, y, x)
                    if to is not None:
                        a = ((z * 2 + c) * 4 + y) * 4 + x
                        b = ((to[0] * 2 + to[1]) * 4 + to[2]) * 4 + to[3]
                        pairs.append((a, b))
    return pairs


def send(value, move):
    return lax.ppermute(value, ALL, device_pairs(move))


def along_x(d):
    return lambda z, c, y, x: (z, c, y, (x + d) % 4)


def along_y(d):
    return lambda z, c, y, x: (z, c, (y + d) % 4, x)


def ffn_rows(d):
    return lambda z, c, y, x: (z, c, y, (x + d) % 4) if c == 0 else (z, c, (y + d) % 4, x)


def ffn_shards(d):
    return lambda z, c, y, x: (z, c, (y + d) % 4, x) if c == 0 else (z, c, y, (x + d) % 4)


def shard_groups():
    at = lambda z, c, y, x: ((z * 2 + c) * 4 + y) * 4 + x
    columns = [[at(z, 0, y, x) for y in range(4)] for z in range(4) for x in range(4)]
    rows = [[at(z, 1, y, x) for x in range(4)] for z in range(4) for y in range(4)]
    return columns + rows


def gather4(value, moves):
    return [value] + [send(value, moves(j)) for j in (1, 2, 3)]


def scatter4(parts, moves):
    moved = [send(parts[j], moves(-j)) for j in (1, 2, 3)]
    total = parts[0].astype(F32)
    for part in moved:
        total = total + part.astype(F32)
    return total


def ring_order(blocks, index, ahead=False):
    if not ahead:
        blocks = [blocks[0], blocks[3], blocks[2], blocks[1]]
    joined = jnp.stack(list(blocks) + list(blocks[:3]))
    return lax.dynamic_slice_in_dim(joined, (-index) % 4, 4, 0)


def split3(v):
    high = lax.reduce_precision(v, 8, 7)
    rest = v - high
    mid = lax.reduce_precision(rest, 8, 7)
    return high.astype(BF), mid.astype(BF), (rest - mid).astype(BF)


def combine(earlier, later):
    return (earlier[0] * later[0], later[0] * earlier[1] + later[1])


def next_block(reverse):
    def move(z, c, y, x):
        at = (z * 2 + c) * 2 + y % 2 + (-1 if reverse else 1)
        if not 0 <= at < 16:
            return None
        return (at // 4, (at // 2) % 2, (y // 2) * 2 + at % 2, x)

    return move


def entering(total, state, core, half, reverse):
    own = jnp.stack([total, state])
    one = jnp.stack([jnp.ones_like(total), jnp.zeros_like(state)])

    def step(own, other, later):
        pre = jnp.where(later, other, one)
        first, second = jnp.where(later, other, own), jnp.where(later, own, other)
        both = combine((first[0], first[1]), (second[0], second[1]))
        return pre, jnp.stack(both)

    other = send(own, lambda z, c, y, x: (z, c, y ^ 1, x))
    pre_h, own = step(own, other, half == (0 if reverse else 1))
    other = send(own, lambda z, c, y, x: (z, 1 - c, y, x))
    pre_c, own = step(own, other, core == (0 if reverse else 1))
    far = []
    for d in (1, 2, 3):
        e = -d if reverse else d
        far.append(
            send(own, lambda z, c, y, x, e=e: (z + e, c, y, x) if 0 <= z + e < 4 else None)
        )
    state = far[2][1]
    for part in (far[1], far[0], pre_c, pre_h):
        state = part[0] * state + part[1]
    return state


def scan_kernel(reverse, a_ref, b_ref, cum_ref, out_ref):
    rows, width = a_ref.shape
    row = lax.broadcasted_iota(jnp.int32, (8, width), 0)
    groups = rows // 8

    def body(i, carry):
        ca, cb = carry
        at = pl.multiple_of((groups - 1 - i if reverse else i) * 8, 8)
        a, b = a_ref[pl.ds(at, 8), :], b_ref[pl.ds(at, 8), :]
        for k in (1, 2, 4):
            seen = row < 8 - k if reverse else row >= k
            by = 8 - k if reverse else k
            pa = jnp.where(seen, pltpu.roll(a, by, 0), 1.0)
            pb = jnp.where(seen, pltpu.roll(b, by, 0), 0.0)
            b = a * pb + b
            a = a * pa
        b = a * cb + b
        a = a * ca
        cum_ref[pl.ds(at, 8), :] = a
        out_ref[pl.ds(at, 8), :] = b
        last = 0 if reverse else 7
        return (
            jnp.broadcast_to(a[last : last + 1], a.shape),
            jnp.broadcast_to(b[last : last + 1], b.shape),
        )

    start = (jnp.ones((8, width), F32), jnp.zeros((8, width), F32))
    lax.fori_loop(0, groups, body, start, unroll=4)


def local_scan(a, b, reverse):
    shape = jax.ShapeDtypeStruct(a.shape, F32)
    return pl.pallas_call(
        functools.partial(scan_kernel, reverse),
        out_shape=(shape, shape),
        in_specs=[pl.BlockSpec(memory_space=pltpu.VMEM)] * 2,
        out_specs=[pl.BlockSpec(memory_space=pltpu.VMEM)] * 2,
        cost_estimate=pl.CostEstimate(
            flops=20 * a.size, bytes_accessed=16 * a.size, transcendentals=0
        ),
        name="scan_back" if reverse else "scan",
    )(a, b)


def nn(a, b):
    return jnp.dot(a, b, preferred_element_type=F32)


def nt(a, b):
    return lax.dot_general(a, b, (((1,), (1,)), ((), ())), preferred_element_type=F32)


def tn(a, b):
    return lax.dot_general(a, b, (((0,), (0,)), ((), ())), preferred_element_type=F32)


def gelu_pair(v):
    t = jnp.tanh(GELU_C * (v + 0.044715 * v * v * v))
    act = 0.5 * v * (1.0 + t)
    pull = 0.5 * (1.0 + t) + 0.5 * v * (1.0 - t * t) * (GELU_C * (1.0 + 0.134145 * v * v))
    return act, pull


def inverse_rms(v):
    return lax.rsqrt(jnp.mean(v * v, axis=-1, keepdims=True) + 1e-06)


def rms_backward(v, inverse, gain, grad):
    scaled = grad * gain
    return inverse * scaled - v * inverse**3 * jnp.mean(v * scaled, axis=-1, keepdims=True)


def pick(table, ids):
    return jnp.stack(
        [lax.dynamic_index_in_dim(table, ids[s], 1, keepdims=False) for s in range(2)], axis=1
    )


def other_core(z, c, y, x):
    return (z, 1 - c, y, x)


def other_half(z, c, y, x):
    return (z, c, y ^ 1, x)


def along_z(d):
    return lambda z, c, y, x: ((z + d) % 4, c, y, x)


def halves(value, index, move):
    count = value.shape[0] // 2
    mine = lax.dynamic_slice_in_dim(value, index * count, count, 0)
    theirs = lax.dynamic_slice_in_dim(value, (1 - index) * count, count, 0)
    return mine.astype(F32) + send(theirs, move).astype(F32)


def ring_scatter(value, index, moves, axis):
    count = value.shape[axis] // 4
    parts = [
        lax.dynamic_slice_in_dim(value, ((index - j) % 4) * count, count, axis) for j in range(4)
    ]
    return scatter4(parts, moves)


def sum_z(value):
    total = value
    for d in (1, 2, 3):
        total = total + send(value, along_z(d))
    return total


def reduce_mix(whole, split):
    core, x, y = lax.axis_index("core"), lax.axis_index("x"), lax.axis_index("y")
    part = halves(jnp.concatenate([whole, split], axis=1).astype(BF), core, other_core)
    split = part[:, 1536:]
    whole = ring_scatter(part[:, :1536].astype(BF), x, along_x, 1)
    part = halves(jnp.concatenate([whole, split], axis=1), y % 2, other_half)
    part = sum_z(part).astype(BF)
    part = ring_order(gather4(part, along_y), y)
    part = ring_order(gather4(part, along_x), x)
    both = send(part, other_core)
    first = jnp.where(core == 0, part, both)
    second = jnp.where(core == 0, both, part)
    joined = jnp.stack([first, second]).astype(F32)
    joined = joined.reshape(2, 4, 2, 2, 12, 896).transpose(2, 0, 3, 4, 1, 5)
    joined = joined.reshape(2, 48, 4, 896)
    whole = joined[..., :384].reshape(2, 48, 1536)
    split = joined[..., 384:].reshape(2, 48, 4, 4, 128)
    return whole, split.transpose(0, 1, 3, 2, 4).reshape(2, 48, 2048)


def reduce_early(whole_1, shards_1, whole_0, shards_0, mix_whole, mix_split):
    core, x, y = lax.axis_index("core"), lax.axis_index("x"), lax.axis_index("y")
    seq = y // 2
    both = lambda v: jnp.concatenate([jnp.where(seq == s, v, 0.0) for s in range(2)], axis=0)
    whole = jnp.concatenate([whole_1, whole_0, both(mix_whole)], axis=0)
    whole = halves(whole.astype(BF), core, other_core)
    whole = ring_scatter(whole.astype(BF), x, along_x, 1)
    whole = ring_scatter(whole.astype(BF), y, along_y, 0)
    shard = jnp.concatenate([shards_1, shards_0], axis=1)
    group = jnp.where(core == 0, y, x)
    shard = ring_scatter(shard.astype(BF), group, ffn_shards, 0)[0]
    shard = halves(shard, core, other_core)
    split = ring_scatter(both(mix_split), y, along_y, 1)
    split = halves(split, core, other_core)
    flat = jnp.concatenate(
        [whole.reshape(108, 128), shard.reshape(216, 128), split], axis=0
    )
    flat = sum_z(flat).astype(BF)
    flat = lax.all_gather(flat, ("core", "y", "x")).reshape(2, 4, 4, 372, 128).astype(F32)
    whole = flat[:, :, :, :108].reshape(2, 4, 4, 36, 384).transpose(0, 1, 3, 2, 4)
    whole = whole.reshape(288, 1536)
    shard = flat[:, :, :, 108:324].reshape(2, 4, 4, 96, 288).transpose(0, 3, 1, 2, 4)
    shard = shard.reshape(192, 4608)
    split = flat[:, :, :, 324:].reshape(2, 4, 4, 48, 128).transpose(0, 3, 1, 2, 4)
    split = split.reshape(2, 48, 2048)
    return (
        (whole[:96], shard[:96]),
        (whole[96:192], shard[96:]),
        (whole[192:].reshape(2, 48, 1536), split),
    )


def shards(
    tokens,
    cotangent,
    lengths,
    adapter_ids,
    mix_gain,
    ffn_gain,
    w_branch,
    input_weight,
    conv_weight,
    conv_bias,
    gate_a_weight,
    gate_a_bias,
    gate_i_weight,
    gate_i_bias,
    decay_param,
    w_out,
    w_gate,
    w_up,
    w_down,
    mix_down,
    mix_up,
    out_down,
    out_up,
    ffn_down,
    ffn_up,
    back_down,
    back_up,
):
    width = tokens.shape[2]
    z, core = lax.axis_index("z"), lax.axis_index("core")
    y, x = lax.axis_index("y"), lax.axis_index("x")
    seq, half = y // 2, y % 2
    mix_down_t = pick(jnp.swapaxes(mix_down, 2, 3), adapter_ids)
    ffn_down_t = pick(jnp.swapaxes(ffn_down, 2, 3), adapter_ids)
    out_up_s = pick(out_up, adapter_ids)
    back_up_s = pick(back_up, adapter_ids)
    mix_up_s = pick(mix_up, adapter_ids).reshape(2, 64, 128)
    out_down_s = pick(jnp.swapaxes(out_down, 2, 3), adapter_ids).reshape(2, 32, 128)
    ffn_up_s = pick(ffn_up, adapter_ids)
    back_down_s = pick(jnp.swapaxes(back_down, 2, 3), adapter_ids)
    own = lambda table: lax.dynamic_index_in_dim(table, seq, 0, keepdims=False)
    ffn_group = jnp.where(core == 0, y, x)
    small32 = jnp.concatenate(
        [
            conv_weight,
            conv_bias[:, None],
            gate_a_bias[:, None],
            gate_i_bias[:, None],
            decay_param[:, None],
        ],
        axis=1,
    )
    small = jnp.concatenate(
        [gate_a_weight[:, 0], gate_i_weight[:, 0], mix_up_s, out_down_s, *split3(small32)], axis=1
    )
    small = ring_order(gather4(small, along_y), y)
    small32 = (
        small[:, :, 352:360].astype(F32)
        + small[:, :, 360:368].astype(F32)
        + small[:, :, 368:].astype(F32)
    )
    small16 = small[:, :, :352]
    ffn_small = jnp.concatenate(
        [
            ffn_up_s.transpose(0, 2, 1, 3, 4).reshape(2, 64, 288),
            back_down_s.reshape(2, 32, 288),
        ],
        axis=1,
    )
    ffn_a = ring_order(gather4(ffn_small, ffn_shards), ffn_group)
    ffn_packs = [
        jnp.concatenate([w_gate[l].T, w_up[l].T, w_down[l]], axis=0) for l in range(2)
    ]
    gather_ffn = lambda pack: lax.all_gather(
        pack, ALL, axis=0, axis_index_groups=shard_groups()
    )
    w_pair = [jnp.concatenate([w_branch[l].T, input_weight[l].T], axis=0) for l in range(2)]
    ffn_w = [gather_ffn(ffn_packs[0]), None]
    w_back = [ring_order(gather4(w_out[0], along_y), y).reshape(512, width), None]
    w_in = [None, None]
    start = (seq, half * BLOCK + x * HOME, 0)
    residual = lax.dynamic_slice(tokens, start, (1, HOME, width))[0]
    position = (z * 2 + core) * 512 + half * BLOCK + x * HOME + jnp.arange(HOME)
    valid = (position < lengths[seq]).astype(F32)[:, None]
    row = jnp.arange(BLOCK)[:, None]
    first = (row == 0) & (z == 0) & (core == 0) & (half == 0)
    of_rows = jnp.where(core == 0, y, (y - jnp.arange(4)) % 4) // 2
    of_rows = jnp.repeat(of_rows, HOME)[:, None]
    of_cols = (jnp.arange(64) // 16) % 2
    mask = (of_rows == of_cols[None, :]).astype(F32)
    mask_back = mask[:, :32]

    def in_order(blocks):
        joined = jnp.concatenate([blocks[i] for i in (0, 3, 2, 1, 0, 3, 2)], axis=0)
        return lax.dynamic_slice(joined, (((-x) % 4) * HOME, 0), (BLOCK, joined.shape[1]))

    def ordered_parts(total):
        low = total.astype(BF)
        return [
            lax.dynamic_slice(low, (((x - j) % 4) * HOME, 0), (HOME, width)) for j in range(4)
        ]

    kept = []
    for l in range(2):
        k = {"residual": residual}
        k["inverse"] = inverse_rms(residual)
        if l == 0:
            everything = (tokens * inverse_rms(tokens) * mix_gain[0]).astype(BF)
            normed = lax.dynamic_slice(everything, (seq, half * BLOCK, 0), (1, BLOCK, width))[0]
        else:
            normed = (residual * k["inverse"] * mix_gain[l]).astype(BF)
            normed = in_order(gather4(normed, along_x))
        k["normed"] = normed
        down = own(mix_down_t[l])
        latent = nt(normed, down).astype(BF)
        k["latent"] = latent
        up = lax.dynamic_slice(small16[:, l, 256:320], (0, seq * 32, 0), (4, 32, 128))
        up = up.transpose(1, 0, 2).reshape(32, 512)
        down_out = lax.dynamic_slice(small16[:, l, 320:352], (0, seq * 16, 0), (4, 16, 128))
        down_out = down_out.transpose(1, 0, 2).reshape(16, 512)
        k["up"], k["down_out"], k["down"] = up, down_out, down
        if l == 0:
            own_up = mix_up_s[0].reshape(2, 2, RANK, 128)
            local = []
            for i in range(2):
                low = nt(everything[i], mix_down_t[0, i]).astype(BF)
                both = nt(everything[i], w_pair[0])
                local.append(
                    jnp.concatenate(
                        [
                            both[:, :128] + nn(low[:, :RANK], own_up[i, 0]),
                            both[:, 128:] + nn(low[:, RANK:], own_up[i, 1]),
                        ],
                        axis=1,
                    )
                )
            local = jnp.concatenate(local, axis=0).astype(BF)
            local = [
                lax.dynamic_slice_in_dim(local, ((y - j) % 4) * BLOCK, BLOCK, 0) for j in range(4)
            ]
            moved = [local[0]] + [send(local[j], along_y(-j)) for j in (1, 2, 3)]
            moved = ring_order(moved, y, ahead=True)
            moved = moved.transpose(1, 0, 2).reshape(BLOCK, 4, 2, 128)
            branch = moved[:, :, 0].reshape(BLOCK, 512).astype(F32)
            inputs = moved[:, :, 1].reshape(BLOCK, 512)
        else:
            both = nt(normed, w_in[l]).reshape(BLOCK, 4, 2, 128)
            branch = both[:, :, 0].reshape(BLOCK, 512) + nn(latent[:, :RANK], up[:RANK])
            inputs = both[:, :, 1].reshape(BLOCK, 512) + nn(latent[:, RANK:], up[RANK:])
            inputs = inputs.astype(BF)
        halo = send(inputs[BLOCK - 3 :], next_block(False))
        params = small32[:, l].transpose(1, 0, 2).reshape(8, 512)
        taps = params[:4]
        k["taps"] = taps
        extended = jnp.concatenate([halo, inputs], axis=0).astype(F32)
        conv = params[4] + taps[0] * extended[3 : 3 + BLOCK]
        for o in (1, 2, 3):
            conv = conv + taps[o] * extended[3 - o : 3 - o + BLOCK]
        heads = conv.astype(BF).reshape(BLOCK, 4, 128)
        gw = small16[:, l, :256].reshape(4, 2, 128, 128)
        k["gw"] = gw
        pre_a = jnp.concatenate([nn(heads[:, h], gw[h, 0]) for h in range(4)], axis=1)
        pre_i = jnp.concatenate([nn(heads[:, h], gw[h, 1]) for h in range(4)], axis=1)
        gate_a = jax.nn.sigmoid(pre_a + params[5])
        gate_i = jax.nn.sigmoid(pre_i + params[6])
        rate = -8.0 * jax.nn.softplus(params[7])
        decay = jnp.exp(gate_a * rate)
        scale = jnp.where(first, 1.0, jnp.sqrt(1.0 - decay * decay + 0.01))
        driven = conv * gate_i * scale
        cum, local = local_scan(decay, driven, False)
        carry = entering(cum[-1], local[-1], core, half, False)
        states = local + cum * carry
        act, pull = gelu_pair(branch)
        mixed = (states * act).astype(BF)
        k.update(
            conv=conv,
            gate_a=gate_a,
            gate_i=gate_i,
            rate=rate,
            decay=decay,
            scale=scale,
            total=cum[-1],
            carry=carry,
            states=states,
            act=act,
            pull=pull,
            mixed=mixed,
        )
        out_latent = nt(mixed, down_out).astype(BF)
        k["out_latent"] = out_latent
        k["up_out"] = own(out_up_s[l])
        partial = nn(mixed, w_back[l]) + nn(out_latent, k["up_out"])
        residual = residual + scatter4(ordered_parts(partial), along_x)
        k["residual_one"] = residual
        if l == 0:
            pair, out, residual = lax.optimization_barrier((w_pair[1], w_out[1], residual))
            w_in[1] = lax.all_gather(pair, "y", axis=0, tiled=True)
            w_back[1] = lax.all_gather(out, "y", axis=0, tiled=True)
            pack, _ = lax.optimization_barrier((ffn_packs[1], residual))
            ffn_w[1] = gather_ffn(pack)
        k["inverse_two"] = inverse_rms(residual)
        normed = (residual * k["inverse_two"] * ffn_gain[l]).astype(BF)
        normed = jnp.concatenate(gather4(normed, ffn_rows), axis=0)
        k["normed_two"] = normed
        down = ffn_down_t[l].reshape(2, 2, 16, width).transpose(1, 0, 2, 3).reshape(64, width)
        k["down_two"] = down
        latent = (nt(normed, down) * mask).astype(BF)
        k["latent_two"] = latent
        k["up_back"] = back_up_s[l].reshape(32, width)
        hidden, gates, ups = [], [], []
        partial = 0.0
        back_latent = 0.0
        for j in range(4):
            w, a = ffn_w[l][j], ffn_a[j, l]
            g = nt(normed, w[:288]) + nn(latent[:, :32], a[:32])
            u = nt(normed, w[288:576]) + nn(latent[:, 32:], a[32:64])
            h = (gelu_pair(g)[0] * u).astype(BF)
            back_latent = back_latent + nt(h, a[64:])
            partial = partial + nn(h, w[576:])
            gates.append(g)
            ups.append(u)
            hidden.append(h)
        back_latent = (back_latent * mask_back).astype(BF)
        k.update(gates=gates, ups=ups, hidden=hidden, back_latent=back_latent)
        partial = (partial + nn(back_latent, k["up_back"])).astype(BF)
        residual = residual + scatter4(
            [partial[j * HOME : (j + 1) * HOME] for j in range(4)], ffn_rows
        )
        kept.append(k)
    output = lax.all_gather((residual * valid).astype(BF), ("y", "x"), axis=0, tiled=True)
    w_in[0] = lax.all_gather(w_pair[0], "y", axis=0, tiled=True)
    grad = lax.dynamic_slice(cotangent, start, (1, HOME, width))[0] * valid

    ffn_sums, mix_sums = [None, None], [None, None]
    for l in (1, 0):
        k = kept[l]
        rows = jnp.concatenate(gather4(grad.astype(BF), ffn_rows), axis=0)
        g_up_back = tn(k["back_latent"], rows)
        g_back_latent = (nt(rows, k["up_back"]) * mask_back).astype(BF)
        g_latent_gate, g_latent_up, g_normed = 0.0, 0.0, 0.0
        g_shards = []
        for j in range(4):
            w, a = ffn_w[l][j], ffn_a[j, l]
            g_hidden = (nt(rows, w[576:]) + nn(g_back_latent, a[64:])).astype(BF).astype(F32)
            act, pull = gelu_pair(k["gates"][j])
            g_gate = (g_hidden * k["ups"][j] * pull).astype(BF)
            g_up = (g_hidden * act).astype(BF)
            g_shards.append(
                jnp.concatenate(
                    [
                        tn(k["latent_two"][:, :32], g_gate),
                        tn(k["latent_two"][:, 32:], g_up),
                        tn(g_back_latent, k["hidden"][j]),
                    ],
                    axis=0,
                )
            )
            g_latent_gate = g_latent_gate + nt(g_gate, a[:32])
            g_latent_up = g_latent_up + nt(g_up, a[32:64])
            g_normed = g_normed + nn(g_gate, w[:288]) + nn(g_up, w[288:576])
        g_latent = (jnp.concatenate([g_latent_gate, g_latent_up], axis=1) * mask).astype(BF)
        g_down_ffn = tn(g_latent, k["normed_two"])
        g_normed = (g_normed + nn(g_latent, k["down_two"])).astype(BF)
        back = scatter4([g_normed[j * HOME : (j + 1) * HOME] for j in range(4)], ffn_rows)
        grad = grad + rms_backward(k["residual_one"], k["inverse_two"], ffn_gain[l], back)
        g_down_ffn = g_down_ffn.reshape(2, 2, 16, width).transpose(1, 0, 2, 3)
        per_seq = jnp.concatenate(
            [g_down_ffn.reshape(2, 32, width), g_up_back.reshape(2, 16, width)], axis=1
        ).reshape(96, width)
        ffn_sums[l] = (per_seq, jnp.stack(g_shards))
        if l == 0:
            early = reduce_early(*ffn_sums[1], *ffn_sums[0], *mix_sums[1])
        rows = in_order(gather4(grad.astype(BF), along_x))
        g_up_out = tn(k["out_latent"], rows)
        g_out_latent = nt(rows, k["up_out"]).astype(BF)
        g_mixed = nt(rows, w_back[l]) + nn(g_out_latent, k["down_out"])
        g_mixed = g_mixed.astype(BF).astype(F32)
        g_down_out = tn(g_out_latent, k["mixed"])
        states, decay, scale = k["states"], k["decay"], k["scale"]
        g_states = g_mixed * k["act"]
        g_branch = (g_mixed * states * k["pull"]).astype(BF)
        shifted = jnp.concatenate([decay[1:], jnp.ones((1, 512), F32)], axis=0)
        suffix, local = local_scan(shifted, g_states, True)
        carry = entering(k["total"], decay[0] * local[0], core, half, True)
        g_driven = local + suffix * carry
        previous = jnp.concatenate([k["carry"][None], states[:-1]], axis=0)
        conv, gate_a, gate_i = k["conv"], k["gate_a"], k["gate_i"]
        g_scale = g_driven * conv * gate_i
        g_decay = g_driven * previous - jnp.where(first, 0.0, g_scale * (decay / scale))
        g_a = (g_decay * decay * k["rate"] * gate_a * (1.0 - gate_a)).astype(BF)
        g_i = (g_scale * scale * (1.0 - gate_i)).astype(BF)
        gw = k["gw"]
        g_conv = g_driven * gate_i * scale + jnp.concatenate(
            [
                nt(g_a[:, h * 128 : h * 128 + 128], gw[h, 0])
                + nt(g_i[:, h * 128 : h * 128 + 128], gw[h, 1])
                for h in range(4)
            ],
            axis=1,
        )
        halo = send(g_conv[:3], next_block(True))
        extended = jnp.concatenate([g_conv, halo], axis=0)
        taps = k["taps"]
        g_inputs = taps[0] * extended[:BLOCK]
        for o in (1, 2, 3):
            g_inputs = g_inputs + taps[o] * extended[o : o + BLOCK]
        g_inputs = g_inputs.astype(BF)
        latent, up = k["latent"], k["up"]
        g_up_mix = jnp.concatenate(
            [tn(latent[:, :RANK], g_branch), tn(latent[:, RANK:], g_inputs)], axis=0
        )
        g_latent = jnp.concatenate(
            [nt(g_branch, up[:RANK]), nt(g_inputs, up[RANK:])], axis=1
        ).astype(BF)
        g_down_mix = tn(g_latent, k["normed"])
        both = jnp.stack(
            [g_branch.reshape(BLOCK, 4, 128), g_inputs.reshape(BLOCK, 4, 128)], axis=2
        ).reshape(BLOCK, 1024)
        g_normed = nn(both, w_in[l]) + nn(g_latent, k["down"])
        back = scatter4(ordered_parts(g_normed), along_x)
        grad = grad + rms_backward(k["residual"], k["inverse"], mix_gain[l], back)
        mix_sums[l] = (
            jnp.concatenate([g_down_mix, g_up_out], axis=0),
            jnp.concatenate([g_up_mix, g_down_out], axis=0),
        )
    grad_tokens = lax.all_gather(grad.astype(BF), ("y", "x"), axis=0, tiled=True)
    grad_tokens = grad_tokens.astype(F32).reshape(tokens.shape)
    output = output.astype(F32).reshape(tokens.shape)
    onehot = adapter_ids[:, None] == jnp.arange(8, dtype=jnp.int32)[None, :]

    def spread(per_seq):
        shape = (1, 8) + (1,) * (per_seq.ndim - 2)
        parts = [
            jnp.where(onehot[s].reshape(shape), per_seq[:, s : s + 1], 0.0) for s in range(2)
        ]
        return parts[0] + parts[1]

    (whole_1, shards_1), (whole_0, shards_0), (mix_1, mix_split_1) = early
    mix_0, mix_split_0 = reduce_mix(*mix_sums[0])
    ffn_whole = jnp.stack([whole_0, whole_1]).reshape(2, 2, 48, width)
    ffn = jnp.stack([shards_0, shards_1])
    mix_whole = jnp.stack([mix_0, mix_1])
    mix = jnp.stack([mix_split_0, mix_split_1])
    ffn_up_g = ffn[:, :64].reshape(2, 2, 2, 16, 4608).transpose(0, 2, 1, 3, 4)
    back_down_g = ffn[:, 64:].reshape(2, 2, 16, 4608)
    turned = lambda v: jnp.swapaxes(v, -1, -2)
    return (
        output,
        grad_tokens,
        turned(spread(mix_whole[:, :, :32])),
        spread(mix[:, :, :32].reshape(2, 2, 2, 16, 2048)),
        turned(spread(mix[:, :, 32:])),
        spread(mix_whole[:, :, 32:]),
        turned(spread(ffn_whole[:, :, :32])),
        spread(ffn_up_g),
        turned(spread(back_down_g)),
        spread(ffn_whole[:, :, 32:]),
    )


def solution(mesh):
    grid = Mesh(mesh.devices.reshape(4, 2, 4, 4), ALL)
    sp, mp = ("z", "core"), ("y", "x")
    in_specs = (
        P(None, sp, None),
        P(None, sp, None),
        P(),
        P(),
        P(),
        P(),
        P(None, None, mp),
        P(None, None, mp),
        P(None, None, mp),
        P(None, mp),
        P(None, mp, None, None),
        P(None, mp),
        P(None, mp, None, None),
        P(None, mp),
        P(None, mp),
        P(None, mp, None),
        P(None, None, mp),
        P(None, None, mp),
        P(None, mp, None),
        P(),
        P(None, None, None, None, mp),
        P(None, None, mp, None),
        P(),
        P(),
        P(None, None, None, None, mp),
        P(None, None, mp, None),
        P(),
    )
    out_specs = (P(None, sp, None), P(None, sp, None)) + (P(),) * 8
    return jax.shard_map(shards, mesh=grid, in_specs=in_specs, out_specs=out_specs, check_vma=False)
```

```python
import functools

import jax
import jax.numpy as jnp
from jax import lax
from jax.experimental import pallas as pl
from jax.experimental.pallas import tpu as pltpu
from jax.sharding import Mesh
from jax.sharding import PartitionSpec as P

ALL = ("z", "core", "y", "x")
BF = jnp.bfloat16
F32 = jnp.float32
RANK = 16
HOME = 64
BLOCK = 256
LIMIT = 60 * 2**20
LARGE = 60 * 2**20
GELU_C = 0.7978845608028654


def device_pairs(move):
    pairs = []
    for z in range(4):
        for c in range(2):
            for y in range(4):
                for x in range(4):
                    to = move(z, c, y, x)
                    if to is not None:
                        a = ((z * 2 + c) * 4 + y) * 4 + x
                        b = ((to[0] * 2 + to[1]) * 4 + to[2]) * 4 + to[3]
                        pairs.append((a, b))
    return pairs


def send(value, move):
    return lax.ppermute(value, ALL, device_pairs(move))


def along_x(d):
    return lambda z, c, y, x: (z, c, y, (x + d) % 4)


def along_y(d):
    return lambda z, c, y, x: (z, c, (y + d) % 4, x)


def ffn_rows(d):
    return lambda z, c, y, x: (z, c, y, (x + d) % 4) if c == 0 else (z, c, (y + d) % 4, x)


def ffn_shards(d):
    return lambda z, c, y, x: (z, c, (y + d) % 4, x) if c == 0 else (z, c, y, (x + d) % 4)


def shard_groups():
    at = lambda z, c, y, x: ((z * 2 + c) * 4 + y) * 4 + x
    columns = [[at(z, 0, y, x) for y in range(4)] for z in range(4) for x in range(4)]
    rows = [[at(z, 1, y, x) for x in range(4)] for z in range(4) for y in range(4)]
    return columns + rows


def gather4(value, moves):
    return [value] + [send(value, moves(j)) for j in (1, 2, 3)]


def deal4(parts, moves):
    return [parts[0]] + [send(parts[j], moves(-j)) for j in (1, 2, 3)]


def scatter4(parts, moves):
    moved = deal4(parts, moves)[1:]
    total = parts[0].astype(F32)
    for part in moved:
        total = total + part.astype(F32)
    return total


def split3(v):
    high = v.astype(BF)
    rest = v - high.astype(F32)
    mid = rest.astype(BF)
    return high, mid, (rest - mid.astype(F32)).astype(BF)


def tie(first, second):
    return lax.optimization_barrier((first, second))


def combine(earlier, later):
    return (earlier[0] * later[0], later[0] * earlier[1] + later[1])


def next_block(reverse):
    def move(z, c, y, x):
        at = (z * 2 + c) * 2 + y % 2 + (-1 if reverse else 1)
        if not 0 <= at < 16:
            return None
        return (at // 4, (at // 2) % 2, (y // 2) * 2 + at % 2, x)

    return move


def entering(own, core, half, reverse):
    one = jnp.stack([jnp.ones_like(own[0]), jnp.zeros_like(own[0])])

    def step(own, other, later):
        pre = jnp.where(later, other, one)
        first, second = jnp.where(later, other, own), jnp.where(later, own, other)
        both = combine((first[0], first[1]), (second[0], second[1]))
        return pre, jnp.stack(both)

    other = send(own, lambda z, c, y, x: (z, c, y ^ 1, x))
    pre_h, own = step(own, other, half == (0 if reverse else 1))
    other = send(own, lambda z, c, y, x: (z, 1 - c, y, x))
    pre_c, own = step(own, other, core == (0 if reverse else 1))
    far = []
    for d in (1, 2, 3):
        e = -d if reverse else d
        far.append(
            send(own, lambda z, c, y, x, e=e: (z + e, c, y, x) if 0 <= z + e < 4 else None)
        )
    state = far[2][1]
    for part in (far[1], far[0], pre_c, pre_h):
        state = part[0] * state + part[1]
    return state[None]


def nn(a, b):
    return jnp.dot(a, b, preferred_element_type=F32)


def nt(a, b):
    return lax.dot_general(a, b, (((1,), (1,)), ((), ())), preferred_element_type=F32)


def tn(a, b):
    return lax.dot_general(a, b, (((0,), (0,)), ((), ())), preferred_element_type=F32)


def gelu_pair(v):
    t = jnp.tanh(GELU_C * (v + 0.044715 * v * v * v))
    act = 0.5 * v * (1.0 + t)
    pull = 0.5 * (1.0 + t) + 0.5 * v * (1.0 - t * t) * (GELU_C * (1.0 + 0.134145 * v * v))
    return act, pull


def inverse_rms(v):
    return lax.rsqrt(jnp.mean(v * v, axis=-1, keepdims=True) + 1e-06)


def rms_backward(v, inverse, gain, grad):
    scaled = grad * gain
    return inverse * scaled - v * inverse**3 * jnp.mean(v * scaled, axis=-1, keepdims=True)


VMEM = pl.BlockSpec(memory_space=pltpu.VMEM)
SMEM = pl.BlockSpec(memory_space=pltpu.SMEM)
HBM = pl.BlockSpec(memory_space=pl.ANY)


def call(kernel, name, ins, outs, scratch=(), scalars=None, far=(), mflops=100, mbytes=4):
    specs = [VMEM] * len(ins) + [HBM] * len(far)
    arrays = list(ins) + list(far)
    if scalars is not None:
        specs, arrays = [SMEM] + specs, [scalars] + arrays
    return pl.pallas_call(
        kernel,
        out_shape=[jax.ShapeDtypeStruct(shape, dtype) for shape, dtype in outs],
        in_specs=specs,
        out_specs=[VMEM] * len(outs),
        scratch_shapes=list(scratch),
        compiler_params=pltpu.CompilerParams(
            vmem_limit_bytes=LARGE if mflops > 1000 else LIMIT
        ),
        cost_estimate=pl.CostEstimate(
            flops=mflops * 10**6, bytes_accessed=mbytes * 10**6, transcendentals=0
        ),
        name=name,
    )(*arrays)


def fetch(source, rows, target, sem):
    first, count = rows
    copies = []
    for j in range(4):
        copy = pltpu.make_async_copy(
            source.at[j, pl.ds(first, count)],
            target.at[pl.ds(j * count, count)],
            sem.at[j],
        )
        copy.start()
        copies.append(copy)
    return copies


def wait_all(copies):
    for copy in copies:
        copy.wait()


def place(scalars, blocks, rows_ref):
    for j in range(4):
        at = pl.multiple_of(lax.rem(scalars[0] + 4 - j, 4) * HOME, HOME)
        rows_ref[pl.ds(at, HOME), :] = blocks[j][...]


def take(scalars, total_ref, parts):
    for j in range(4):
        at = pl.multiple_of(lax.rem(scalars[0] + 4 - j, 4) * HOME, HOME)
        parts[j][...] = total_ref[pl.ds(at, HOME), :]


def scan_rows(reverse, a_ref, b_ref, cum_ref, out_ref):
    rows, width = a_ref.shape
    row = lax.broadcasted_iota(jnp.int32, (8, width), 0)
    groups = rows // 8

    def body(i, carry):
        ca, cb = carry
        at = pl.multiple_of((groups - 1 - i if reverse else i) * 8, 8)
        a, b = a_ref[pl.ds(at, 8), :], b_ref[pl.ds(at, 8), :]
        for k in (1, 2, 4):
            seen = row < 8 - k if reverse else row >= k
            by = 8 - k if reverse else k
            pa = jnp.where(seen, pltpu.roll(a, by, 0), 1.0)
            pb = jnp.where(seen, pltpu.roll(b, by, 0), 0.0)
            b = a * pb + b
            a = a * pa
        b = a * cb + b
        a = a * ca
        cum_ref[pl.ds(at, 8), :] = a
        out_ref[pl.ds(at, 8), :] = b
        last = 0 if reverse else 7
        return (
            jnp.broadcast_to(a[last : last + 1], a.shape),
            jnp.broadcast_to(b[last : last + 1], b.shape),
        )

    start = (jnp.ones((8, width), F32), jnp.zeros((8, width), F32))
    lax.fori_loop(0, groups, body, start, unroll=4)


def add_norm_kernel(p0, p1, p2, p3, residual, gain, out, normed):
    total = p0[...].astype(F32) + p1[...].astype(F32) + p2[...].astype(F32)
    v = residual[...] + total + p3[...].astype(F32)
    out[...] = v
    normed[...] = (v * inverse_rms(v) * gain[...]).astype(BF)


def norm_back_kernel(p0, p1, p2, p3, grad, v_ref, gain, out, low):
    total = p0[...].astype(F32) + p1[...].astype(F32) + p2[...].astype(F32)
    total = total + p3[...].astype(F32)
    v = v_ref[...]
    g = grad[...] + rms_backward(v, inverse_rms(v), gain[...], total)
    out[...] = g
    low[...] = g.astype(BF)


def inputs_kernel(
    sc, n0, n1, n2, n3, down, up, w, normed, inputs, last, lat_b, lat_i, wi, sem
):
    copies = fetch(w, (128, 128), wi, sem)
    place(sc, (n0, n1, n2, n3), normed)
    rows = normed[...]
    lat_b[...] = nt(rows, down[:RANK]).astype(BF)
    low = nt(rows, down[RANK:]).astype(BF)
    lat_i[...] = low
    wait_all(copies)
    inputs[...] = (nt(rows, wi[...]) + nn(low, up[RANK:])).astype(BF)
    last[...] = inputs[BLOCK - 16 :]


def branch_kernel(normed, lat_b, up, w, acts, wb, sem):
    copies = fetch(w, (0, 128), wb, sem)
    wait_all(copies)
    branch = nt(normed[...], wb[...]) + nn(lat_b[...], up[:RANK])
    acts[0], acts[1] = gelu_pair(branch)


def gates_kernel(
    sc, inputs, halo, params, gw, saved, scan, ends, ext, driven
):
    conv, gate_a, gate_i, decay = (saved.at[i] for i in range(4))
    cum, local = scan.at[0], scan.at[1]
    ext[:16] = halo[...].astype(F32)
    ext[16:] = inputs[...].astype(F32)
    value = params[4:5] + params[0:1] * ext[pl.ds(16, BLOCK)]
    for o in (1, 2, 3):
        value = value + params[o : o + 1] * ext[pl.ds(16 - o, BLOCK)]
    conv[...] = value
    row = lax.broadcasted_iota(jnp.int32, (BLOCK, 128), 0)
    first = (row == 0) & (sc[1] == 1)
    for h in range(4):
        at = slice(h * 128, h * 128 + 128)
        c = conv[:, at]
        pre = nn(c.astype(BF), gw[h])
        a = jax.nn.sigmoid(pre[:, :128] + params[5:6, at])
        i = jax.nn.sigmoid(pre[:, 128:] + params[6:7, at])
        d = jnp.exp(a * params[7:8, at])
        gate_a[:, at] = a
        gate_i[:, at] = i
        decay[:, at] = d
        driven[:, at] = c * i * jnp.where(first, 1.0, jnp.sqrt(1.0 - d * d + 0.01))
    scan_rows(False, decay, driven, cum, local)
    ends[0:1] = cum[BLOCK - 1 :]
    ends[1:2] = local[BLOCK - 1 :]


def mixed_kernel(
    sc, carry, scan, acts, down_out, up_out, w, states, mixed, out_latent, q0, q1, q2, q3,
    wo, total, sem,
):
    copies = fetch(w, (0, 128), wo, sem)
    s = scan[1] + scan[0] * carry[...]
    states[...] = s
    m = (s * acts[0]).astype(BF)
    mixed[...] = m
    low = nt(m, down_out[...]).astype(BF)
    out_latent[...] = low
    wait_all(copies)
    total[...] = (nn(m, wo[...]) + nn(low, up_out[...])).astype(BF)
    take(sc, total, (q0, q1, q2, q3))


def ffn_kernel(
    n0, n1, n2, n3, a, down, up_back, mask, w, gate, up, hidden, latent, back_latent,
    q0, q1, q2, q3, rows_ref, wg, wu, wd, sem,
):
    cg = fetch(w, (0, 288), wg, sem.at[0])
    cu = fetch(w, (288, 288), wu, sem.at[1])
    cd = fetch(w, (576, 288), wd, sem.at[2])
    for j, n in enumerate((n0, n1, n2, n3)):
        rows_ref[j * HOME : (j + 1) * HOME] = n[...]
    rows = rows_ref[...]
    lat_g = (nt(rows, down[:32]) * mask[...]).astype(BF)
    lat_u = (nt(rows, down[32:]) * mask[...]).astype(BF)
    latent[0] = lat_g
    latent[1] = lat_u
    wait_all(cg)
    g = nt(rows, wg[...]) + nn(lat_g, a[:32])
    gate[...] = g
    wait_all(cu)
    u = nt(rows, wu[...]) + nn(lat_u, a[32:64])
    up[...] = u
    hidden[...] = (gelu_pair(g)[0] * u).astype(BF)
    h = hidden[...]
    low = (nt(h, a[64:]) * mask[...]).astype(BF)
    back_latent[...] = low
    wait_all(cd)
    total = (nn(h, wd[...]) + nn(low, up_back[...])).astype(BF)
    for j, q in enumerate((q0, q1, q2, q3)):
        q[...] = total[j * HOME : (j + 1) * HOME]


def ffn_back_kernel(
    r0, r1, r2, r3, a, down, up_back, mask, gate, up, w, g_gate, g_up, g_back, g_latent, rows_ref,
    q0, q1, q2, q3, wg, wu, wd, sem,
):
    cd = fetch(w, (576, 288), wd, sem.at[2])
    cg = fetch(w, (0, 288), wg, sem.at[0])
    cu = fetch(w, (288, 288), wu, sem.at[1])
    for j, r in enumerate((r0, r1, r2, r3)):
        rows_ref[j * HOME : (j + 1) * HOME] = r[...]
    rows = rows_ref[...]
    low = (nt(rows, up_back[...]) * mask[...]).astype(BF)
    g_back[...] = low
    wait_all(cd)
    gh = (nt(rows, wd[...]) + nn(low, a[64:])).astype(BF).astype(F32)
    act, pull = gelu_pair(gate[...])
    g_up[...] = (gh * act).astype(BF)
    g_gate[...] = (gh * up[...] * pull).astype(BF)
    gg, gu = g_gate[...], g_up[...]
    lat_g = (nt(gg, a[:32]) * mask[...]).astype(BF)
    lat_u = (nt(gu, a[32:64]) * mask[...]).astype(BF)
    g_latent[0] = lat_g
    g_latent[1] = lat_u
    wait_all(cg)
    total = nn(gg, wg[...]) + nn(lat_g, down[:32]) + nn(lat_u, down[32:])
    wait_all(cu)
    total = (total + nn(gu, wu[...])).astype(BF)
    for j, q in enumerate((q0, q1, q2, q3)):
        q[...] = total[j * HOME : (j + 1) * HOME]


def ffn_adapters_kernel(
    n0, n1, n2, n3, rows, latent, back_latent, hidden, g_gate, g_up, g_back, g_latent,
    whole, split, normed_ref,
):
    for j, n in enumerate((n0, n1, n2, n3)):
        normed_ref[j * HOME : (j + 1) * HOME] = n[...]
    normed = normed_ref[...]
    g_down = [tn(g_latent[0], normed), tn(g_latent[1], normed)]
    g_up_back = tn(back_latent[...], rows[...])
    for s in range(2):
        at = slice(s * RANK, s * RANK + RANK)
        whole[s * 48 : s * 48 + 16] = g_down[0][at].astype(BF)
        whole[s * 48 + 16 : s * 48 + 32] = g_down[1][at].astype(BF)
        whole[s * 48 + 32 : s * 48 + 48] = g_up_back[at].astype(BF)
    split[:32] = tn(latent[0], g_gate[...]).astype(BF)
    split[32:64] = tn(latent[1], g_up[...]).astype(BF)
    split[64:] = tn(g_back[...], hidden[...]).astype(BF)


def states_back_kernel(
    sc, r0, r1, r2, r3, down_out, up_out, acts, saved, scan, w,
    rows_ref, g_mixed, g_low, back, ends, wo, ext, g_states, sem,
):
    decay, cum, suffix, local = saved.at[3], scan.at[0], back.at[0], back.at[1]
    copies = fetch(w, (0, 128), wo, sem)
    place(sc, (r0, r1, r2, r3), rows_ref)
    rows = rows_ref[...]
    low = nt(rows, up_out[...]).astype(BF)
    g_low[...] = low
    ext[:BLOCK] = decay[...]
    ext[BLOCK:] = jnp.ones((8, 512), F32)
    ext[:BLOCK] = ext[pl.ds(1, BLOCK)]
    wait_all(copies)
    gm = (nt(rows, wo[...]) + nn(low, down_out[...])).astype(BF)
    g_mixed[...] = gm
    g_states[...] = gm.astype(F32) * acts[0]
    scan_rows(True, ext.at[pl.ds(0, BLOCK)], g_states, suffix, local)
    ends[0:1] = cum[BLOCK - 1 :]
    ends[1:2] = decay[0:1] * local[0:1]


def branch_back_kernel(
    rows, g_mixed, g_low, states, acts, mixed, out_latent, lat_b, up, down, w,
    part, g_up_out, g_down_out, g_up_b, g_branch_low, wb, sem,
):
    copies = fetch(w, (0, 128), wb, sem)
    gb = (g_mixed[...].astype(F32) * states[...] * acts[1]).astype(BF)
    low = nt(gb, up[:RANK]).astype(BF)
    g_branch_low[...] = low
    g_up_out[...] = tn(out_latent[...], rows[...])
    g_down_out[...] = tn(g_low[...], mixed[...])
    g_up_b[...] = tn(lat_b[...], gb)
    wait_all(copies)
    part[...] = nn(gb, wb[...]) + nn(low, down[:RANK])


def gates_back_kernel(
    sc, carry, carry_in, back, states, saved, params, gw, g_conv, rim, ext
):
    conv, gate_a, gate_i, decay = (saved.at[i] for i in range(4))
    suffix, local = back.at[0], back.at[1]
    ext[:8] = jnp.broadcast_to(carry_in[...], (8, 512))
    ext[8:] = states[...]
    row = lax.broadcasted_iota(jnp.int32, (BLOCK, 128), 0)
    first = (row == 0) & (sc[1] == 1)
    for h in range(4):
        at = slice(h * 128, h * 128 + 128)
        gd = local[:, at] + suffix[:, at] * carry[:, at]
        d, i, a, c = decay[:, at], gate_i[:, at], gate_a[:, at], conv[:, at]
        scale = jnp.where(first, 1.0, jnp.sqrt(1.0 - d * d + 0.01))
        g_scale = gd * c * i
        previous = ext[pl.ds(7, BLOCK), at]
        g_decay = gd * previous - jnp.where(first, 0.0, g_scale * (d / scale))
        ga = (g_decay * d * params[7:8, at] * a * (1.0 - a)).astype(BF)
        gi = (g_scale * scale * (1.0 - i)).astype(BF)
        g_conv[:, at] = gd * i * scale + nt(ga, gw[h, :, :128]) + nt(gi, gw[h, :, 128:])
    rim[...] = g_conv[:8]


def inputs_back_kernel(
    sc, g_conv, halo, params, up, down, part, w, g_inputs, g_low, q0, q1, q2, q3,
    ext, wi, total, sem,
):
    copies = fetch(w, (128, 128), wi, sem)
    ext[:BLOCK] = g_conv[...]
    ext[BLOCK:] = halo[...]
    value = params[0:1] * ext[:BLOCK]
    for o in (1, 2, 3):
        value = value + params[o : o + 1] * ext[pl.ds(o, BLOCK)]
    gi = value.astype(BF)
    g_inputs[...] = gi
    low = nt(gi, up[RANK:]).astype(BF)
    g_low[...] = low
    wait_all(copies)
    total[...] = (part[...] + nn(gi, wi[...]) + nn(low, down[RANK:])).astype(BF)
    take(sc, total, (q0, q1, q2, q3))


def mix_adapters_kernel(
    normed, lat_i, g_inputs, g_low_b, g_low_i, g_up_b, g_up_out, g_down_out, out, whole, split,
    wide,
):
    whole[:RANK] = tn(g_low_b[...], normed[...])
    whole[RANK:32] = tn(g_low_i[...], normed[...])
    whole[32:] = g_up_out[...]
    split[:RANK] = g_up_b[...]
    split[RANK:32] = tn(lat_i[...], g_inputs[...])
    split[32:] = g_down_out[...]
    for c in range(2):
        wide[c, :24] = whole[c * 24 : c * 24 + 24]
        for i in range(3):
            at = c * 24 + i * 8
            wide[c, 24:, i * 512 : i * 512 + 512] = split[at : at + 8]
    out[...] = wide[...].astype(BF)


def head_kernel(
    sc, tokens, down, up, gain, wb, wi, o0, o1, o2, o3, normed, lat_b, lat_i, w
):
    j = pl.program_id(0)

    @pl.when(j == 0)
    def _():
        w[:, :128] = wb[0]
        w[:, 128:] = wi[0]

    v = tokens[0]
    rows = (v * inverse_rms(v) * gain[...]).astype(BF)
    low_b = nt(rows, down[0, 0, :RANK]).astype(BF)
    low_i = nt(rows, down[0, 0, RANK:]).astype(BF)
    both = nn(rows, w[...])
    branch = (both[:, :128] + nn(low_b, up[0, 0, :RANK])).astype(BF)
    inputs = (both[:, 128:] + nn(low_i, up[0, 0, RANK:])).astype(BF)
    for i, out in enumerate((o0, o1, o2, o3)):

        @pl.when(j == i)
        def _():
            out[:, :128] = branch
            out[:, 128:] = inputs

    @pl.when(j == 0)
    def _():
        normed[...] = rows
        lat_b[...] = low_b
        lat_i[...] = low_i


def head(scalars, tokens, down, up, gain, wb, wi):
    at = lambda j, sc: lax.rem(sc[0] + 4 - j, 4)
    own = lambda j, sc: (0, sc[1 + at(j, sc) // 2], 0, 0)
    fixed = lambda j, sc: (0, 0)
    block = ((BLOCK, 256), BF)
    outs = [block] * 4 + [((BLOCK, 1536), BF), ((BLOCK, RANK), BF), ((BLOCK, RANK), BF)]
    return pl.pallas_call(
        head_kernel,
        out_shape=[jax.ShapeDtypeStruct(shape, dtype) for shape, dtype in outs],
        grid_spec=pltpu.PrefetchScalarGridSpec(
            num_scalar_prefetch=1,
            grid=(4,),
            in_specs=[
                pl.BlockSpec((1, BLOCK, 1536), lambda j, sc: (at(j, sc) // 2, at(j, sc) % 2, 0)),
                pl.BlockSpec((1, 1, 32, 1536), own),
                pl.BlockSpec((1, 1, 32, 128), own),
                pl.BlockSpec((1, 1536), fixed),
                pl.BlockSpec((1, 1536, 128), lambda j, sc: (0, 0, 0)),
                pl.BlockSpec((1, 1536, 128), lambda j, sc: (0, 0, 0)),
            ],
            out_specs=[pl.BlockSpec(shape, fixed) for shape, _ in outs],
            scratch_shapes=[pltpu.VMEM((1536, 256), BF)],
        ),
        compiler_params=pltpu.CompilerParams(vmem_limit_bytes=LIMIT),
        cost_estimate=pl.CostEstimate(
            flops=900 * 10**6, bytes_accessed=9 * 10**6, transcendentals=0
        ),
        name="head",
    )(scalars, tokens, down, up, gain, wb, wi)


def prepare_kernel(
    sc, md0, md1, fd0, fd1, ou0, ou1, bu0, bu1, mu0, mu1, od0, od1, fu0, fu1, bd0, bd1,
    ga, gi, cw, cb, ab, ib, dp, mix_d, ffn_d, out_u, back_u, small, ffn_small,
):
    l = pl.program_id(0)
    ffn_small[...] = jnp.zeros(ffn_small.shape, BF)
    for s, (md, fd, ou, bu) in enumerate(((md0, fd0, ou0, bu0), (md1, fd1, ou1, bu1))):
        mix_d[0, s] = md[0, 0]
        ffn_d[0, s * 16 : s * 16 + 16] = fd[0, 0, :16]
        ffn_d[0, 32 + s * 16 : 48 + s * 16] = fd[0, 0, 16:]
        out_u[0, s] = ou[0, 0]
        back_u[0, s * 16 : s * 16 + 16] = bu[0, 0]
    small[0, :128] = ga[0, 0]
    small[0, 128:256] = gi[0, 0]
    for s, (mu, od, fu, bd) in enumerate(((mu0, od0, fu0, bd0), (mu1, od1, fu1, bd1))):
        small[0, 256 + s * 32 : 288 + s * 32] = mu[0, 0]
        small[0, 320 + s * 16 : 336 + s * 16] = od[0, 0]
        at = slice(s * 16, s * 16 + 16)
        ffn_small[0, at, :288] = fu[0, 0, :16]
        ffn_small[0, at, 384:672] = fu[0, 0, 16:]
        ffn_small[0, at, 768:1056] = bd[0, 0]
    vectors = [ref[pl.ds(l, 1), :] for ref in (cb, ab, ib, dp)]
    wide = jnp.concatenate([cw[0]] + vectors + [jnp.zeros((8, 128), F32)], axis=0)
    for i, part in enumerate(split3(wide)):
        small[0, 352 + 16 * i : 368 + 16 * i] = part


def prepare(ids, tables, singles, vectors):
    specs, arrays = [], []
    for table in tables:
        for s in range(2):
            specs.append(
                pl.BlockSpec((1, 1) + table.shape[2:], lambda l, sc, s=s: (l, sc[s], 0, 0))
            )
            arrays.append(table)
    for single in singles:
        dims = single.ndim - 1
        specs.append(
            pl.BlockSpec((1,) + single.shape[1:], lambda l, sc, dims=dims: (l,) + (0,) * dims)
        )
        arrays.append(single)
    for vector in vectors:
        specs.append(pl.BlockSpec(vector.shape, lambda l, sc: (0, 0)))
        arrays.append(vector)
    outs = [(2, 32, 1536), (64, 1536), (2, 16, 1536), (32, 1536), (400, 128), (32, 1536)]
    return pl.pallas_call(
        prepare_kernel,
        out_shape=[jax.ShapeDtypeStruct((2,) + shape, BF) for shape in outs],
        grid_spec=pltpu.PrefetchScalarGridSpec(
            num_scalar_prefetch=1,
            grid=(2,),
            in_specs=specs,
            out_specs=[
                pl.BlockSpec((1,) + shape, lambda l, sc, n=len(shape): (l,) + (0,) * n)
                for shape in outs
            ],
        ),
        compiler_params=pltpu.CompilerParams(vmem_limit_bytes=LIMIT),
        cost_estimate=pl.CostEstimate(flops=10**6, bytes_accessed=4 * 10**6, transcendentals=0),
        name="prepare",
    )(ids, *arrays)


def arrange_kernel(
    sc, s0, s1, s2, s3, gw, up, down_out, params, small
):
    for j, block in enumerate((s0, s1, s2, s3)):
        small[lax.rem(sc[2] + 4 - j, 4)] = block[...]
    for l in range(2):
        for p in range(4):
            at = slice(p * 128, p * 128 + 128)
            gw[l, p, :, :128] = small[p, l, :128]
            gw[l, p, :, 128:] = small[p, l, 128:256]
            for s in range(2):
                up[l, s, :, at] = small[p, l, 256 + s * 32 : 288 + s * 32]
                down_out[l, s, :, at] = small[p, l, 320 + s * 16 : 336 + s * 16]
            parts = [small[p, l, 352 + 16 * i : 368 + 16 * i].astype(F32) for i in range(3)]
            total = parts[0] + parts[1] + parts[2]
            params[l, :, at] = total[:8]
            params[l, 7:8, at] = -8.0 * jax.nn.softplus(total[7:8])


def join_kernel(w, a, held, wide, sem):
    copies = []
    for j in range(4):
        copy = pltpu.make_async_copy(w.at[j, pl.ds(864, 32)], held.at[j], sem.at[j])
        copy.start()
        copies.append(copy)
    wait_all(copies)
    for j in range(4):
        for i in range(3):
            part = held[j, :, i * 384 : i * 384 + 288].astype(F32)
            wide[i * 32 : i * 32 + 32, j * 288 : j * 288 + 288] = part
    a[...] = wide[...].astype(BF)


def order_kernel(sc, b0, b1, b2, b3, out):
    for j, block in enumerate((b0, b1, b2, b3)):
        out[lax.rem(sc[2] + 4 - j, 4)] = block[...]


def order_x_kernel(sc, b0, b1, b2, b3, out):
    for j, block in enumerate((b0, b1, b2, b3)):
        out[lax.rem(sc[0] + 4 - j, 4)] = block[...]


def unpack_kernel(sc, b0, b1, b2, b3, inputs, last, acts, held):
    for j, block in enumerate((b0, b1, b2, b3)):
        held[lax.rem(sc[2] + j, 4)] = block[...]
    for p in range(4):
        at = slice(p * 128, p * 128 + 128)
        inputs[:, at] = held[p, :, 128:]
        acts[0, :, at], acts[1, :, at] = gelu_pair(held[p, :, :128].astype(F32))
    last[...] = inputs[BLOCK - 16 :]


def pack_kernel(a_ref, b_ref, c_ref, d_ref, out):
    at = 0
    for ref in (a_ref, b_ref, c_ref, d_ref):
        count = ref.shape[1]
        out[at : at + count] = ref[0]
        at += count


def pack(l, parts):
    width = parts[0].shape[2]
    total = sum(part.shape[1] for part in parts)
    return pl.pallas_call(
        pack_kernel,
        out_shape=jax.ShapeDtypeStruct((total, width), BF),
        grid=(2,),
        in_specs=[pl.BlockSpec((1, p.shape[1], width // 2), lambda i: (l, 0, i)) for p in parts],
        out_specs=pl.BlockSpec((total, width // 2), lambda i: (0, i)),
        compiler_params=pltpu.CompilerParams(vmem_limit_bytes=LIMIT),
        cost_estimate=pl.CostEstimate(flops=0, bytes_accessed=5 * 10**6, transcendentals=0),
        name="pack",
    )(*parts)


def pair_kernel(a_ref, b_ref, out):
    out[:128] = a_ref[0].T
    out[128:] = b_ref[0].T


def pair_of(l, a, b):
    rows = a.shape[1] // 3
    piece = pl.BlockSpec((1, rows, 128), lambda i: (l, i, 0))
    return pl.pallas_call(
        pair_kernel,
        out_shape=jax.ShapeDtypeStruct((256, a.shape[1]), BF),
        grid=(3,),
        in_specs=[piece] * 2,
        out_specs=pl.BlockSpec((256, rows), lambda i: (0, i)),
        compiler_params=pltpu.CompilerParams(vmem_limit_bytes=LIMIT),
        cost_estimate=pl.CostEstimate(flops=0, bytes_accessed=2 * 10**6, transcendentals=0),
        name="pair",
    )(a, b)


def finish_kernel(ranked, sc, *refs):
    mix_d, mix_u, out_d, out_u, ffn_d, ffn_u, back_d, back_u, whole, shard, split = refs[-11:]
    a = pl.program_id(0)

    @pl.when(a == 0)
    def _():
        for c in range(2):
            for y in range(4):
                for x in range(4):
                    if ranked:
                        mine, other = (ref[x, y].astype(F32) for ref in refs[:2])
                        v = jnp.where(sc[2] == c, mine, other)
                    else:
                        v = refs[0][c, y, x].astype(F32)
                    row = c * 24 + (y % 2) * 12
                    for k in range(3):
                        lane = x * 384 + k * 128
                        whole[c, y * 12 : y * 12 + 12, lane : lane + 128] = v[
                            k * 16 : k * 16 + 12
                        ]
                        whole[y // 2, 48 + row : 60 + row, lane : lane + 128] = v[
                            192 + k * 16 : 204 + k * 16
                        ]
                        lane = (y * 4 + x) * 288 + k * 128
                        part = v[48 + k * 48 : 96 + k * 48]
                        wide = 32 if k == 2 else 128
                        shard[c * 48 : c * 48 + 48, lane : lane + wide] = part[:, :wide]
                    for p in range(4):
                        lane = (p * 4 + x) * 128
                        k = 192 + (3 + p) * 16
                        split[y // 2, row : row + 12, lane : lane + 128] = v[k : k + 12]

    w = [(sc[s] == a).astype(F32) for s in range(2)]
    both = lambda get: get(0) * w[0] + get(1) * w[1]
    ffn_d[0, 0] = both(lambda s: whole[s, :32])
    back_u[0, 0] = both(lambda s: whole[s, 32:48])
    mix_d[0, 0] = both(lambda s: whole[s, 48:80])
    out_u[0, 0] = both(lambda s: whole[s, 80:])
    ffn_u[0, 0, :16] = both(lambda s: shard[s * 16 : s * 16 + 16])
    ffn_u[0, 0, 16:] = both(lambda s: shard[32 + s * 16 : 48 + s * 16])
    back_d[0, 0] = both(lambda s: shard[64 + s * 16 : 80 + s * 16])
    mix_u[0, 0] = both(lambda s: split[s, :32])
    out_d[0, 0] = both(lambda s: split[s, 32:])


def finish(ids, layer, flats, tables=()):
    outs = [(32, 1536), (32, 2048), (16, 2048), (16, 1536), (32, 1536), (32, 4608), (16, 4608)]
    outs.append((16, 1536))
    return pl.pallas_call(
        functools.partial(finish_kernel, len(flats) == 2),
        out_shape=[jax.ShapeDtypeStruct((2, 8) + shape, F32) for shape in outs],
        grid_spec=pltpu.PrefetchScalarGridSpec(
            num_scalar_prefetch=1,
            grid=(8,),
            in_specs=[VMEM] * len(flats) + [HBM] * len(tables),
            out_specs=[
                pl.BlockSpec((1, 1) + shape, lambda a, sc: (layer, a, 0, 0)) for shape in outs
            ],
            scratch_shapes=[
                pltpu.VMEM((2, 96, 1536), F32),
                pltpu.VMEM((96, 4608), F32),
                pltpu.VMEM((2, 48, 2048), F32),
            ],
        ),
        input_output_aliases={1 + len(flats) + i: i for i in range(len(tables))},
        compiler_params=pltpu.CompilerParams(vmem_limit_bytes=LIMIT),
        cost_estimate=pl.CostEstimate(flops=10**7, bytes_accessed=12 * 10**6, transcendentals=0),
        name="finish",
    )(ids, *flats, *tables)


def widen_kernel(v, out):
    out[...] = v[...].astype(F32)


def widen(v):
    rows, width = v.shape
    spec = pl.BlockSpec((BLOCK, width), lambda i: (i, 0))
    return pl.pallas_call(
        widen_kernel,
        out_shape=jax.ShapeDtypeStruct(v.shape, F32),
        grid=(rows // BLOCK,),
        in_specs=[spec],
        out_specs=spec,
        cost_estimate=pl.CostEstimate(flops=10**6, bytes_accessed=10**7, transcendentals=0),
        name="widen",
    )(v)


def other_core(z, c, y, x):
    return (z, 1 - c, y, x)


def other_half(z, c, y, x):
    return (z, c, y ^ 1, x)


def along_z(d):
    return lambda z, c, y, x: ((z + d) % 4, c, y, x)


def halves(value, index, move):
    count = value.shape[0] // 2
    mine = lax.dynamic_slice_in_dim(value, index * count, count, 0)
    theirs = lax.dynamic_slice_in_dim(value, (1 - index) * count, count, 0)
    return mine.astype(F32) + send(theirs, move).astype(F32)


def ring_scatter(value, index, moves, axis):
    count = value.shape[axis] // 4
    parts = [
        lax.dynamic_slice_in_dim(value, ((index - j) % 4) * count, count, axis) for j in range(4)
    ]
    return scatter4(parts, moves)


def sum_z(value):
    total = value
    for d in (1, 2, 3):
        total = total + send(value, along_z(d))
    return total


def blocks_of(v, rows):
    n, width = v.shape
    v = jnp.pad(v, ((0, rows - n), (0, -width % 128)))
    return jnp.concatenate([v[:, i : i + 128] for i in range(0, width, 128)], axis=0)


def reduce_shards(split):
    core, x, y = lax.axis_index("core"), lax.axis_index("x"), lax.axis_index("y")
    group = jnp.where(core == 0, y, x)
    shard = split.astype(BF).reshape(96, 4, 288).transpose(1, 0, 2)
    return ring_scatter(shard, group, ffn_shards, 0)[0]


def reduce_steps(ffn_whole, mix_sums):
    core, x, y = lax.axis_index("core"), lax.axis_index("x"), lax.axis_index("y")
    both = jnp.concatenate([ffn_whole.reshape(2, 48, 1536), mix_sums], axis=1).astype(BF)
    part = halves(both.reshape(160, 1536), core, other_core)
    part = yield part
    split = jnp.concatenate([part[72:, i * 512 : i * 512 + 512] for i in range(3)], axis=0)
    whole = ring_scatter(part[:72].astype(BF), x, along_x, 1)
    whole, split = yield whole, split
    mix = jnp.concatenate([whole[48:], split], axis=1)
    pieces = []
    for q in range(4):
        here = jnp.where(y // 2 == q // 2, mix[(q % 2) * 12 : (q % 2) * 12 + 12], 0.0)
        pieces.append(jnp.concatenate([whole[q * 12 : q * 12 + 12], here], axis=1))
    part = ring_scatter(jnp.stack(pieces).astype(BF), y, along_y, 0)[0]
    yield blocks_of(part, 16)


def spread_flat(scalars, flat):
    for move, kernel, shape in (
        (along_y, order_kernel, (4, 304, 128)),
        (along_x, order_x_kernel, (4, 4, 304, 128)),
    ):
        (flat,) = call(kernel, "order", gather4(flat, move), [(shape, BF)], (), scalars)
    return flat, send(flat, other_core)


def shards(
    tokens,
    cotangent,
    lengths,
    adapter_ids,
    mix_gain,
    ffn_gain,
    w_branch,
    input_weight,
    conv_weight,
    conv_bias,
    gate_a_weight,
    gate_a_bias,
    gate_i_weight,
    gate_i_bias,
    decay_param,
    w_out,
    w_gate,
    w_up,
    w_down,
    mix_down,
    mix_up,
    out_down,
    out_up,
    ffn_down,
    ffn_up,
    back_down,
    back_up,
):
    width = tokens.shape[2]
    z, core = lax.axis_index("z"), lax.axis_index("core")
    y, x = lax.axis_index("y"), lax.axis_index("x")
    seq, half = y // 2, y % 2
    ids = adapter_ids
    ffn_group = jnp.where(core == 0, y, x)
    first = (z + core + half == 0).astype(jnp.int32)
    scalars = jnp.stack([x, first, y, ffn_group]).astype(jnp.int32)
    turned = lambda v: jnp.swapaxes(v, -1, -2)
    mix_down_t = turned(mix_down)
    mix_up_f = mix_up.reshape(2, 8, 32, 128)
    *local, normed_0, lat_b_0, lat_i_0 = head(
        jnp.stack([y, ids[0], ids[1]]),
        tokens,
        mix_down_t,
        mix_up_f,
        mix_gain[:1],
        w_branch,
        input_weight,
    )
    mine = local[0]
    local = deal4(local, along_y)
    picked, mine = tie(ids, mine)
    mix_d, ffn_d, out_u, back_u, small, ffn_small = prepare(
        picked,
        [
            mix_down_t, turned(ffn_down), out_up, back_up, mix_up_f, turned(out_down),
            ffn_up.reshape(2, 8, 32, 288), turned(back_down),
        ],
        [gate_a_weight, gate_i_weight, conv_weight],
        [conv_bias, gate_a_bias, gate_i_bias, decay_param],
    )
    small, local = tie(small, local)
    own = lambda table: lax.dynamic_index_in_dim(table, seq, 0, keepdims=False)
    gw, up_all, down_out_all, params_all = call(
        arrange_kernel,
        "arrange",
        gather4(small, along_y),
        [
            ((2, 4, 128, 256), BF), ((2, 2, 32, 512), BF), ((2, 2, 16, 512), BF),
            ((2, 8, 512), F32),
        ],
        [pltpu.VMEM((4, 2, 400, 128), BF)],
        scalars,
    )
    ffn_parts = [turned(w_gate), turned(w_up), w_down, ffn_small]
    gather_ffn = lambda v: lax.all_gather(v, ALL, axis=0, axis_index_groups=shard_groups())
    w_pair = [None, pair_of(1, w_branch, input_weight)]
    early, local = tie(ffn_parts, local)
    ffn_w = [gather_ffn(pack(0, early)), None]
    w_back = [lax.all_gather(w_out[0], "y"), None]
    w_in = [None, None]
    start = (seq, half * BLOCK + x * HOME, 0)
    residual = lax.dynamic_slice(tokens, start, (1, HOME, width))[0]
    position = (z * 2 + core) * 512 + half * BLOCK + x * HOME + jnp.arange(HOME)
    valid = (position < lengths[seq]).astype(F32)[:, None]
    of_rows = jnp.where(core == 0, y, (y - jnp.arange(4)) % 4) // 2
    of_rows = jnp.repeat(of_rows, HOME)[:, None]
    of_cols = jnp.arange(32) // RANK
    mask = (of_rows == of_cols[None, :]).astype(F32)
    rows_like = [((HOME, width), BF)] * 4
    group_sem = pltpu.SemaphoreType.DMA((4,))
    ffn_sem = pltpu.SemaphoreType.DMA((3, 4))
    ffn_buffers = [pltpu.VMEM((1152, width), BF)] * 3
    mix_buffer = pltpu.VMEM((512, width), BF)
    half_f = ((BLOCK, 512), F32)
    pair_f = ((2, BLOCK, 512), F32)
    half_b = ((BLOCK, 512), BF)
    low_b = ((BLOCK, RANK), BF)

    kept = []
    for l in range(2):
        k = {"residual": residual}
        down, up_out = own(mix_d[l]), own(out_u[l])
        up, down_out = own(up_all[l]), own(down_out_all[l])
        params = params_all[l]
        if l == 0:
            normed, lat_b, lat_i = normed_0, lat_b_0, lat_i_0
            inputs, last, acts = call(
                unpack_kernel,
                "unpack",
                local,
                [half_b, ((16, 512), BF), pair_f],
                [pltpu.VMEM((4, BLOCK, 256), BF)],
                scalars,
            )
            halo = send(last, next_block(False))
        else:
            blocks = gather4(normed_low, along_x)
            normed, inputs, last, lat_b, lat_i = call(
                inputs_kernel,
                "inputs",
                [*blocks, down, up],
                [((BLOCK, width), BF), half_b, ((16, 512), BF), low_b, low_b],
                [mix_buffer, group_sem],
                scalars,
                [w_in[l]],
                mflops=420,
            )
            halo = send(last, next_block(False))
            (acts,) = call(
                branch_kernel,
                "branch",
                [normed, lat_b, up],
                [pair_f],
                [mix_buffer, group_sem],
                far=[w_in[l]],
                mflops=420,
            )
        saved, scan, ends = call(
            gates_kernel,
            "gates",
            [inputs, halo, params, gw[l]],
            [((4, BLOCK, 512), F32), pair_f, ((2, 512), F32)],
            [pltpu.VMEM((BLOCK + 16, 512), F32), pltpu.VMEM((BLOCK, 512), F32)],
            scalars,
        )
        carry = entering(ends, core, half, False)
        if l == 0:
            pair, out, carry = lax.optimization_barrier((w_pair[1], w_out[1], carry))
            w_in[1] = lax.all_gather(pair, "y")
            w_back[1] = lax.all_gather(out, "y")
            more, carry = tie(ffn_parts, carry)
            ffn_w[1] = gather_ffn(pack(1, more))
        states, mixed, out_latent, *parts = call(
            mixed_kernel,
            "mixed",
            [carry, scan, acts, down_out, up_out],
            [half_f, half_b, low_b] + rows_like,
            [mix_buffer, pltpu.VMEM((BLOCK, width), BF), group_sem],
            scalars,
            [w_back[l]],
            mflops=420,
        )
        parts = deal4(parts, along_x)
        residual, normed_low = call(
            add_norm_kernel,
            "add_norm",
            [*parts, residual, ffn_gain[l][None]],
            [((HOME, width), F32), ((HOME, width), BF)],
        )
        k.update(
            down=down, up=up, down_out=down_out, up_out=up_out, gw=gw[l], params=params,
            normed=normed, lat_b=lat_b, lat_i=lat_i, acts=acts, saved=saved, scan=scan,
            carry=carry, states=states, mixed=mixed, out_latent=out_latent,
            residual_one=residual,
        )
        if l == 1:
            grad = lax.dynamic_slice(cotangent, start, (1, HOME, width))[0] * valid
            grad_low, _ = tie(grad.astype(BF), carry)
            grad_blocks = gather4(grad_low, ffn_rows)
        blocks = gather4(normed_low, ffn_rows)
        down, up_back = ffn_d[l], back_u[l]
        (ffn_a,) = call(
            join_kernel,
            "join",
            [],
            [((96, 1152), BF)],
            [pltpu.VMEM((4, 32, width), BF), pltpu.VMEM((96, 1152), F32), group_sem],
            far=[ffn_w[l]],
        )
        gate, ups, hidden, latent, back_latent, *parts = call(
            ffn_kernel,
            "ffn",
            [*blocks, ffn_a, down, up_back, mask],
            [((BLOCK, 1152), F32)] * 2
            + [((BLOCK, 1152), BF), ((2, BLOCK, 32), BF), ((BLOCK, 32), BF)]
            + rows_like,
            [pltpu.VMEM((BLOCK, width), BF)] + ffn_buffers + [ffn_sem],
            far=[ffn_w[l]],
            mflops=2800,
            mbytes=15,
        )
        k.update(
            ffn_a=ffn_a, down_two=down, up_back=up_back, blocks=blocks, gate=gate, ups=ups, hidden=hidden,
            latent=latent, back_latent=back_latent,
        )
        out_parts = parts
        if l == 0:
            parts = deal4(parts, ffn_rows)
            residual, normed_low = call(
                add_norm_kernel,
                "add_norm",
                [*parts, residual, mix_gain[1][None]],
                [((HOME, width), F32), ((HOME, width), BF)],
            )
        kept.append(k)
    sums, shards_ = {}, {}
    pair, grad_blocks = tie((w_branch, input_weight), grad_blocks)
    w_in[0] = lax.all_gather(pair_of(0, *pair), "y")
    for l in (1, 0):
        k = kept[l]
        blocks = grad_blocks if l == 1 else gather4(grad_low, ffn_rows)
        if l == 0:
            blocks, side = tie(blocks, side)
            side = steps.send(side)
        g_gate, g_up, g_back, g_latent, rows, *parts = call(
            ffn_back_kernel,
            "ffn_back",
            [*blocks, k["ffn_a"], k["down_two"], k["up_back"], mask, k["gate"], k["ups"]],
            [((BLOCK, 1152), BF)] * 2
            + [((BLOCK, 32), BF), ((2, BLOCK, 32), BF), ((BLOCK, width), BF)]
            + rows_like,
            ffn_buffers + [ffn_sem],
            far=[ffn_w[l]],
            mflops=2800,
            mbytes=15,
        )
        parts = deal4(parts, ffn_rows)
        sums["ffn"] = call(
            ffn_adapters_kernel,
            "ffn_adapters",
            [
                *k["blocks"], rows, k["latent"], k["back_latent"], k["hidden"], g_gate, g_up,
                g_back, g_latent,
            ],
            [((96, width), BF), ((96, 1152), BF)],
            [pltpu.VMEM((BLOCK, width), BF)],
            mflops=200,
        )
        parts, sums["ffn"] = tie(parts, sums["ffn"])
        if l == 0:
            parts, side = tie(parts, side)
            side = steps.send(side)
        grad, grad_low = call(
            norm_back_kernel,
            "norm_back",
            [*parts, grad, k["residual_one"], ffn_gain[l][None]],
            [((HOME, width), F32), ((HOME, width), BF)],
        )
        blocks = gather4(grad_low, along_x)
        shard_part = reduce_shards(sums["ffn"][1])
        if l == 0:
            blocks, side = tie(blocks, side)
        blocks, shard_part = tie(blocks, shard_part)
        rows, g_mixed, g_low, back, ends = call(
            states_back_kernel,
            "states_back",
            [*blocks, k["down_out"], k["up_out"], k["acts"], k["saved"], k["scan"]],
            [((BLOCK, width), BF), half_b, low_b, pair_f, ((2, 512), F32)],
            [mix_buffer, pltpu.VMEM((BLOCK + 8, 512), F32), pltpu.VMEM((BLOCK, 512), F32)]
            + [group_sem],
            scalars,
            [w_back[l]],
            mflops=420,
        )
        if l == 1:
            out_parts, ends = tie(out_parts, ends)
            out_parts = deal4(out_parts, ffn_rows)
        else:
            flat = jnp.concatenate([side[:48], shards_[1], side[48:]], axis=0)
            flat, ends = tie(flat, ends)
            flat = sum_z(flat).astype(BF)
        shard_part, ends = tie(shard_part, ends)
        shards_[l] = blocks_of(halves(shard_part, core, other_core), 48)
        carry = entering(ends, core, half, True)
        part, g_up_out, g_down_out, g_up_b, g_low_b = call(
            branch_back_kernel,
            "branch_back",
            [
                rows, g_mixed, g_low, k["states"], k["acts"], k["mixed"], k["out_latent"],
                k["lat_b"], k["up"], k["down"],
            ],
            [((BLOCK, width), F32), ((RANK, width), F32), ((RANK, 512), F32), ((RANK, 512), F32)]
            + [low_b],
            [mix_buffer, group_sem],
            far=[w_in[l]],
            mflops=420,
        )
        carry, (part, shards_[l]) = tie(carry, (part, shards_[l]))
        if l == 1:
            carry, out_parts = tie(carry, out_parts)
            output, _ = call(
                add_norm_kernel,
                "add_norm",
                [*out_parts, residual, mix_gain[1][None]],
                [((HOME, width), F32), ((HOME, width), BF)],
            )
            output = lax.all_gather((output * valid).astype(BF), ("y", "x"), axis=0, tiled=True)
        else:
            carry, (flat, output) = tie(carry, (flat, output))
            flat = lax.all_gather(flat, ("core", "y", "x")).reshape(2, 4, 4, 304, 128)
        g_conv, rim = call(
            gates_back_kernel,
            "gates_back",
            [
                carry, k["carry"], back, k["states"], k["saved"], k["params"], k["gw"],
            ],
            [half_f, ((8, 512), F32)],
            [pltpu.VMEM((BLOCK + 8, 512), F32)],
            scalars,
        )
        halo = send(rim, next_block(True))
        g_inputs, g_low_i, *parts = call(
            inputs_back_kernel,
            "inputs_back",
            [g_conv, halo, k["params"], k["up"], k["down"], part],
            [half_b, low_b] + rows_like,
            [pltpu.VMEM((BLOCK + 8, 512), F32), mix_buffer, pltpu.VMEM((BLOCK, width), BF)]
            + [group_sem],
            scalars,
            [w_in[l]],
            mflops=420,
        )
        parts = deal4(parts, along_x)
        if l == 1:
            g_low_i, parts[1] = tie(g_low_i, parts[1])
        sums["mix"] = call(
            mix_adapters_kernel,
            "mix_adapters",
            [
                k["normed"], k["lat_i"], g_inputs, g_low_b, g_low_i, g_up_b, g_up_out,
                g_down_out,
            ],
            [((2, 32, width), BF)],
            [
                pltpu.VMEM((48, width), F32), pltpu.VMEM((48, 512), F32),
                pltpu.VMEM((2, 32, width), F32),
            ],
            mflops=60,
        )
        grad, grad_low = call(
            norm_back_kernel,
            "norm_back",
            [*parts, grad, k["residual"], mix_gain[l][None]],
            [((HOME, width), F32), ((HOME, width), BF)],
        )
        steps = reduce_steps(sums["ffn"][0], *sums["mix"])
        side = next(steps)
    grad_tokens = lax.all_gather(grad_low, ("y", "x"), axis=0, tiled=True)
    side = steps.send(side)
    side = steps.send(side)
    last = jnp.concatenate([side[:48], shards_[0], side[48:]], axis=0)
    last = sum_z(last).astype(BF)
    output = widen(output)
    last, output = tie(last, output)
    tables = finish(ids, 1, [flat])
    last = spread_flat(scalars, last)
    ids = jnp.concatenate([ids, core[None].astype(jnp.int32)])
    gmd, gmu, god, gou, gfd, gfu, gbd, gbu = finish(ids, 0, last, tables)
    return (
        output.reshape(tokens.shape),
        widen(grad_tokens).reshape(tokens.shape),
        turned(gmd),
        gmu.reshape(2, 8, 2, RANK, 2048),
        turned(god),
        gou,
        turned(gfd),
        gfu.reshape(2, 8, 2, RANK, 4608),
        turned(gbd),
        gbu,
    )


def solution(mesh):
    grid = Mesh(mesh.devices.reshape(4, 2, 4, 4), ALL)
    sp, mp = ("z", "core"), ("y", "x")
    in_specs = (
        P(None, sp, None),
        P(None, sp, None),
        P(),
        P(),
        P(),
        P(),
        P(None, None, mp),
        P(None, None, mp),
        P(None, None, mp),
        P(None, mp),
        P(None, mp, None, None),
        P(None, mp),
        P(None, mp, None, None),
        P(None, mp),
        P(None, mp),
        P(None, mp, None),
        P(None, None, mp),
        P(None, None, mp),
        P(None, mp, None),
        P(),
        P(None, None, None, None, mp),
        P(None, None, mp, None),
        P(),
        P(),
        P(None, None, None, None, mp),
        P(None, None, mp, None),
        P(),
    )
    out_specs = (P(None, sp, None), P(None, sp, None)) + (P(),) * 8
    return jax.shard_map(shards, mesh=grid, in_specs=in_specs, out_specs=out_specs, check_vma=False)
```

```python
import functools

import jax
import jax.numpy as jnp
from jax import lax
from jax.experimental import pallas as pl
from jax.experimental.pallas import tpu as pltpu
from jax.sharding import Mesh
from jax.sharding import PartitionSpec as P

ALL = ("z", "core", "y", "x")
BF = jnp.bfloat16
F32 = jnp.float32
RANK = 16
HOME = 64
BLOCK = 256
LIMIT = 60 * 2**20
LARGE = 60 * 2**20
GELU_C = 0.7978845608028654


def device_pairs(move):
    pairs = []
    for z in range(4):
        for c in range(2):
            for y in range(4):
                for x in range(4):
                    to = move(z, c, y, x)
                    if to is not None:
                        a = ((z * 2 + c) * 4 + y) * 4 + x
                        b = ((to[0] * 2 + to[1]) * 4 + to[2]) * 4 + to[3]
                        pairs.append((a, b))
    return pairs


def send(value, move):
    return lax.ppermute(value, ALL, device_pairs(move))


def along_x(d):
    return lambda z, c, y, x: (z, c, y, (x + d) % 4)


def along_y(d):
    return lambda z, c, y, x: (z, c, (y + d) % 4, x)


def ffn_rows(d):
    return lambda z, c, y, x: (z, c, y, (x + d) % 4) if c == 0 else (z, c, (y + d) % 4, x)


def ffn_shards(d):
    return lambda z, c, y, x: (z, c, (y + d) % 4, x) if c == 0 else (z, c, y, (x + d) % 4)


def shard_groups():
    at = lambda z, c, y, x: ((z * 2 + c) * 4 + y) * 4 + x
    columns = [[at(z, 0, y, x) for y in range(4)] for z in range(4) for x in range(4)]
    rows = [[at(z, 1, y, x) for x in range(4)] for z in range(4) for y in range(4)]
    return columns + rows


def gather4(value, moves):
    return [value] + [send(value, moves(j)) for j in (1, 2, 3)]


def deal4(parts, moves):
    return [parts[0]] + [send(parts[j], moves(-j)) for j in (1, 2, 3)]


def scatter4(parts, moves):
    moved = deal4(parts, moves)[1:]
    total = parts[0].astype(F32)
    for part in moved:
        total = total + part.astype(F32)
    return total


def split3(v):
    high = v.astype(BF)
    rest = v - high.astype(F32)
    mid = rest.astype(BF)
    return high, mid, (rest - mid.astype(F32)).astype(BF)


def tie(first, second):
    return lax.optimization_barrier((first, second))


def combine(earlier, later):
    return (earlier[0] * later[0], later[0] * earlier[1] + later[1])


def next_block(reverse):
    def move(z, c, y, x):
        at = (z * 2 + c) * 2 + y % 2 + (-1 if reverse else 1)
        if not 0 <= at < 16:
            return None
        return (at // 4, (at // 2) % 2, (y // 2) * 2 + at % 2, x)

    return move


def entering(own, core, half, reverse):
    one = jnp.stack([jnp.ones_like(own[0]), jnp.zeros_like(own[0])])

    def step(own, other, later):
        pre = jnp.where(later, other, one)
        first, second = jnp.where(later, other, own), jnp.where(later, own, other)
        both = combine((first[0], first[1]), (second[0], second[1]))
        return pre, jnp.stack(both)

    other = send(own, lambda z, c, y, x: (z, c, y ^ 1, x))
    pre_h, own = step(own, other, half == (0 if reverse else 1))
    other = send(own, lambda z, c, y, x: (z, 1 - c, y, x))
    pre_c, own = step(own, other, core == (0 if reverse else 1))
    far = []
    for d in (1, 2, 3):
        e = -d if reverse else d
        far.append(
            send(own, lambda z, c, y, x, e=e: (z + e, c, y, x) if 0 <= z + e < 4 else None)
        )
    state = far[2][1]
    for part in (far[1], far[0], pre_c, pre_h):
        state = part[0] * state + part[1]
    return state[None]


def nn(a, b):
    return jnp.dot(a, b, preferred_element_type=F32)


def nt(a, b):
    return lax.dot_general(a, b, (((1,), (1,)), ((), ())), preferred_element_type=F32)


def tn(a, b):
    return lax.dot_general(a, b, (((0,), (0,)), ((), ())), preferred_element_type=F32)


def gelu_pair(v):
    t = jnp.tanh(GELU_C * (v + 0.044715 * v * v * v))
    act = 0.5 * v * (1.0 + t)
    pull = 0.5 * (1.0 + t) + 0.5 * v * (1.0 - t * t) * (GELU_C * (1.0 + 0.134145 * v * v))
    return act, pull


def inverse_rms(v):
    return lax.rsqrt(jnp.mean(v * v, axis=-1, keepdims=True) + 1e-06)


def rms_backward(v, inverse, gain, grad):
    scaled = grad * gain
    return inverse * scaled - v * inverse**3 * jnp.mean(v * scaled, axis=-1, keepdims=True)


VMEM = pl.BlockSpec(memory_space=pltpu.VMEM)
SMEM = pl.BlockSpec(memory_space=pltpu.SMEM)
HBM = pl.BlockSpec(memory_space=pl.ANY)


def grouped(kernel, n_in, n_far):
    def run(sc, *refs):
        kernel(sc, refs[n_in : n_in + n_far], *refs[:n_in], *refs[n_in + n_far :])

    return run


def mixer(kernel, name, ins, outs, scratch, scalars, far):
    return call(
        grouped(kernel, len(ins), len(far)), name, ins, outs, scratch, scalars, far, mflops=420
    )


def call(kernel, name, ins, outs, scratch=(), scalars=None, far=(), mflops=100, mbytes=4):
    specs = [VMEM] * len(ins) + [HBM] * len(far)
    arrays = list(ins) + list(far)
    if scalars is not None:
        specs, arrays = [SMEM] + specs, [scalars] + arrays
    return pl.pallas_call(
        kernel,
        out_shape=[jax.ShapeDtypeStruct(shape, dtype) for shape, dtype in outs],
        in_specs=specs,
        out_specs=[VMEM] * len(outs),
        scratch_shapes=list(scratch),
        compiler_params=pltpu.CompilerParams(
            vmem_limit_bytes=LARGE if mflops > 1000 else LIMIT
        ),
        cost_estimate=pl.CostEstimate(
            flops=mflops * 10**6, bytes_accessed=mbytes * 10**6, transcendentals=0
        ),
        name=name,
    )(*arrays)


def fetch(source, rows, target, sem):
    first, count = rows
    copies = []
    for j in range(4):
        copy = pltpu.make_async_copy(
            source.at[j, pl.ds(first, count)],
            target.at[pl.ds(j * count, count)],
            sem.at[j],
        )
        copy.start()
        copies.append(copy)
    return copies


def fetch_half(sc, mine, other, rows, target, sem):
    first, count = rows
    pieces = []
    for half in range(2):
        low, high = max(first, half * 192), min(first + count, half * 192 + 192)
        if low < high:
            pieces.append((half, low - half * 192, high - low, low - first))
    copies = []
    for core in range(2):

        @pl.when(sc[4] == core)
        def _():
            for i, (half, low, size, at) in enumerate(pieces):
                source = mine if half == core else other
                for j in range(4):
                    pltpu.make_async_copy(
                        source.at[j, pl.ds(low, size)],
                        target.at[pl.ds(j * count + at, size)],
                        sem.at[i, j],
                    ).start()

    for i, (half, low, size, at) in enumerate(pieces):
        for j in range(4):
            copies.append(
                pltpu.make_async_copy(
                    mine.at[j, pl.ds(low, size)],
                    target.at[pl.ds(j * count + at, size)],
                    sem.at[i, j],
                )
            )
    return copies


def weights(sc, w, rows, target, sem):
    if len(w) == 2:
        return fetch_half(sc, *w, rows, target, sem)
    return fetch(w[0], (rows[0] % w[0].shape[1], rows[1]), target, sem.at[0])


def wait_all(copies):
    for copy in copies:
        copy.wait()


def place(scalars, blocks, rows_ref):
    for j in range(4):
        at = pl.multiple_of(lax.rem(scalars[0] + 4 - j, 4) * HOME, HOME)
        rows_ref[pl.ds(at, HOME), :] = blocks[j][...]


def take(scalars, total_ref, parts):
    for j in range(4):
        at = pl.multiple_of(lax.rem(scalars[0] + 4 - j, 4) * HOME, HOME)
        parts[j][...] = total_ref[pl.ds(at, HOME), :]


def scan_rows(reverse, a_ref, b_ref, cum_ref, out_ref):
    rows, width = a_ref.shape
    row = lax.broadcasted_iota(jnp.int32, (8, width), 0)
    groups = rows // 8

    def body(i, carry):
        ca, cb = carry
        at = pl.multiple_of((groups - 1 - i if reverse else i) * 8, 8)
        a, b = a_ref[pl.ds(at, 8), :], b_ref[pl.ds(at, 8), :]
        for k in (1, 2, 4):
            seen = row < 8 - k if reverse else row >= k
            by = 8 - k if reverse else k
            pa = jnp.where(seen, pltpu.roll(a, by, 0), 1.0)
            pb = jnp.where(seen, pltpu.roll(b, by, 0), 0.0)
            b = a * pb + b
            a = a * pa
        b = a * cb + b
        a = a * ca
        cum_ref[pl.ds(at, 8), :] = a
        out_ref[pl.ds(at, 8), :] = b
        last = 0 if reverse else 7
        return (
            jnp.broadcast_to(a[last : last + 1], a.shape),
            jnp.broadcast_to(b[last : last + 1], b.shape),
        )

    start = (jnp.ones((8, width), F32), jnp.zeros((8, width), F32))
    lax.fori_loop(0, groups, body, start, unroll=4)


def add_norm_kernel(l, p0, p1, p2, p3, residual, gain, out, normed):
    total = p0[...].astype(F32) + p1[...].astype(F32) + p2[...].astype(F32)
    v = residual[...] + total + p3[...].astype(F32)
    out[...] = v
    normed[...] = (v * inverse_rms(v) * gain[l : l + 1]).astype(BF)


def norm_back_kernel(l, p0, p1, p2, p3, grad, v_ref, gain, out, low):
    total = p0[...].astype(F32) + p1[...].astype(F32) + p2[...].astype(F32)
    total = total + p3[...].astype(F32)
    v = v_ref[...]
    g = grad[...] + rms_backward(v, inverse_rms(v), gain[l : l + 1], total)
    out[...] = g
    low[...] = g.astype(BF)


def inputs_kernel(
    sc, w, n0, n1, n2, n3, down, up, normed, inputs, last, lat_b, lat_i, wi, sem
):
    copies = weights(sc, w, (128, 128), wi, sem)
    place(sc, (n0, n1, n2, n3), normed)
    rows = normed[...]
    lat_b[...] = nt(rows, down[:RANK]).astype(BF)
    low = nt(rows, down[RANK:]).astype(BF)
    lat_i[...] = low
    wait_all(copies)
    inputs[...] = (nt(rows, wi[...]) + nn(low, up[RANK:])).astype(BF)
    last[...] = inputs[BLOCK - 16 :]


def branch_kernel(sc, w, normed, lat_b, up, acts, wb, sem):
    copies = weights(sc, w, (0, 128), wb, sem)
    wait_all(copies)
    branch = nt(normed[...], wb[...]) + nn(lat_b[...], up[:RANK])
    acts[0], acts[1] = gelu_pair(branch)


def gates_kernel(
    sc, inputs, halo, params, gw, saved, scan, ends, ext, driven
):
    conv, gate_a, gate_i, decay = (saved.at[i] for i in range(4))
    cum, local = scan.at[0], scan.at[1]
    ext[:16] = halo[...].astype(F32)
    ext[16:] = inputs[...].astype(F32)
    value = params[4:5] + params[0:1] * ext[pl.ds(16, BLOCK)]
    for o in (1, 2, 3):
        value = value + params[o : o + 1] * ext[pl.ds(16 - o, BLOCK)]
    conv[...] = value
    row = lax.broadcasted_iota(jnp.int32, (BLOCK, 128), 0)
    first = (row == 0) & (sc[1] == 1)
    for h in range(4):
        at = slice(h * 128, h * 128 + 128)
        c = conv[:, at]
        pre = nn(c.astype(BF), gw[h])
        a = jax.nn.sigmoid(pre[:, :128] + params[5:6, at])
        i = jax.nn.sigmoid(pre[:, 128:] + params[6:7, at])
        d = jnp.exp(a * params[7:8, at])
        gate_a[:, at] = a
        gate_i[:, at] = i
        decay[:, at] = d
        driven[:, at] = c * i * jnp.where(first, 1.0, jnp.sqrt(1.0 - d * d + 0.01))
    scan_rows(False, decay, driven, cum, local)
    ends[0:1] = cum[BLOCK - 1 :]
    ends[1:2] = local[BLOCK - 1 :]


def mixed_kernel(
    sc, w, carry, scan, acts, down_out, up_out, states, mixed, out_latent, q0, q1, q2, q3,
    wo, total, sem,
):
    copies = weights(sc, w, (256, 128), wo, sem)
    s = scan[1] + scan[0] * carry[...]
    states[...] = s
    m = (s * acts[0]).astype(BF)
    mixed[...] = m
    low = nt(m, down_out[...]).astype(BF)
    out_latent[...] = low
    wait_all(copies)
    total[...] = (nn(m, wo[...]) + nn(low, up_out[...])).astype(BF)
    take(sc, total, (q0, q1, q2, q3))


def ffn_kernel(
    n0, n1, n2, n3, a, down, up_back, mask, w, gate, up, hidden, latent, back_latent,
    q0, q1, q2, q3, rows_ref, wg, wu, wd, sem,
):
    cg = fetch(w, (0, 288), wg, sem.at[0])
    cu = fetch(w, (288, 288), wu, sem.at[1])
    cd = fetch(w, (576, 288), wd, sem.at[2])
    for j, n in enumerate((n0, n1, n2, n3)):
        rows_ref[j * HOME : (j + 1) * HOME] = n[...]
    rows = rows_ref[...]
    lat_g = (nt(rows, down[:32]) * mask[...]).astype(BF)
    lat_u = (nt(rows, down[32:]) * mask[...]).astype(BF)
    latent[0] = lat_g
    latent[1] = lat_u
    wait_all(cg)
    g = nt(rows, wg[...]) + nn(lat_g, a[:32])
    gate[...] = g
    wait_all(cu)
    u = nt(rows, wu[...]) + nn(lat_u, a[32:64])
    up[...] = u
    hidden[...] = (gelu_pair(g)[0] * u).astype(BF)
    h = hidden[...]
    low = (nt(h, a[64:]) * mask[...]).astype(BF)
    back_latent[...] = low
    wait_all(cd)
    total = (nn(h, wd[...]) + nn(low, up_back[...])).astype(BF)
    for j, q in enumerate((q0, q1, q2, q3)):
        q[...] = total[j * HOME : (j + 1) * HOME]


def ffn_back_kernel(
    r0, r1, r2, r3, a, down, up_back, mask, gate, up, w, g_gate, g_up, g_back, g_latent, rows_ref,
    q0, q1, q2, q3, wg, wu, wd, sem,
):
    cd = fetch(w, (576, 288), wd, sem.at[2])
    cg = fetch(w, (0, 288), wg, sem.at[0])
    cu = fetch(w, (288, 288), wu, sem.at[1])
    for j, r in enumerate((r0, r1, r2, r3)):
        rows_ref[j * HOME : (j + 1) * HOME] = r[...]
    rows = rows_ref[...]
    low = (nt(rows, up_back[...]) * mask[...]).astype(BF)
    g_back[...] = low
    wait_all(cd)
    gh = (nt(rows, wd[...]) + nn(low, a[64:])).astype(BF).astype(F32)
    act, pull = gelu_pair(gate[...])
    g_up[...] = (gh * act).astype(BF)
    g_gate[...] = (gh * up[...] * pull).astype(BF)
    gg, gu = g_gate[...], g_up[...]
    lat_g = (nt(gg, a[:32]) * mask[...]).astype(BF)
    lat_u = (nt(gu, a[32:64]) * mask[...]).astype(BF)
    g_latent[0] = lat_g
    g_latent[1] = lat_u
    wait_all(cg)
    total = nn(gg, wg[...]) + nn(lat_g, down[:32]) + nn(lat_u, down[32:])
    wait_all(cu)
    total = (total + nn(gu, wu[...])).astype(BF)
    for j, q in enumerate((q0, q1, q2, q3)):
        q[...] = total[j * HOME : (j + 1) * HOME]


def ffn_adapters_kernel(
    n0, n1, n2, n3, rows, latent, back_latent, hidden, g_gate, g_up, g_back, g_latent,
    whole, split, normed_ref,
):
    for j, n in enumerate((n0, n1, n2, n3)):
        normed_ref[j * HOME : (j + 1) * HOME] = n[...]
    normed = normed_ref[...]
    g_down = [tn(g_latent[0], normed), tn(g_latent[1], normed)]
    g_up_back = tn(back_latent[...], rows[...])
    for s in range(2):
        at = slice(s * RANK, s * RANK + RANK)
        whole[s * 48 : s * 48 + 16] = g_down[0][at].astype(BF)
        whole[s * 48 + 16 : s * 48 + 32] = g_down[1][at].astype(BF)
        whole[s * 48 + 32 : s * 48 + 48] = g_up_back[at].astype(BF)
    split[:32] = tn(latent[0], g_gate[...]).astype(BF)
    split[32:64] = tn(latent[1], g_up[...]).astype(BF)
    split[64:] = tn(g_back[...], hidden[...]).astype(BF)


def states_back_kernel(
    sc, w, r0, r1, r2, r3, down_out, up_out, acts, saved, scan,
    rows_ref, g_mixed, g_low, back, ends, wo, ext, g_states, sem,
):
    decay, cum, suffix, local = saved.at[3], scan.at[0], back.at[0], back.at[1]
    copies = weights(sc, w, (256, 128), wo, sem)
    place(sc, (r0, r1, r2, r3), rows_ref)
    rows = rows_ref[...]
    low = nt(rows, up_out[...]).astype(BF)
    g_low[...] = low
    ext[:BLOCK] = decay[...]
    ext[BLOCK:] = jnp.ones((8, 512), F32)
    ext[:BLOCK] = ext[pl.ds(1, BLOCK)]
    wait_all(copies)
    gm = (nt(rows, wo[...]) + nn(low, down_out[...])).astype(BF)
    g_mixed[...] = gm
    g_states[...] = gm.astype(F32) * acts[0]
    scan_rows(True, ext.at[pl.ds(0, BLOCK)], g_states, suffix, local)
    ends[0:1] = cum[BLOCK - 1 :]
    ends[1:2] = decay[0:1] * local[0:1]


def branch_back_kernel(
    sc, w, rows, g_mixed, g_low, states, acts, mixed, out_latent, lat_b, up, down,
    part, g_up_out, g_down_out, g_up_b, g_branch_low, wb, sem,
):
    copies = weights(sc, w, (0, 128), wb, sem)
    gb = (g_mixed[...].astype(F32) * states[...] * acts[1]).astype(BF)
    low = nt(gb, up[:RANK]).astype(BF)
    g_branch_low[...] = low
    g_up_out[...] = tn(out_latent[...], rows[...])
    g_down_out[...] = tn(g_low[...], mixed[...])
    g_up_b[...] = tn(lat_b[...], gb)
    wait_all(copies)
    part[...] = nn(gb, wb[...]) + nn(low, down[:RANK])


def gates_back_kernel(
    sc, carry, carry_in, back, states, saved, params, gw, g_conv, rim, ext
):
    conv, gate_a, gate_i, decay = (saved.at[i] for i in range(4))
    suffix, local = back.at[0], back.at[1]
    ext[:8] = jnp.broadcast_to(carry_in[...], (8, 512))
    ext[8:] = states[...]
    row = lax.broadcasted_iota(jnp.int32, (BLOCK, 128), 0)
    first = (row == 0) & (sc[1] == 1)
    for h in range(4):
        at = slice(h * 128, h * 128 + 128)
        gd = local[:, at] + suffix[:, at] * carry[:, at]
        d, i, a, c = decay[:, at], gate_i[:, at], gate_a[:, at], conv[:, at]
        scale = jnp.where(first, 1.0, jnp.sqrt(1.0 - d * d + 0.01))
        g_scale = gd * c * i
        previous = ext[pl.ds(7, BLOCK), at]
        g_decay = gd * previous - jnp.where(first, 0.0, g_scale * (d / scale))
        ga = (g_decay * d * params[7:8, at] * a * (1.0 - a)).astype(BF)
        gi = (g_scale * scale * (1.0 - i)).astype(BF)
        g_conv[:, at] = gd * i * scale + nt(ga, gw[h, :, :128]) + nt(gi, gw[h, :, 128:])
    rim[...] = g_conv[:8]


def inputs_back_kernel(
    sc, w, g_conv, halo, params, up, down, part, normed, lat_i, g_low_b, g_up_b, g_up_out,
    g_down_out, ffn_whole, q0, q1, q2, q3, mine, theirs, ext, wi, total, whole, split, wide, sem,
):
    copies = weights(sc, w, (128, 128), wi, sem)
    ext[:BLOCK] = g_conv[...]
    ext[BLOCK:] = halo[...]
    value = params[0:1] * ext[:BLOCK]
    for o in (1, 2, 3):
        value = value + params[o : o + 1] * ext[pl.ds(o, BLOCK)]
    gi = value.astype(BF)
    low = nt(gi, up[RANK:]).astype(BF)
    whole[:RANK] = tn(g_low_b[...], normed[...])
    whole[RANK:32] = tn(low, normed[...])
    whole[32:] = g_up_out[...]
    split[:RANK] = g_up_b[...]
    split[RANK:32] = tn(lat_i[...], gi)
    split[32:] = g_down_out[...]
    for c in range(2):
        wide[c, :48] = ffn_whole[c * 48 : c * 48 + 48].astype(F32)
        wide[c, 48:72] = whole[c * 24 : c * 24 + 24]
        for i in range(3):
            at = c * 24 + i * 8
            wide[c, 72:, i * 512 : i * 512 + 512] = split[at : at + 8]
    mine[...] = wide[sc[4]]
    theirs[...] = wide[1 - sc[4]].astype(BF)
    wait_all(copies)
    total[...] = (part[...] + nn(gi, wi[...]) + nn(low, down[RANK:])).astype(BF)
    take(sc, total, (q0, q1, q2, q3))


def head_kernel(
    sc, tokens, down, up, gain, wb, wi, o0, o1, o2, o3, normed, lat_b, lat_i, w
):
    j = pl.program_id(0)

    @pl.when(j == 0)
    def _():
        w[:, :128] = wb[0]
        w[:, 128:] = wi[0]

    v = tokens[0]
    rows = (v * inverse_rms(v) * gain[0:1]).astype(BF)
    low_b = nt(rows, down[0, 0, :RANK]).astype(BF)
    low_i = nt(rows, down[0, 0, RANK:]).astype(BF)
    both = nn(rows, w[...])
    branch = (both[:, :128] + nn(low_b, up[0, 0, :RANK])).astype(BF)
    inputs = (both[:, 128:] + nn(low_i, up[0, 0, RANK:])).astype(BF)
    for i, out in enumerate((o0, o1, o2, o3)):

        @pl.when(j == i)
        def _():
            out[:, :128] = branch
            out[:, 128:] = inputs

    @pl.when(j == 0)
    def _():
        normed[...] = rows
        lat_b[...] = low_b
        lat_i[...] = low_i


def head(scalars, tokens, down, up, gain, wb, wi):
    at = lambda j, sc: lax.rem(sc[0] + 4 - j, 4)
    own = lambda j, sc: (0, sc[1 + at(j, sc) // 2], 0, 0)
    fixed = lambda j, sc: (0, 0)
    block = ((BLOCK, 256), BF)
    outs = [block] * 4 + [((BLOCK, 1536), BF), ((BLOCK, RANK), BF), ((BLOCK, RANK), BF)]
    return pl.pallas_call(
        head_kernel,
        out_shape=[jax.ShapeDtypeStruct(shape, dtype) for shape, dtype in outs],
        grid_spec=pltpu.PrefetchScalarGridSpec(
            num_scalar_prefetch=1,
            grid=(4,),
            in_specs=[
                pl.BlockSpec((1, BLOCK, 1536), lambda j, sc: (at(j, sc) // 2, at(j, sc) % 2, 0)),
                pl.BlockSpec((1, 1, 32, 1536), own),
                pl.BlockSpec((1, 1, 32, 128), own),
                pl.BlockSpec((2, 1536), fixed),
                pl.BlockSpec((1, 1536, 128), lambda j, sc: (0, 0, 0)),
                pl.BlockSpec((1, 1536, 128), lambda j, sc: (0, 0, 0)),
            ],
            out_specs=[pl.BlockSpec(shape, fixed) for shape, _ in outs],
            scratch_shapes=[pltpu.VMEM((1536, 256), BF)],
        ),
        compiler_params=pltpu.CompilerParams(vmem_limit_bytes=LIMIT),
        cost_estimate=pl.CostEstimate(
            flops=900 * 10**6, bytes_accessed=9 * 10**6, transcendentals=0
        ),
        name="head",
    )(scalars, tokens, down, up, gain, wb, wi)


def prepare_kernel(
    sc, md, ou, fd0, fd1, bu0, bu1, mu0, mu1, od0, od1, fu0, fu1, bd0, bd1,
    ga, gi, cw, cb, ab, ib, dp, mix_d0, mix_d1, out_u0, out_u1, ffn_d0, ffn_d1, back_u0, back_u1,
    small, ffn_small,
):
    l = pl.program_id(0)
    for i, (mix_d, out_u, ffn_d, back_u) in enumerate(
        ((mix_d0, out_u0, ffn_d0, back_u0), (mix_d1, out_u1, ffn_d1, back_u1))
    ):

        @pl.when(l == i)
        def _():
            mix_d[...] = md[0, 0]
            out_u[...] = ou[0, 0]
            for s, (fd, bu) in enumerate(((fd0, bu0), (fd1, bu1))):
                ffn_d[s * 16 : s * 16 + 16] = fd[0, 0, :16]
                ffn_d[32 + s * 16 : 48 + s * 16] = fd[0, 0, 16:]
                back_u[s * 16 : s * 16 + 16] = bu[0, 0]

    ffn_small[...] = jnp.zeros(ffn_small.shape, BF)
    small[0, :128] = ga[0, 0]
    small[0, 128:256] = gi[0, 0]
    for s, (mu, od, fu, bd) in enumerate(((mu0, od0, fu0, bd0), (mu1, od1, fu1, bd1))):
        small[0, 256 + s * 32 : 288 + s * 32] = mu[0, 0]
        small[0, 320 + s * 16 : 336 + s * 16] = od[0, 0]
        at = slice(s * 16, s * 16 + 16)
        ffn_small[0, at, :288] = fu[0, 0, :16]
        ffn_small[0, at, 384:672] = fu[0, 0, 16:]
        ffn_small[0, at, 768:1056] = bd[0, 0]
    vectors = [ref[pl.ds(l, 1), :] for ref in (cb, ab, ib, dp)]
    wide = jnp.concatenate([cw[0]] + vectors + [jnp.zeros((8, 128), F32)], axis=0)
    for i, part in enumerate(split3(wide)):
        small[0, 352 + 16 * i : 368 + 16 * i] = part


def prepare(picks, owned, tables, singles, vectors):
    specs, arrays = [], []
    for table, which in [(t, (2,)) for t in owned] + [(t, (0, 1)) for t in tables]:
        for s in which:
            specs.append(
                pl.BlockSpec((1, 1) + table.shape[2:], lambda l, sc, s=s: (l, sc[s], 0, 0))
            )
            arrays.append(table)
    for single in singles:
        dims = single.ndim - 1
        specs.append(
            pl.BlockSpec((1,) + single.shape[1:], lambda l, sc, dims=dims: (l,) + (0,) * dims)
        )
        arrays.append(single)
    for vector in vectors:
        specs.append(pl.BlockSpec(vector.shape, lambda l, sc: (0, 0)))
        arrays.append(vector)
    flat = [(32, 1536), (16, 1536), (64, 1536), (32, 1536)]
    flat = [shape for shape in flat for _ in range(2)]
    tall = [(400, 128), (32, 1536)]
    return pl.pallas_call(
        prepare_kernel,
        out_shape=[jax.ShapeDtypeStruct(shape, BF) for shape in flat]
        + [jax.ShapeDtypeStruct((2,) + shape, BF) for shape in tall],
        grid_spec=pltpu.PrefetchScalarGridSpec(
            num_scalar_prefetch=1,
            grid=(2,),
            in_specs=specs,
            out_specs=[pl.BlockSpec(shape, lambda l, sc: (0, 0)) for shape in flat]
            + [pl.BlockSpec((1,) + shape, lambda l, sc: (l, 0, 0)) for shape in tall],
        ),
        compiler_params=pltpu.CompilerParams(vmem_limit_bytes=LIMIT),
        cost_estimate=pl.CostEstimate(flops=10**6, bytes_accessed=4 * 10**6, transcendentals=0),
        name="prepare",
    )(picks, *arrays)


def arrange_kernel(sc, s0, s1, s2, s3, *refs):
    small = refs[-1]
    for j, block in enumerate((s0, s1, s2, s3)):
        small[lax.rem(sc[2] + 4 - j, 4)] = block[...]
    seq = sc[2] // 2
    for l in range(2):
        gw, up, down_out, params = refs[l * 4 : l * 4 + 4]
        for p in range(4):
            at = slice(p * 128, p * 128 + 128)
            gw[p, :, :128] = small[p, l, :128]
            gw[p, :, 128:] = small[p, l, 128:256]
            start = pl.multiple_of(256 + seq * 32, 32)
            up[:, at] = small[p, l, pl.ds(start, 32), :]
            start = pl.multiple_of(320 + seq * 16, 16)
            down_out[:, at] = small[p, l, pl.ds(start, 16), :]
            parts = [small[p, l, 352 + 16 * i : 368 + 16 * i].astype(F32) for i in range(3)]
            total = parts[0] + parts[1] + parts[2]
            params[:, at] = total[:8]
            params[7:8, at] = -8.0 * jax.nn.softplus(total[7:8])


def join_kernel(w, a, held, wide, sem):
    copies = []
    for j in range(4):
        copy = pltpu.make_async_copy(w.at[j, pl.ds(864, 32)], held.at[j], sem.at[j])
        copy.start()
        copies.append(copy)
    wait_all(copies)
    for j in range(4):
        for i in range(3):
            part = held[j, :, i * 384 : i * 384 + 288].astype(F32)
            wide[i * 32 : i * 32 + 32, j * 288 : j * 288 + 288] = part
    a[...] = wide[...].astype(BF)


def order_kernel(sc, b0, b1, b2, b3, out):
    for j, block in enumerate((b0, b1, b2, b3)):
        out[lax.rem(sc[2] + 4 - j, 4)] = block[...]


def order_x_kernel(sc, b0, b1, b2, b3, out):
    for j, block in enumerate((b0, b1, b2, b3)):
        out[lax.rem(sc[0] + 4 - j, 4)] = block[...]


def unpack_kernel(sc, b0, b1, b2, b3, inputs, last, acts, held):
    for j, block in enumerate((b0, b1, b2, b3)):
        held[lax.rem(sc[2] + j, 4)] = block[...]
    for p in range(4):
        at = slice(p * 128, p * 128 + 128)
        inputs[:, at] = held[p, :, 128:]
        acts[0, :, at], acts[1, :, at] = gelu_pair(held[p, :, :128].astype(F32))
    last[...] = inputs[BLOCK - 16 :]


def pack_kernel(a_ref, b_ref, c_ref, d_ref, out):
    at = 0
    for ref in (a_ref, b_ref, c_ref, d_ref):
        count = ref.shape[1]
        out[at : at + count] = ref[0]
        at += count


def pack(l, parts):
    width = parts[0].shape[2]
    total = sum(part.shape[1] for part in parts)
    return pl.pallas_call(
        pack_kernel,
        out_shape=jax.ShapeDtypeStruct((total, width), BF),
        grid=(2,),
        in_specs=[pl.BlockSpec((1, p.shape[1], width // 2), lambda i: (l, 0, i)) for p in parts],
        out_specs=pl.BlockSpec((total, width // 2), lambda i: (0, i)),
        compiler_params=pltpu.CompilerParams(vmem_limit_bytes=LIMIT),
        cost_estimate=pl.CostEstimate(flops=0, bytes_accessed=5 * 10**6, transcendentals=0),
        name="pack",
    )(*parts)


def pair_kernel(a_ref, b_ref, out):
    out[:128] = a_ref[0].T
    out[128:] = b_ref[0].T


def pair_of(l, a, b):
    rows = a.shape[1] // 3
    piece = pl.BlockSpec((1, rows, 128), lambda i: (l, i, 0))
    return pl.pallas_call(
        pair_kernel,
        out_shape=jax.ShapeDtypeStruct((256, a.shape[1]), BF),
        grid=(3,),
        in_specs=[piece] * 2,
        out_specs=pl.BlockSpec((256, rows), lambda i: (0, i)),
        compiler_params=pltpu.CompilerParams(vmem_limit_bytes=LIMIT),
        cost_estimate=pl.CostEstimate(flops=0, bytes_accessed=2 * 10**6, transcendentals=0),
        name="pair",
    )(a, b)


def half_kernel(sc, a_ref, b_ref, c_ref, out):
    @pl.when(sc[4] == 0)
    def _():
        out[:128] = a_ref[0].T
        out[128:] = b_ref[0, :, :].T[:64]

    @pl.when(sc[4] == 1)
    def _():
        out[:64] = b_ref[0, :, :].T[64:]
        out[64:] = c_ref[0]


def half_of(scalars, l, a, b, c):
    rows = a.shape[1] // 3
    piece = pl.BlockSpec((1, rows, 128), lambda i, sc: (l, i, 0))
    return pl.pallas_call(
        half_kernel,
        out_shape=jax.ShapeDtypeStruct((192, a.shape[1]), BF),
        grid_spec=pltpu.PrefetchScalarGridSpec(
            num_scalar_prefetch=1,
            grid=(3,),
            in_specs=[piece] * 2 + [pl.BlockSpec((1, 128, rows), lambda i, sc: (l, 0, i))],
            out_specs=pl.BlockSpec((192, rows), lambda i, sc: (0, i)),
        ),
        compiler_params=pltpu.CompilerParams(vmem_limit_bytes=LIMIT),
        cost_estimate=pl.CostEstimate(flops=0, bytes_accessed=2 * 10**6, transcendentals=0),
        name="half",
    )(scalars, a, b, c)


def finish_kernel(ranked, sc, *refs):
    mix_d, mix_u, out_d, out_u, ffn_d, ffn_u, back_d, back_u, whole, shard, split = refs[-11:]
    a = pl.program_id(0)

    @pl.when(a == 0)
    def _():
        for c in range(2):
            for y in range(4):
                for x in range(4):
                    if ranked:
                        mine, other = (ref[x, y].astype(F32) for ref in refs[:2])
                        v = jnp.where(sc[2] == c, mine, other)
                    else:
                        v = refs[0][c, y, x].astype(F32)
                    row = c * 24 + (y % 2) * 12
                    for k in range(3):
                        lane = x * 384 + k * 128
                        whole[c, y * 12 : y * 12 + 12, lane : lane + 128] = v[
                            k * 16 : k * 16 + 12
                        ]
                        whole[y // 2, 48 + row : 60 + row, lane : lane + 128] = v[
                            192 + k * 16 : 204 + k * 16
                        ]
                        lane = (y * 4 + x) * 288 + k * 128
                        part = v[48 + k * 48 : 96 + k * 48]
                        wide = 32 if k == 2 else 128
                        shard[c * 48 : c * 48 + 48, lane : lane + wide] = part[:, :wide]
                    for p in range(4):
                        lane = (p * 4 + x) * 128
                        k = 192 + (3 + p) * 16
                        split[y // 2, row : row + 12, lane : lane + 128] = v[k : k + 12]

    w = [((sc[s] == sc[0]) == (sc[a] == sc[0])).astype(F32) for s in range(2)]
    both = lambda get: get(0) * w[0] + get(1) * w[1]
    ffn_d[0, 0] = both(lambda s: whole[s, :32])
    back_u[0, 0] = both(lambda s: whole[s, 32:48])
    mix_d[0, 0] = both(lambda s: whole[s, 48:80])
    out_u[0, 0] = both(lambda s: whole[s, 80:])
    ffn_u[0, 0, :16] = both(lambda s: shard[s * 16 : s * 16 + 16])
    ffn_u[0, 0, 16:] = both(lambda s: shard[32 + s * 16 : 48 + s * 16])
    back_d[0, 0] = both(lambda s: shard[64 + s * 16 : 80 + s * 16])
    mix_u[0, 0] = both(lambda s: split[s, :32])
    out_d[0, 0] = both(lambda s: split[s, 32:])


TABLES = [(32, 1536), (32, 2048), (16, 2048), (16, 1536), (32, 1536), (32, 4608), (16, 4608)]
TABLES.append((16, 1536))


def zeros_kernel(*refs):
    for ref in refs:
        ref[...] = jnp.zeros(ref.shape, F32)


def empty_tables():
    return pl.pallas_call(
        zeros_kernel,
        out_shape=[jax.ShapeDtypeStruct((2, 8) + shape, F32) for shape in TABLES],
        grid=(2, 4),
        out_specs=[pl.BlockSpec((1, 2) + shape, lambda l, a: (l, a, 0, 0)) for shape in TABLES],
        compiler_params=pltpu.CompilerParams(vmem_limit_bytes=LIMIT),
        cost_estimate=pl.CostEstimate(flops=10**6, bytes_accessed=20 * 10**6, transcendentals=0),
        name="zeros",
    )()


def finish(ids, layer, flats, tables):
    return pl.pallas_call(
        functools.partial(finish_kernel, len(flats) == 2),
        out_shape=[jax.ShapeDtypeStruct((2, 8) + shape, F32) for shape in TABLES],
        grid_spec=pltpu.PrefetchScalarGridSpec(
            num_scalar_prefetch=1,
            grid=(2,),
            in_specs=[VMEM] * len(flats) + [HBM] * len(tables),
            out_specs=[
                pl.BlockSpec((1, 1) + shape, lambda a, sc: (layer, sc[a], 0, 0))
                for shape in TABLES
            ],
            scratch_shapes=[
                pltpu.VMEM((2, 96, 1536), F32),
                pltpu.VMEM((96, 4608), F32),
                pltpu.VMEM((2, 48, 2048), F32),
            ],
        ),
        input_output_aliases={1 + len(flats) + i: i for i in range(len(tables))},
        compiler_params=pltpu.CompilerParams(vmem_limit_bytes=LIMIT),
        cost_estimate=pl.CostEstimate(flops=10**7, bytes_accessed=4 * 10**6, transcendentals=0),
        name="finish",
    )(ids, *flats, *tables)


def widen_kernel(v, out):
    out[...] = v[...].astype(F32)


def widen(v):
    rows, width = v.shape
    spec = pl.BlockSpec((BLOCK, width), lambda i: (i, 0))
    return pl.pallas_call(
        widen_kernel,
        out_shape=jax.ShapeDtypeStruct(v.shape, F32),
        grid=(rows // BLOCK,),
        in_specs=[spec],
        out_specs=spec,
        cost_estimate=pl.CostEstimate(flops=10**6, bytes_accessed=10**7, transcendentals=0),
        name="widen",
    )(v)


def other_core(z, c, y, x):
    return (z, 1 - c, y, x)


def other_half(z, c, y, x):
    return (z, c, y ^ 1, x)


def along_z(d):
    return lambda z, c, y, x: ((z + d) % 4, c, y, x)


def halves(value, index, move):
    count = value.shape[0] // 2
    mine = lax.dynamic_slice_in_dim(value, index * count, count, 0)
    theirs = lax.dynamic_slice_in_dim(value, (1 - index) * count, count, 0)
    return mine.astype(F32) + send(theirs, move).astype(F32)


def ring_scatter(value, index, moves, axis):
    count = value.shape[axis] // 4
    parts = [
        lax.dynamic_slice_in_dim(value, ((index - j) % 4) * count, count, axis) for j in range(4)
    ]
    return scatter4(parts, moves)


def sum_z(value):
    low = value.astype(BF)
    total = value
    for d in (1, 2, 3):
        total = total + send(low, along_z(d)).astype(F32)
    return total.astype(BF)


def blocks_of(v, rows):
    n, width = v.shape
    v = jnp.pad(v, ((0, rows - n), (0, -width % 128)))
    return jnp.concatenate([v[:, i : i + 128] for i in range(0, width, 128)], axis=0)


def reduce_shards(split):
    core, x, y = lax.axis_index("core"), lax.axis_index("x"), lax.axis_index("y")
    group = jnp.where(core == 0, y, x)
    shard = split.astype(BF).reshape(96, 4, 288).transpose(1, 0, 2)
    return ring_scatter(shard, group, ffn_shards, 0)[0]


def reduce_steps(mine, theirs):
    x, y = lax.axis_index("x"), lax.axis_index("y")
    part = mine + send(theirs, other_core).astype(F32)
    part = yield part
    split = jnp.concatenate([part[72:, i * 512 : i * 512 + 512] for i in range(3)], axis=0)
    whole = ring_scatter(part[:72].astype(BF), x, along_x, 1)
    whole, split = yield whole, split
    mix = jnp.concatenate([whole[48:], split], axis=1)
    pieces = []
    for q in range(4):
        here = jnp.where(y // 2 == q // 2, mix[(q % 2) * 12 : (q % 2) * 12 + 12], 0.0)
        pieces.append(jnp.concatenate([whole[q * 12 : q * 12 + 12], here], axis=1))
    part = ring_scatter(jnp.stack(pieces).astype(BF), y, along_y, 0)[0]
    yield blocks_of(part, 16)


def shards(
    tokens,
    cotangent,
    lengths,
    adapter_ids,
    mix_gain,
    ffn_gain,
    w_branch,
    input_weight,
    conv_weight,
    conv_bias,
    gate_a_weight,
    gate_a_bias,
    gate_i_weight,
    gate_i_bias,
    decay_param,
    w_out,
    w_gate,
    w_up,
    w_down,
    mix_down,
    mix_up,
    out_down,
    out_up,
    ffn_down,
    ffn_up,
    back_down,
    back_up,
):
    width = tokens.shape[2]
    z, core = lax.axis_index("z"), lax.axis_index("core")
    y, x = lax.axis_index("y"), lax.axis_index("x")
    seq, half = y // 2, y % 2
    w_back = lax.all_gather(w_out[0], "y")
    ids = adapter_ids
    ffn_group = jnp.where(core == 0, y, x)
    first = (z + core + half == 0).astype(jnp.int32)
    scalars = jnp.stack([x, first, y, ffn_group, core]).astype(jnp.int32)
    turned = lambda v: jnp.swapaxes(v, -1, -2)
    mix_down_t = turned(mix_down)
    mix_up_f = mix_up.reshape(2, 8, 32, 128)
    *local, normed_0, lat_b_0, lat_i_0 = head(
        jnp.stack([y, ids[0], ids[1]]),
        tokens,
        mix_down_t,
        mix_up_f,
        mix_gain,
        w_branch,
        input_weight,
    )
    mine = local[0]
    local = deal4(local, along_y)
    ffn_parts = [turned(w_gate), turned(w_up), w_down]
    gather_ffn = lambda v: lax.all_gather(v, ALL, axis=0, axis_index_groups=shard_groups())
    picked, mine = tie(ids, mine)
    prepared = prepare(
        jnp.concatenate([picked, lax.dynamic_index_in_dim(picked, seq, 0)]),
        [mix_down_t, out_up],
        [
            turned(ffn_down), back_up, mix_up_f, turned(out_down),
            ffn_up.reshape(2, 8, 32, 288), turned(back_down),
        ],
        [gate_a_weight, gate_i_weight, conv_weight],
        [conv_bias, gate_a_bias, gate_i_bias, decay_param],
    )
    mix_d, out_u, ffn_d, back_u = (prepared[i : i + 2] for i in (0, 2, 4, 6))
    small, ffn_small = prepared[8:]
    more, mine = tie(ffn_parts, mine)
    ffn_parts.append(ffn_small)
    packed, local = tie(pack(0, more + [ffn_small]), local)
    ffn_w = [gather_ffn(packed), None]
    arranged = call(
        arrange_kernel,
        "arrange",
        gather4(small, along_y),
        [((4, 128, 256), BF), ((32, 512), BF), ((16, 512), BF), ((8, 512), F32)] * 2,
        [pltpu.VMEM((4, 2, 400, 128), BF)],
        scalars,
    )
    w_mix = {}
    start = (seq, half * BLOCK + x * HOME, 0)
    residual = lax.dynamic_slice(tokens, start, (1, HOME, width))[0]
    position = (z * 2 + core) * 512 + half * BLOCK + x * HOME + jnp.arange(HOME)
    valid = (position < lengths[seq]).astype(F32)[:, None]
    of_rows = jnp.where(core == 0, y, (y - jnp.arange(4)) % 4) // 2
    of_rows = jnp.repeat(of_rows, HOME)[:, None]
    of_cols = jnp.arange(32) // RANK
    mask = (of_rows == of_cols[None, :]).astype(F32)
    rows_like = [((HOME, width), BF)] * 4
    group_sem = pltpu.SemaphoreType.DMA((2, 4))
    ffn_sem = pltpu.SemaphoreType.DMA((3, 4))
    ffn_buffers = [pltpu.VMEM((1152, width), BF)] * 3
    mix_buffer = pltpu.VMEM((512, width), BF)
    half_f = ((BLOCK, 512), F32)
    pair_f = ((2, BLOCK, 512), F32)
    half_b = ((BLOCK, 512), BF)
    low_b = ((BLOCK, RANK), BF)

    kept = []
    for l in range(2):
        k = {"residual": residual}
        down, up_out = mix_d[l], out_u[l]
        gw, up, down_out, params = arranged[l * 4 : l * 4 + 4]
        if l == 0:
            normed, lat_b, lat_i = normed_0, lat_b_0, lat_i_0
            inputs, last, acts = call(
                unpack_kernel,
                "unpack",
                local,
                [half_b, ((16, 512), BF), pair_f],
                [pltpu.VMEM((4, BLOCK, 256), BF)],
                scalars,
            )
            halo = send(last, next_block(False))
        else:
            blocks = gather4(normed_low, along_x)
            packed, _ = tie(packed, (mine, blocks))
            ffn_w[1] = gather_ffn(packed)
            w_mix[1] = [mine, send(mine, other_core)]
            normed, inputs, last, lat_b, lat_i = mixer(
                inputs_kernel,
                "inputs",
                [*blocks, down, up],
                [((BLOCK, width), BF), half_b, ((16, 512), BF), low_b, low_b],
                [mix_buffer, group_sem],
                scalars,
                w_mix[l],
            )
            halo = send(last, next_block(False))
            (acts,) = mixer(
                branch_kernel,
                "branch",
                [normed, lat_b, up],
                [pair_f],
                [mix_buffer, group_sem],
                scalars,
                w_mix[l],
            )
        saved, scan, ends = call(
            gates_kernel,
            "gates",
            [inputs, halo, params, gw],
            [((4, BLOCK, 512), F32), pair_f, ((2, 512), F32)],
            [pltpu.VMEM((BLOCK + 16, 512), F32), pltpu.VMEM((BLOCK, 512), F32)],
            scalars,
        )
        carry = entering(ends, core, half, False)
        w_back_l = [w_back] if l == 0 else w_mix[1]
        states, mixed, out_latent, *parts = mixer(
            mixed_kernel,
            "mixed",
            [carry, scan, acts, down_out, up_out],
            [half_f, half_b, low_b] + rows_like,
            [mix_buffer, pltpu.VMEM((BLOCK, width), BF), group_sem],
            scalars,
            w_back_l,
        )
        if l == 0:
            (halves_of, more), _ = tie(((w_branch, input_weight, w_out), ffn_parts), parts[0])
            mine, packed = half_of(scalars, 1, *halves_of), pack(1, more)
        parts = deal4(parts, along_x)
        if l == 0:
            parts, w_pair = tie(parts, pair_of(0, w_branch, input_weight))
        residual, normed_low = call(
            functools.partial(add_norm_kernel, l),
            "add_norm",
            [*parts, residual, ffn_gain],
            [((HOME, width), F32), ((HOME, width), BF)],
        )
        k.update(
            down=down, up=up, down_out=down_out, up_out=up_out, gw=gw, params=params,
            normed=normed, lat_b=lat_b, lat_i=lat_i, acts=acts, saved=saved, scan=scan,
            carry=carry, states=states, mixed=mixed, out_latent=out_latent,
            residual_one=residual,
        )
        if l == 1:
            grad = lax.dynamic_slice(cotangent, start, (1, HOME, width))[0] * valid
            grad_low, _ = tie(grad.astype(BF), carry)
            grad_blocks = gather4(grad_low, ffn_rows)
        blocks = gather4(normed_low, ffn_rows)
        if l == 0:
            mine, _ = tie(mine, (ffn_w[0], blocks))
            mine = lax.all_gather(mine, "y")
        down, up_back = ffn_d[l], back_u[l]
        (ffn_a,) = call(
            join_kernel,
            "join",
            [],
            [((96, 1152), BF)],
            [
                pltpu.VMEM((4, 32, width), BF), pltpu.VMEM((96, 1152), F32),
                pltpu.SemaphoreType.DMA((4,)),
            ],

            far=[ffn_w[l]],
        )
        gate, ups, hidden, latent, back_latent, *parts = call(
            ffn_kernel,
            "ffn",
            [*blocks, ffn_a, down, up_back, mask],
            [((BLOCK, 1152), F32)] * 2
            + [((BLOCK, 1152), BF), ((2, BLOCK, 32), BF), ((BLOCK, 32), BF)]
            + rows_like,
            [pltpu.VMEM((BLOCK, width), BF)] + ffn_buffers + [ffn_sem],
            far=[ffn_w[l]],
            mflops=2800,
            mbytes=15,
        )
        k.update(
            ffn_a=ffn_a, down_two=down, up_back=up_back, blocks=blocks, gate=gate, ups=ups, hidden=hidden,
            latent=latent, back_latent=back_latent,
        )
        out_parts = parts
        if l == 0:
            parts, tables = tie(deal4(parts, ffn_rows), empty_tables())
            residual, normed_low = call(
                functools.partial(add_norm_kernel, 1),
                "add_norm",
                [*parts, residual, mix_gain],
                [((HOME, width), F32), ((HOME, width), BF)],
            )
        kept.append(k)
    for l in (1, 0):
        k = kept[l]
        w_back_l, w_in_l = ([w_back], [w_in]) if l == 0 else (w_mix[1], w_mix[1])
        blocks = grad_blocks if l == 1 else gather4(grad_low, ffn_rows)
        if l == 0:
            blocks, side = tie(blocks, side)
            side = steps.send(side)
        g_gate, g_up, g_back, g_latent, rows, *parts = call(
            ffn_back_kernel,
            "ffn_back",
            [*blocks, k["ffn_a"], k["down_two"], k["up_back"], mask, k["gate"], k["ups"]],
            [((BLOCK, 1152), BF)] * 2
            + [((BLOCK, 32), BF), ((2, BLOCK, 32), BF), ((BLOCK, width), BF)]
            + rows_like,
            ffn_buffers + [ffn_sem],
            far=[ffn_w[l]],
            mflops=2800,
            mbytes=15,
        )
        if l == 1:
            parts, out_parts = tie(parts, deal4(out_parts, ffn_rows))
        else:
            parts, side = tie(parts, side)
        parts = deal4(parts, ffn_rows)
        if l == 0:
            side, parts[1] = tie(side, parts[1])
            side = steps.send(side)
        ffn_whole, ffn_split = call(
            ffn_adapters_kernel,
            "ffn_adapters",
            [
                *k["blocks"], rows, k["latent"], k["back_latent"], k["hidden"], g_gate, g_up,
                g_back, g_latent,
            ],
            [((96, width), BF), ((96, 1152), BF)],
            [pltpu.VMEM((BLOCK, width), BF)],
            mflops=200,
        )
        parts, (ffn_whole, ffn_split) = tie(parts, (ffn_whole, ffn_split))
        grad, grad_low = call(
            functools.partial(norm_back_kernel, l),
            "norm_back",
            [*parts, grad, k["residual_one"], ffn_gain],
            [((HOME, width), F32), ((HOME, width), BF)],
        )
        blocks = gather4(grad_low, along_x)
        if l == 1:
            (out_parts, shard_part), _ = tie((out_parts, ffn_split), grad_low)
            output, _ = call(
                functools.partial(add_norm_kernel, 1),
                "add_norm",
                [*out_parts, residual, mix_gain],
                [((HOME, width), F32), ((HOME, width), BF)],
            )
            output = lax.all_gather((output * valid).astype(BF), ("y", "x"), axis=0, tiled=True)
            shard_part = reduce_shards(shard_part)
        else:
            flat = jnp.concatenate([side[:48], shard_1, side[48:]], axis=0)
            flat, _ = tie(flat, grad_low)
            flat = sum_z(flat)
        rows, g_mixed, g_low, back, ends = mixer(
            states_back_kernel,
            "states_back",
            [*blocks, k["down_out"], k["up_out"], k["acts"], k["saved"], k["scan"]],
            [((BLOCK, width), BF), half_b, low_b, pair_f, ((2, 512), F32)],
            [mix_buffer, pltpu.VMEM((BLOCK + 8, 512), F32), pltpu.VMEM((BLOCK, 512), F32)]
            + [group_sem],
            scalars,
            w_back_l,
        )
        if l == 1:
            ends, shard_part = tie(ends, shard_part)
        else:
            ends, (flat, output) = tie(ends, (flat, output))
            flat = lax.all_gather(flat, ("core", "y", "x")).reshape(2, 4, 4, 304, 128)
        if l == 1:
            w_pair, _ = tie(w_pair, ends)
            w_in = lax.all_gather(w_pair, "y")
        carry = entering(ends, core, half, True)
        part, g_up_out, g_down_out, g_up_b, g_low_b = mixer(
            branch_back_kernel,
            "branch_back",
            [
                rows, g_mixed, g_low, k["states"], k["acts"], k["mixed"], k["out_latent"],
                k["lat_b"], k["up"], k["down"],
            ],
            [((BLOCK, width), F32), ((RANK, width), F32), ((RANK, 512), F32), ((RANK, 512), F32)]
            + [low_b],
            [mix_buffer, group_sem],
            scalars,
            w_in_l,
        )
        carry, part = tie(carry, part)
        if l == 1:
            shard_part, _ = tie(shard_part, carry)
            shard_1 = halves(shard_part, core, other_core)

        g_conv, rim = call(
            gates_back_kernel,
            "gates_back",
            [
                carry, k["carry"], back, k["states"], k["saved"], k["params"], k["gw"],
            ],
            [half_f, ((8, 512), F32)],
            [pltpu.VMEM((BLOCK + 8, 512), F32)],
            scalars,
        )
        halo = send(rim, next_block(True))
        if l == 1:
            halo, shard_1 = tie(halo, shard_1)
            shard_1 = blocks_of(shard_1, 48)
        *parts, mine, theirs = mixer(
            inputs_back_kernel,
            "inputs_back",
            [
                g_conv, halo, k["params"], k["up"], k["down"], part, k["normed"], k["lat_i"],
                g_low_b, g_up_b, g_up_out, g_down_out, ffn_whole,
            ],
            rows_like + [((80, width), F32), ((80, width), BF)],
            [
                pltpu.VMEM((BLOCK + 8, 512), F32), mix_buffer, pltpu.VMEM((BLOCK, width), BF),
                pltpu.VMEM((48, width), F32), pltpu.VMEM((48, 512), F32),
                pltpu.VMEM((2, 80, width), F32), group_sem,
            ],
            scalars,
            w_in_l,
        )
        parts = deal4(parts, along_x)
        steps = reduce_steps(mine, theirs)
        side = next(steps)
        grad, grad_low = call(
            functools.partial(norm_back_kernel, l),
            "norm_back",
            [*parts, grad, k["residual"], mix_gain],
            [((HOME, width), F32), ((HOME, width), BF)],
        )
    grad_tokens = lax.all_gather(grad_low, ("y", "x"), axis=0, tiled=True)
    shard_0, _ = tie(ffn_split, grad_low)
    shard_0 = reduce_shards(shard_0)
    side, shard_0 = tie(steps.send(side), shard_0)
    shard_0 = blocks_of(halves(shard_0, core, other_core), 48)
    side = steps.send(side)
    last = jnp.concatenate([side[:48], shard_0, side[48:]], axis=0)
    last = sum_z(last)
    flat, _ = tie(flat, last)
    tables = finish(ids, 1, [flat], tables)
    last, tables = tie(gather4(last, along_y), tables)
    (last,) = call(order_kernel, "order", last, [((4, 304, 128), BF)], (), scalars)
    output, _ = tie(output, last)
    last, output = tie(gather4(last, along_x), widen(output))
    (last,) = call(order_x_kernel, "order", last, [((4, 4, 304, 128), BF)], (), scalars)
    grad_tokens, _ = tie(grad_tokens, last)
    other, grad_tokens = tie(send(last, other_core), widen(grad_tokens))
    last = last, other
    ids = jnp.concatenate([ids, core[None].astype(jnp.int32)])
    gmd, gmu, god, gou, gfd, gfu, gbd, gbu = finish(ids, 0, last, tables)
    return (
        output.reshape(tokens.shape),
        grad_tokens.reshape(tokens.shape),
        turned(gmd),
        gmu.reshape(2, 8, 2, RANK, 2048),
        turned(god),
        gou,
        turned(gfd),
        gfu.reshape(2, 8, 2, RANK, 4608),
        turned(gbd),
        gbu,
    )


def solution(mesh):
    grid = Mesh(mesh.devices.reshape(4, 2, 4, 4), ALL)
    sp, mp = ("z", "core"), ("y", "x")
    in_specs = (
        P(None, sp, None),
        P(None, sp, None),
        P(),
        P(),
        P(),
        P(),
        P(None, None, mp),
        P(None, None, mp),
        P(None, None, mp),
        P(None, mp),
        P(None, mp, None, None),
        P(None, mp),
        P(None, mp, None, None),
        P(None, mp),
        P(None, mp),
        P(None, mp, None),
        P(None, None, mp),
        P(None, None, mp),
        P(None, mp, None),
        P(),
        P(None, None, None, None, mp),
        P(None, None, mp, None),
        P(),
        P(),
        P(None, None, None, None, mp),
        P(None, None, mp, None),
        P(),
    )
    out_specs = (P(None, sp, None), P(None, sp, None)) + (P(),) * 8
    return jax.shard_map(shards, mesh=grid, in_specs=in_specs, out_specs=out_specs, check_vma=False)
```

```python
import functools

import jax
import jax.numpy as jnp
from jax import lax
from jax.experimental import pallas as pl
from jax.experimental.pallas import tpu as pltpu
from jax.sharding import Mesh
from jax.sharding import PartitionSpec as P

ALL = ("z", "core", "y", "x")
BF = jnp.bfloat16
F32 = jnp.float32
RANK = 16
HOME = 64
BLOCK = 256
LIMIT = 60 * 2**20
LARGE = 60 * 2**20
GELU_C = 0.7978845608028654


def device_pairs(move):
    pairs = []
    for z in range(4):
        for c in range(2):
            for y in range(4):
                for x in range(4):
                    to = move(z, c, y, x)
                    if to is not None:
                        a = ((z * 2 + c) * 4 + y) * 4 + x
                        b = ((to[0] * 2 + to[1]) * 4 + to[2]) * 4 + to[3]
                        pairs.append((a, b))
    return pairs


def send(value, move):
    return lax.ppermute(value, ALL, device_pairs(move))


def along_x(d):
    return lambda z, c, y, x: (z, c, y, (x + d) % 4)


def along_y(d):
    return lambda z, c, y, x: (z, c, (y + d) % 4, x)


def ffn_rows(d):
    return lambda z, c, y, x: (z, c, y, (x + d) % 4) if c == 0 else (z, c, (y + d) % 4, x)


def ffn_shards(d):
    return lambda z, c, y, x: (z, c, (y + d) % 4, x) if c == 0 else (z, c, y, (x + d) % 4)


def shard_groups():
    at = lambda z, c, y, x: ((z * 2 + c) * 4 + y) * 4 + x
    columns = [[at(z, 0, y, x) for y in range(4)] for z in range(4) for x in range(4)]
    rows = [[at(z, 1, y, x) for x in range(4)] for z in range(4) for y in range(4)]
    return columns + rows


def gather4(value, moves):
    return [value] + [send(value, moves(j)) for j in (1, 2, 3)]


def deal4(parts, moves):
    return [parts[0]] + [send(parts[j], moves(-j)) for j in (1, 2, 3)]


def scatter4(parts, moves):
    moved = deal4(parts, moves)[1:]
    total = parts[0].astype(F32)
    for part in moved:
        total = total + part.astype(F32)
    return total


def split3(v):
    high = v.astype(BF)
    rest = v - high.astype(F32)
    mid = rest.astype(BF)
    return high, mid, (rest - mid.astype(F32)).astype(BF)


def tie(first, second):
    return lax.optimization_barrier((first, second))


def combine(earlier, later):
    return (earlier[0] * later[0], later[0] * earlier[1] + later[1])


def next_block(reverse):
    def move(z, c, y, x):
        at = (z * 2 + c) * 2 + y % 2 + (-1 if reverse else 1)
        if not 0 <= at < 16:
            return None
        return (at // 4, (at // 2) % 2, (y // 2) * 2 + at % 2, x)

    return move


def entering(own, core, half, reverse):
    one = jnp.stack([jnp.ones_like(own[0]), jnp.zeros_like(own[0])])

    def step(own, other, later):
        pre = jnp.where(later, other, one)
        first, second = jnp.where(later, other, own), jnp.where(later, own, other)
        both = combine((first[0], first[1]), (second[0], second[1]))
        return pre, jnp.stack(both)

    other = send(own, lambda z, c, y, x: (z, c, y ^ 1, x))
    pre_h, own = step(own, other, half == (0 if reverse else 1))
    other = send(own, lambda z, c, y, x: (z, 1 - c, y, x))
    pre_c, own = step(own, other, core == (0 if reverse else 1))
    far = []
    for d in (1, 2, 3):
        e = -d if reverse else d
        far.append(
            send(own, lambda z, c, y, x, e=e: (z + e, c, y, x) if 0 <= z + e < 4 else None)
        )
    state = far[2][1]
    for part in (far[1], far[0], pre_c, pre_h):
        state = part[0] * state + part[1]
    return state[None]


def nn(a, b):
    return jnp.dot(a, b, preferred_element_type=F32)


def nt(a, b):
    return lax.dot_general(a, b, (((1,), (1,)), ((), ())), preferred_element_type=F32)


def tn(a, b):
    return lax.dot_general(a, b, (((0,), (0,)), ((), ())), preferred_element_type=F32)


def gelu_pair(v):
    t = jnp.tanh(GELU_C * (v + 0.044715 * v * v * v))
    act = 0.5 * v * (1.0 + t)
    pull = 0.5 * (1.0 + t) + 0.5 * v * (1.0 - t * t) * (GELU_C * (1.0 + 0.134145 * v * v))
    return act, pull


def inverse_rms(v):
    return lax.rsqrt(jnp.mean(v * v, axis=-1, keepdims=True) + 1e-06)


def rms_backward(v, inverse, gain, grad):
    scaled = grad * gain
    return inverse * scaled - v * inverse**3 * jnp.mean(v * scaled, axis=-1, keepdims=True)


VMEM = pl.BlockSpec(memory_space=pltpu.VMEM)
SMEM = pl.BlockSpec(memory_space=pltpu.SMEM)
HBM = pl.BlockSpec(memory_space=pl.ANY)


def grouped(kernel, n_in, n_far):
    def run(sc, *refs):
        kernel(sc, refs[n_in : n_in + n_far], *refs[:n_in], *refs[n_in + n_far :])

    return run


def mixer(kernel, name, ins, outs, scratch, scalars, far):
    return call(
        grouped(kernel, len(ins), len(far)), name, ins, outs, scratch, scalars, far, mflops=420
    )


def call(kernel, name, ins, outs, scratch=(), scalars=None, far=(), mflops=100, mbytes=4):
    specs = [VMEM] * len(ins) + [HBM] * len(far)
    arrays = list(ins) + list(far)
    if scalars is not None:
        specs, arrays = [SMEM] + specs, [scalars] + arrays
    return pl.pallas_call(
        kernel,
        out_shape=[jax.ShapeDtypeStruct(shape, dtype) for shape, dtype in outs],
        in_specs=specs,
        out_specs=[VMEM] * len(outs),
        scratch_shapes=list(scratch),
        compiler_params=pltpu.CompilerParams(
            vmem_limit_bytes=LARGE if mflops > 1000 else LIMIT
        ),
        cost_estimate=pl.CostEstimate(
            flops=mflops * 10**6, bytes_accessed=mbytes * 10**6, transcendentals=0
        ),
        name=name,
    )(*arrays)


def fetch(source, rows, target, sem):
    first, count = rows
    copies = []
    for j in range(4):
        copy = pltpu.make_async_copy(
            source.at[j, pl.ds(first, count)],
            target.at[pl.ds(j * count, count)],
            sem.at[j],
        )
        copy.start()
        copies.append(copy)
    return copies


def fetch_half(sc, mine, other, rows, target, sem):
    first, count = rows
    pieces = []
    for half in range(2):
        low, high = max(first, half * 192), min(first + count, half * 192 + 192)
        if low < high:
            pieces.append((half, low - half * 192, high - low, low - first))
    copies = []
    for core in range(2):

        @pl.when(sc[4] == core)
        def _():
            for i, (half, low, size, at) in enumerate(pieces):
                source = mine if half == core else other
                for j in range(4):
                    pltpu.make_async_copy(
                        source.at[j, pl.ds(low, size)],
                        target.at[pl.ds(j * count + at, size)],
                        sem.at[i, j],
                    ).start()

    for i, (half, low, size, at) in enumerate(pieces):
        for j in range(4):
            copies.append(
                pltpu.make_async_copy(
                    mine.at[j, pl.ds(low, size)],
                    target.at[pl.ds(j * count + at, size)],
                    sem.at[i, j],
                )
            )
    return copies


def weights(sc, w, rows, target, sem):
    if len(w) == 2:
        return fetch_half(sc, *w, rows, target, sem)
    return fetch(w[0], (rows[0] % w[0].shape[1], rows[1]), target, sem.at[0])


def wait_all(copies):
    for copy in copies:
        copy.wait()


def place(scalars, blocks, rows_ref):
    for j in range(4):
        at = pl.multiple_of(lax.rem(scalars[0] + 4 - j, 4) * HOME, HOME)
        rows_ref[pl.ds(at, HOME), :] = blocks[j][...]


def take(scalars, total_ref, parts):
    for j in range(4):
        at = pl.multiple_of(lax.rem(scalars[0] + 4 - j, 4) * HOME, HOME)
        parts[j][...] = total_ref[pl.ds(at, HOME), :]


def scan_rows(reverse, a_ref, b_ref, cum_ref, out_ref):
    rows, width = a_ref.shape
    row = lax.broadcasted_iota(jnp.int32, (8, width), 0)
    groups = rows // 8

    def body(i, carry):
        ca, cb = carry
        at = pl.multiple_of((groups - 1 - i if reverse else i) * 8, 8)
        a, b = a_ref[pl.ds(at, 8), :], b_ref[pl.ds(at, 8), :]
        for k in (1, 2, 4):
            seen = row < 8 - k if reverse else row >= k
            by = 8 - k if reverse else k
            pa = jnp.where(seen, pltpu.roll(a, by, 0), 1.0)
            pb = jnp.where(seen, pltpu.roll(b, by, 0), 0.0)
            b = a * pb + b
            a = a * pa
        b = a * cb + b
        a = a * ca
        cum_ref[pl.ds(at, 8), :] = a
        out_ref[pl.ds(at, 8), :] = b
        last = 0 if reverse else 7
        return (
            jnp.broadcast_to(a[last : last + 1], a.shape),
            jnp.broadcast_to(b[last : last + 1], b.shape),
        )

    start = (jnp.ones((8, width), F32), jnp.zeros((8, width), F32))
    lax.fori_loop(0, groups, body, start, unroll=4)


def add_norm_kernel(l, p0, p1, p2, p3, residual, gain, out, normed):
    total = p0[...].astype(F32) + p1[...].astype(F32) + p2[...].astype(F32)
    v = residual[...] + total + p3[...].astype(F32)
    out[...] = v
    normed[...] = (v * inverse_rms(v) * gain[l : l + 1]).astype(BF)


def output_kernel(p0, p1, p2, p3, residual, valid, out):
    total = p0[HOME:].astype(F32) + p1[HOME:].astype(F32) + p2[HOME:].astype(F32)
    out[...] = ((residual[...] + total + p3[HOME:].astype(F32)) * valid[...]).astype(BF)


def norm_back_kernel(l, p0, p1, p2, p3, grad, v_ref, gain, out, low):
    total = p0[:HOME].astype(F32) + p1[:HOME].astype(F32) + p2[:HOME].astype(F32)
    total = total + p3[:HOME].astype(F32)
    v = v_ref[...]
    g = grad[...] + rms_backward(v, inverse_rms(v), gain[l : l + 1], total)
    out[...] = g
    low[...] = g.astype(BF)


def inputs_kernel(
    sc, w, n0, n1, n2, n3, down, up, normed, inputs, last, lat_b, lat_i, wi, sem
):
    copies = weights(sc, w, (128, 128), wi, sem)
    place(sc, (n0, n1, n2, n3), normed)
    rows = normed[...]
    lat_b[...] = nt(rows, down[:RANK]).astype(BF)
    low = nt(rows, down[RANK:]).astype(BF)
    lat_i[...] = low
    wait_all(copies)
    inputs[...] = (nt(rows, wi[...]) + nn(low, up[RANK:])).astype(BF)
    last[...] = inputs[BLOCK - 16 :]


def branch_kernel(sc, w, normed, lat_b, up, act, pull, wb, sem):
    copies = weights(sc, w, (0, 128), wb, sem)
    wait_all(copies)
    branch = nt(normed[...], wb[...]) + nn(lat_b[...], up[:RANK])
    act[...], pull[...] = gelu_pair(branch)


def gates_kernel(
    sc, inputs, halo, params, gw, saved, decay, scan, ends, ext, driven
):
    conv, gate_a, gate_i = (saved.at[i] for i in range(3))
    cum, local = scan.at[0], scan.at[1]
    ext[:16] = halo[...].astype(F32)
    ext[16:] = inputs[...].astype(F32)
    value = params[4:5] + params[0:1] * ext[pl.ds(16, BLOCK)]
    for o in (1, 2, 3):
        value = value + params[o : o + 1] * ext[pl.ds(16 - o, BLOCK)]
    conv[...] = value
    row = lax.broadcasted_iota(jnp.int32, (BLOCK, 128), 0)
    first = (row == 0) & (sc[1] == 1)
    for h in range(4):
        at = slice(h * 128, h * 128 + 128)
        c = conv[:, at]
        pre = nn(c.astype(BF), gw[h])
        a = jax.nn.sigmoid(pre[:, :128] + params[5:6, at])
        i = jax.nn.sigmoid(pre[:, 128:] + params[6:7, at])
        d = jnp.exp(a * params[7:8, at])
        gate_a[:, at] = a
        gate_i[:, at] = i
        decay[:, at] = d
        driven[:, at] = c * i * jnp.where(first, 1.0, jnp.sqrt(1.0 - d * d + 0.01))
    scan_rows(False, decay, driven, cum, local)
    ends[0:1] = cum[BLOCK - 1 :]
    ends[1:2] = local[BLOCK - 1 :]


def mixed_kernel(
    sc, w, carry, scan, act, down_out, up_out, states, mixed, out_latent, q0, q1, q2, q3,
    wo, total, sem,
):
    copies = weights(sc, w, (256, 128), wo, sem)
    s = scan[1] + scan[0] * carry[...]
    states[...] = s
    m = (s * act[...]).astype(BF)
    mixed[...] = m
    low = nt(m, down_out[...]).astype(BF)
    out_latent[...] = low
    wait_all(copies)
    total[...] = (nn(m, wo[...]) + nn(low, up_out[...])).astype(BF)
    take(sc, total, (q0, q1, q2, q3))


def ffn_kernel(
    n0, n1, n2, n3, a, down, up_back, mask, w, gate, up, hidden, latent, back_latent,
    q0, q1, q2, q3, rows_ref, wg, wu, wd, sem,
):
    cg = fetch(w, (0, 288), wg, sem.at[0])
    cu = fetch(w, (288, 288), wu, sem.at[1])
    cd = fetch(w, (576, 288), wd, sem.at[2])
    for j, n in enumerate((n0, n1, n2, n3)):
        rows_ref[j * HOME : (j + 1) * HOME] = n[...]
    rows = rows_ref[...]
    lat_g = (nt(rows, down[:32]) * mask[...]).astype(BF)
    lat_u = (nt(rows, down[32:]) * mask[...]).astype(BF)
    latent[0] = lat_g
    latent[1] = lat_u
    wait_all(cg)
    g = nt(rows, wg[...]) + nn(lat_g, a[:32])
    gate[...] = g
    wait_all(cu)
    u = nt(rows, wu[...]) + nn(lat_u, a[32:64])
    up[...] = u
    hidden[...] = (gelu_pair(g)[0] * u).astype(BF)
    h = hidden[...]
    low = (nt(h, a[64:]) * mask[...]).astype(BF)
    back_latent[...] = low
    wait_all(cd)
    total = (nn(h, wd[...]) + nn(low, up_back[...])).astype(BF)
    for j, q in enumerate((q0, q1, q2, q3)):
        q[...] = total[j * HOME : (j + 1) * HOME]


def ffn_back_kernel(
    r0, r1, r2, r3, a, down, up_back, mask, gate, up, w, g_gate, g_up, g_back, g_latent, rows_ref,
    q0, q1, q2, q3, wg, wu, wd, sem,
):
    cd = fetch(w, (576, 288), wd, sem.at[2])
    cg = fetch(w, (0, 288), wg, sem.at[0])
    cu = fetch(w, (288, 288), wu, sem.at[1])
    for j, r in enumerate((r0, r1, r2, r3)):
        rows_ref[j * HOME : (j + 1) * HOME] = r[...]
    rows = rows_ref[...]
    low = (nt(rows, up_back[...]) * mask[...]).astype(BF)
    g_back[...] = low
    wait_all(cd)
    gh = (nt(rows, wd[...]) + nn(low, a[64:])).astype(BF).astype(F32)
    act, pull = gelu_pair(gate[...])
    g_up[...] = (gh * act).astype(BF)
    g_gate[...] = (gh * up[...] * pull).astype(BF)
    gg, gu = g_gate[...], g_up[...]
    lat_g = (nt(gg, a[:32]) * mask[...]).astype(BF)
    lat_u = (nt(gu, a[32:64]) * mask[...]).astype(BF)
    g_latent[0] = lat_g
    g_latent[1] = lat_u
    wait_all(cg)
    total = nn(gg, wg[...]) + nn(lat_g, down[:32]) + nn(lat_u, down[32:])
    wait_all(cu)
    total = (total + nn(gu, wu[...])).astype(BF)
    for j, q in enumerate((q0, q1, q2, q3)):
        q[...] = total[j * HOME : (j + 1) * HOME]


def ffn_turn_kernel(
    n0, n1, n2, n3, r0, r1, r2, r3, a, down, up_back, mask, w,
    hidden, latent, back_latent, g_gate, g_up, g_back, g_latent, rows_ref,
    q0, q1, q2, q3, normed_ref, wg, wu, wd, sem,
):
    cg = fetch(w, (0, 288), wg, sem.at[0])
    cu = fetch(w, (288, 288), wu, sem.at[1])
    cd = fetch(w, (576, 288), wd, sem.at[2])
    for j, (n, r) in enumerate(((n0, r0), (n1, r1), (n2, r2), (n3, r3))):
        normed_ref[j * HOME : (j + 1) * HOME] = n[...]
        rows_ref[j * HOME : (j + 1) * HOME] = r[...]
    normed, rows = normed_ref[...], rows_ref[...]
    lat_g = (nt(normed, down[:32]) * mask[...]).astype(BF)
    lat_u = (nt(normed, down[32:]) * mask[...]).astype(BF)
    latent[0] = lat_g
    latent[1] = lat_u
    low = (nt(rows, up_back[...]) * mask[...]).astype(BF)
    g_back[...] = low
    wait_all(cg)
    g = nt(normed, wg[...]) + nn(lat_g, a[:32])
    wait_all(cu)
    u = nt(normed, wu[...]) + nn(lat_u, a[32:64])
    act, pull = gelu_pair(g)
    hidden[...] = (act * u).astype(BF)
    wait_all(cd)
    gh = (nt(rows, wd[...]) + nn(low, a[64:])).astype(BF).astype(F32)
    g_up[...] = (gh * act).astype(BF)
    g_gate[...] = (gh * u * pull).astype(BF)
    gg, gu = g_gate[...], g_up[...]
    lat_g = (nt(gg, a[:32]) * mask[...]).astype(BF)
    lat_u = (nt(gu, a[32:64]) * mask[...]).astype(BF)
    g_latent[0] = lat_g
    g_latent[1] = lat_u
    total = nn(gg, wg[...]) + nn(lat_g, down[:32]) + nn(lat_u, down[32:])
    total = (total + nn(gu, wu[...])).astype(BF)
    for j, q in enumerate((q0, q1, q2, q3)):
        q[:HOME] = total[j * HOME : (j + 1) * HOME]
    h = hidden[...]
    low = (nt(h, a[64:]) * mask[...]).astype(BF)
    back_latent[...] = low
    total = (nn(h, wd[...]) + nn(low, up_back[...])).astype(BF)
    for j, q in enumerate((q0, q1, q2, q3)):
        q[HOME:] = total[j * HOME : (j + 1) * HOME]


def ffn_adapters_kernel(
    n0, n1, n2, n3, rows, latent, back_latent, hidden, g_gate, g_up, g_back, g_latent,
    whole, split, normed_ref,
):
    for j, n in enumerate((n0, n1, n2, n3)):
        normed_ref[j * HOME : (j + 1) * HOME] = n[...]
    normed = normed_ref[...]
    g_down = [tn(g_latent[0], normed), tn(g_latent[1], normed)]
    g_up_back = tn(back_latent[...], rows[...])
    for s in range(2):
        at = slice(s * RANK, s * RANK + RANK)
        whole[s * 48 : s * 48 + 16] = g_down[0][at].astype(BF)
        whole[s * 48 + 16 : s * 48 + 32] = g_down[1][at].astype(BF)
        whole[s * 48 + 32 : s * 48 + 48] = g_up_back[at].astype(BF)
    split[:32] = tn(latent[0], g_gate[...]).astype(BF)
    split[32:64] = tn(latent[1], g_up[...]).astype(BF)
    split[64:] = tn(g_back[...], hidden[...]).astype(BF)


def states_back_kernel(
    sc, w, r0, r1, r2, r3, down_out, up_out, act, decay, forward_ends,
    rows_ref, g_mixed, g_low, back, ends, wo, ext, g_states, sem,
):
    suffix, local = back.at[0], back.at[1]
    copies = weights(sc, w, (256, 128), wo, sem)
    place(sc, (r0, r1, r2, r3), rows_ref)
    rows = rows_ref[...]
    low = nt(rows, up_out[...]).astype(BF)
    g_low[...] = low
    ext[:BLOCK] = decay[...]
    ext[BLOCK:] = jnp.ones((8, 512), F32)
    ext[:BLOCK] = ext[pl.ds(1, BLOCK)]
    wait_all(copies)
    gm = (nt(rows, wo[...]) + nn(low, down_out[...])).astype(BF)
    g_mixed[...] = gm
    g_states[...] = gm.astype(F32) * act[...]
    scan_rows(True, ext.at[pl.ds(0, BLOCK)], g_states, suffix, local)
    ends[0:1] = forward_ends[0:1]
    ends[1:2] = decay[0:1] * local[0:1]


def branch_back_kernel(
    sc, w, rows, g_mixed, g_low, states, pull, mixed, out_latent, lat_b, up, down,
    part, g_up_out, g_down_out, g_up_b, g_branch_low, wb, sem,
):
    copies = weights(sc, w, (0, 128), wb, sem)
    gb = (g_mixed[...].astype(F32) * states[...] * pull[...]).astype(BF)
    low = nt(gb, up[:RANK]).astype(BF)
    g_branch_low[...] = low
    g_up_out[...] = tn(out_latent[...], rows[...])
    g_down_out[...] = tn(g_low[...], mixed[...])
    g_up_b[...] = tn(lat_b[...], gb)
    wait_all(copies)
    part[...] = nn(gb, wb[...]) + nn(low, down[:RANK])


def gates_back_kernel(
    sc, carry, carry_in, back, states, saved, decay, params, gw, g_conv, rim, ext
):
    conv, gate_a, gate_i = (saved.at[i] for i in range(3))
    suffix, local = back.at[0], back.at[1]
    ext[:8] = jnp.broadcast_to(carry_in[...], (8, 512))
    ext[8:] = states[...]
    row = lax.broadcasted_iota(jnp.int32, (BLOCK, 128), 0)
    first = (row == 0) & (sc[1] == 1)
    for h in range(4):
        at = slice(h * 128, h * 128 + 128)
        gd = local[:, at] + suffix[:, at] * carry[:, at]
        d, i, a, c = decay[:, at], gate_i[:, at], gate_a[:, at], conv[:, at]
        scale = jnp.where(first, 1.0, jnp.sqrt(1.0 - d * d + 0.01))
        g_scale = gd * c * i
        previous = ext[pl.ds(7, BLOCK), at]
        g_decay = gd * previous - jnp.where(first, 0.0, g_scale * (d / scale))
        ga = (g_decay * d * params[7:8, at] * a * (1.0 - a)).astype(BF)
        gi = (g_scale * scale * (1.0 - i)).astype(BF)
        g_conv[:, at] = gd * i * scale + nt(ga, gw[h, :, :128]) + nt(gi, gw[h, :, 128:])
    rim[...] = g_conv[:8]


def inputs_back_kernel(
    sc, w, g_conv, halo, params, up, down, part, normed, lat_i, g_low_b, g_up_b, g_up_out,
    g_down_out, ffn_whole, q0, q1, q2, q3, mine, theirs, ext, wi, total, whole, split, wide, sem,
):
    copies = weights(sc, w, (128, 128), wi, sem)
    ext[:BLOCK] = g_conv[...]
    ext[BLOCK:] = halo[...]
    value = params[0:1] * ext[:BLOCK]
    for o in (1, 2, 3):
        value = value + params[o : o + 1] * ext[pl.ds(o, BLOCK)]
    gi = value.astype(BF)
    low = nt(gi, up[RANK:]).astype(BF)
    whole[:RANK] = tn(g_low_b[...], normed[...])
    whole[RANK:32] = tn(low, normed[...])
    whole[32:] = g_up_out[...]
    split[:RANK] = g_up_b[...]
    split[RANK:32] = tn(lat_i[...], gi)
    split[32:] = g_down_out[...]
    for c in range(2):
        wide[c, :48] = ffn_whole[c * 48 : c * 48 + 48].astype(F32)
        wide[c, 48:72] = whole[c * 24 : c * 24 + 24]
        for i in range(3):
            at = c * 24 + i * 8
            wide[c, 72:, i * 512 : i * 512 + 512] = split[at : at + 8]
    mine[...] = wide[sc[4]]
    theirs[...] = wide[1 - sc[4]].astype(BF)
    wait_all(copies)
    total[...] = (part[...] + nn(gi, wi[...]) + nn(low, down[RANK:])).astype(BF)
    take(sc, total, (q0, q1, q2, q3))


def head_kernel(
    sc, tokens, down, up, gain, wb, wi, o0, o1, o2, o3, normed, lat_b, lat_i, w
):
    j = pl.program_id(0)

    @pl.when(j == 0)
    def _():
        w[:, :128] = wb[0]
        w[:, 128:] = wi[0]

    v = tokens[0]
    rows = (v * inverse_rms(v) * gain[0:1]).astype(BF)
    low_b = nt(rows, down[0, 0, :RANK]).astype(BF)
    low_i = nt(rows, down[0, 0, RANK:]).astype(BF)
    both = nn(rows, w[...])
    branch = (both[:, :128] + nn(low_b, up[0, 0, :RANK])).astype(BF)
    inputs = (both[:, 128:] + nn(low_i, up[0, 0, RANK:])).astype(BF)
    for i, out in enumerate((o0, o1, o2, o3)):

        @pl.when(j == i)
        def _():
            out[:, :128] = branch
            out[:, 128:] = inputs

    @pl.when(j == 0)
    def _():
        normed[...] = rows
        lat_b[...] = low_b
        lat_i[...] = low_i


def head(scalars, tokens, down, up, gain, wb, wi):
    at = lambda j, sc: lax.rem(sc[0] + 4 - j, 4)
    own = lambda j, sc: (0, sc[1 + at(j, sc) // 2], 0, 0)
    fixed = lambda j, sc: (0, 0)
    block = ((BLOCK, 256), BF)
    outs = [block] * 4 + [((BLOCK, 1536), BF), ((BLOCK, RANK), BF), ((BLOCK, RANK), BF)]
    return pl.pallas_call(
        head_kernel,
        out_shape=[jax.ShapeDtypeStruct(shape, dtype) for shape, dtype in outs],
        grid_spec=pltpu.PrefetchScalarGridSpec(
            num_scalar_prefetch=1,
            grid=(4,),
            in_specs=[
                pl.BlockSpec((1, BLOCK, 1536), lambda j, sc: (at(j, sc) // 2, at(j, sc) % 2, 0)),
                pl.BlockSpec((1, 1, 32, 1536), own),
                pl.BlockSpec((1, 1, 32, 128), own),
                pl.BlockSpec((2, 1536), fixed),
                pl.BlockSpec((1, 1536, 128), lambda j, sc: (0, 0, 0)),
                pl.BlockSpec((1, 1536, 128), lambda j, sc: (0, 0, 0)),
            ],
            out_specs=[pl.BlockSpec(shape, fixed) for shape, _ in outs],
            scratch_shapes=[pltpu.VMEM((1536, 256), BF)],
        ),
        compiler_params=pltpu.CompilerParams(vmem_limit_bytes=LIMIT),
        cost_estimate=pl.CostEstimate(
            flops=900 * 10**6, bytes_accessed=9 * 10**6, transcendentals=0
        ),
        name="head",
    )(scalars, tokens, down, up, gain, wb, wi)


def prepare_kernel(
    sc, md, ou, fd0, fd1, bu0, bu1, mu0, mu1, od0, od1, fu0, fu1, bd0, bd1,
    ga, gi, cw, cb, ab, ib, dp, mix_d0, mix_d1, out_u0, out_u1, ffn_d0, ffn_d1, back_u0, back_u1,
    small, ffn_small,
):
    l = pl.program_id(0)
    for i, (mix_d, out_u, ffn_d, back_u) in enumerate(
        ((mix_d0, out_u0, ffn_d0, back_u0), (mix_d1, out_u1, ffn_d1, back_u1))
    ):

        @pl.when(l == i)
        def _():
            mix_d[...] = md[0, 0]
            out_u[...] = ou[0, 0]
            for s, (fd, bu) in enumerate(((fd0, bu0), (fd1, bu1))):
                ffn_d[s * 16 : s * 16 + 16] = fd[0, 0, :16]
                ffn_d[32 + s * 16 : 48 + s * 16] = fd[0, 0, 16:]
                back_u[s * 16 : s * 16 + 16] = bu[0, 0]

    ffn_small[...] = jnp.zeros(ffn_small.shape, BF)
    small[0, :128] = ga[0, 0]
    small[0, 128:256] = gi[0, 0]
    for s, (mu, od, fu, bd) in enumerate(((mu0, od0, fu0, bd0), (mu1, od1, fu1, bd1))):
        small[0, 256 + s * 32 : 288 + s * 32] = mu[0, 0]
        small[0, 320 + s * 16 : 336 + s * 16] = od[0, 0]
        at = slice(s * 16, s * 16 + 16)
        ffn_small[0, at, :288] = fu[0, 0, :16]
        ffn_small[0, at, 384:672] = fu[0, 0, 16:]
        ffn_small[0, at, 768:1056] = bd[0, 0]
    vectors = [ref[pl.ds(l, 1), :] for ref in (cb, ab, ib, dp)]
    wide = jnp.concatenate([cw[0]] + vectors + [jnp.zeros((8, 128), F32)], axis=0)
    for i, part in enumerate(split3(wide)):
        small[0, 352 + 16 * i : 368 + 16 * i] = part


def prepare(picks, owned, tables, singles, vectors):
    specs, arrays = [], []
    for table, which in [(t, (2,)) for t in owned] + [(t, (0, 1)) for t in tables]:
        for s in which:
            specs.append(
                pl.BlockSpec((1, 1) + table.shape[2:], lambda l, sc, s=s: (l, sc[s], 0, 0))
            )
            arrays.append(table)
    for single in singles:
        dims = single.ndim - 1
        specs.append(
            pl.BlockSpec((1,) + single.shape[1:], lambda l, sc, dims=dims: (l,) + (0,) * dims)
        )
        arrays.append(single)
    for vector in vectors:
        specs.append(pl.BlockSpec(vector.shape, lambda l, sc: (0, 0)))
        arrays.append(vector)
    flat = [(32, 1536), (16, 1536), (64, 1536), (32, 1536)]
    flat = [shape for shape in flat for _ in range(2)]
    tall = [(400, 128), (32, 1536)]
    return pl.pallas_call(
        prepare_kernel,
        out_shape=[jax.ShapeDtypeStruct(shape, BF) for shape in flat]
        + [jax.ShapeDtypeStruct((2,) + shape, BF) for shape in tall],
        grid_spec=pltpu.PrefetchScalarGridSpec(
            num_scalar_prefetch=1,
            grid=(2,),
            in_specs=specs,
            out_specs=[pl.BlockSpec(shape, lambda l, sc: (0, 0)) for shape in flat]
            + [pl.BlockSpec((1,) + shape, lambda l, sc: (l, 0, 0)) for shape in tall],
        ),
        compiler_params=pltpu.CompilerParams(vmem_limit_bytes=LIMIT),
        cost_estimate=pl.CostEstimate(flops=10**6, bytes_accessed=4 * 10**6, transcendentals=0),
        name="prepare",
    )(picks, *arrays)


def arrange_kernel(sc, s0, s1, s2, s3, *refs):
    small = refs[-1]
    for j, block in enumerate((s0, s1, s2, s3)):
        small[lax.rem(sc[2] + 4 - j, 4)] = block[...]
    seq = sc[2] // 2
    for l in range(2):
        gw, up, down_out, params = refs[l * 4 : l * 4 + 4]
        for p in range(4):
            at = slice(p * 128, p * 128 + 128)
            gw[p, :, :128] = small[p, l, :128]
            gw[p, :, 128:] = small[p, l, 128:256]
            start = pl.multiple_of(256 + seq * 32, 32)
            up[:, at] = small[p, l, pl.ds(start, 32), :]
            start = pl.multiple_of(320 + seq * 16, 16)
            down_out[:, at] = small[p, l, pl.ds(start, 16), :]
            parts = [small[p, l, 352 + 16 * i : 368 + 16 * i].astype(F32) for i in range(3)]
            total = parts[0] + parts[1] + parts[2]
            params[:, at] = total[:8]
            params[7:8, at] = -8.0 * jax.nn.softplus(total[7:8])


def join_kernel(w, a, held, wide, sem):
    copies = []
    for j in range(4):
        copy = pltpu.make_async_copy(w.at[j, pl.ds(864, 32)], held.at[j], sem.at[j])
        copy.start()
        copies.append(copy)
    wait_all(copies)
    for j in range(4):
        for i in range(3):
            part = held[j, :, i * 384 : i * 384 + 288].astype(F32)
            wide[i * 32 : i * 32 + 32, j * 288 : j * 288 + 288] = part
    a[...] = wide[...].astype(BF)


def order_kernel(sc, b0, b1, b2, b3, out):
    for j, block in enumerate((b0, b1, b2, b3)):
        out[lax.rem(sc[2] + 4 - j, 4)] = block[...]


def order_x_kernel(sc, b0, b1, b2, b3, out):
    for j, block in enumerate((b0, b1, b2, b3)):
        out[lax.rem(sc[0] + 4 - j, 4)] = block[...]


def unpack_kernel(sc, b0, b1, b2, b3, inputs, last, act, pull, held):
    for j, block in enumerate((b0, b1, b2, b3)):
        held[lax.rem(sc[2] + j, 4)] = block[...]
    for p in range(4):
        at = slice(p * 128, p * 128 + 128)
        inputs[:, at] = held[p, :, 128:]
        act[:, at], pull[:, at] = gelu_pair(held[p, :, :128].astype(F32))
    last[...] = inputs[BLOCK - 16 :]


def pack_kernel(a_ref, b_ref, c_ref, d_ref, out):
    at = 0
    for ref in (a_ref, b_ref, c_ref, d_ref):
        count = ref.shape[1]
        out[at : at + count] = ref[0]
        at += count


def pack(l, parts):
    width = parts[0].shape[2]
    total = sum(part.shape[1] for part in parts)
    return pl.pallas_call(
        pack_kernel,
        out_shape=jax.ShapeDtypeStruct((total, width), BF),
        grid=(2,),
        in_specs=[pl.BlockSpec((1, p.shape[1], width // 2), lambda i: (l, 0, i)) for p in parts],
        out_specs=pl.BlockSpec((total, width // 2), lambda i: (0, i)),
        compiler_params=pltpu.CompilerParams(vmem_limit_bytes=LIMIT),
        cost_estimate=pl.CostEstimate(flops=0, bytes_accessed=5 * 10**6, transcendentals=0),
        name="pack",
    )(*parts)


def pair_kernel(a_ref, b_ref, out):
    out[:128] = a_ref[0].T
    out[128:] = b_ref[0].T


def pair_of(l, a, b):
    rows = a.shape[1] // 3
    piece = pl.BlockSpec((1, rows, 128), lambda i: (l, i, 0))
    return pl.pallas_call(
        pair_kernel,
        out_shape=jax.ShapeDtypeStruct((256, a.shape[1]), BF),
        grid=(3,),
        in_specs=[piece] * 2,
        out_specs=pl.BlockSpec((256, rows), lambda i: (0, i)),
        compiler_params=pltpu.CompilerParams(vmem_limit_bytes=LIMIT),
        cost_estimate=pl.CostEstimate(flops=0, bytes_accessed=2 * 10**6, transcendentals=0),
        name="pair",
    )(a, b)


def half_kernel(sc, a_ref, b_ref, c_ref, out):
    @pl.when(sc[4] == 0)
    def _():
        out[:128] = a_ref[0].T
        out[128:] = b_ref[0, :, :].T[:64]

    @pl.when(sc[4] == 1)
    def _():
        out[:64] = b_ref[0, :, :].T[64:]
        out[64:] = c_ref[0]


def half_of(scalars, l, a, b, c):
    rows = a.shape[1] // 3
    piece = pl.BlockSpec((1, rows, 128), lambda i, sc: (l, i, 0))
    return pl.pallas_call(
        half_kernel,
        out_shape=jax.ShapeDtypeStruct((192, a.shape[1]), BF),
        grid_spec=pltpu.PrefetchScalarGridSpec(
            num_scalar_prefetch=1,
            grid=(3,),
            in_specs=[piece] * 2 + [pl.BlockSpec((1, 128, rows), lambda i, sc: (l, 0, i))],
            out_specs=pl.BlockSpec((192, rows), lambda i, sc: (0, i)),
        ),
        compiler_params=pltpu.CompilerParams(vmem_limit_bytes=LIMIT),
        cost_estimate=pl.CostEstimate(flops=0, bytes_accessed=2 * 10**6, transcendentals=0),
        name="half",
    )(scalars, a, b, c)


def finish_kernel(ranked, sc, *refs):
    mix_d, mix_u, out_d, out_u, ffn_d, ffn_u, back_d, back_u, whole, shard, split = refs[-11:]
    a = pl.program_id(0)

    @pl.when(a == 0)
    def _():
        for c in range(2):
            for y in range(4):
                for x in range(4):
                    if ranked:
                        mine, other = (ref[y * 4 + x].astype(F32) for ref in refs[:2])
                        v = jnp.where(sc[2] == c, mine, other)
                    else:
                        v = refs[0][c, y, x].astype(F32)
                    row = c * 24 + (y % 2) * 12
                    for k in range(3):
                        lane = x * 384 + k * 128
                        whole[c, y * 12 : y * 12 + 12, lane : lane + 128] = v[
                            k * 16 : k * 16 + 12
                        ]
                        whole[y // 2, 48 + row : 60 + row, lane : lane + 128] = v[
                            192 + k * 16 : 204 + k * 16
                        ]
                        lane = (y * 4 + x) * 288 + k * 128
                        part = v[48 + k * 48 : 96 + k * 48]
                        wide = 32 if k == 2 else 128
                        shard[c * 48 : c * 48 + 48, lane : lane + wide] = part[:, :wide]
                    for p in range(4):
                        lane = (p * 4 + x) * 128
                        k = 192 + (3 + p) * 16
                        split[y // 2, row : row + 12, lane : lane + 128] = v[k : k + 12]

    w = [((sc[s] == sc[0]) == (sc[a] == sc[0])).astype(F32) for s in range(2)]
    both = lambda get: get(0) * w[0] + get(1) * w[1]
    ffn_d[0, 0] = both(lambda s: whole[s, :32])
    back_u[0, 0] = both(lambda s: whole[s, 32:48])
    mix_d[0, 0] = both(lambda s: whole[s, 48:80])
    out_u[0, 0] = both(lambda s: whole[s, 80:])
    ffn_u[0, 0, :16] = both(lambda s: shard[s * 16 : s * 16 + 16])
    ffn_u[0, 0, 16:] = both(lambda s: shard[32 + s * 16 : 48 + s * 16])
    back_d[0, 0] = both(lambda s: shard[64 + s * 16 : 80 + s * 16])
    mix_u[0, 0] = both(lambda s: split[s, :32])
    out_d[0, 0] = both(lambda s: split[s, 32:])


TABLES = [(32, 1536), (32, 2048), (16, 2048), (16, 1536), (32, 1536), (32, 4608), (16, 4608)]
TABLES.append((16, 1536))


def zeros_kernel(*refs):
    for ref in refs:
        ref[...] = jnp.zeros(ref.shape, F32)


def empty_tables():
    return pl.pallas_call(
        zeros_kernel,
        out_shape=[jax.ShapeDtypeStruct((2, 8) + shape, F32) for shape in TABLES],
        grid=(2, 4),
        out_specs=[pl.BlockSpec((1, 2) + shape, lambda l, a: (l, a, 0, 0)) for shape in TABLES],
        compiler_params=pltpu.CompilerParams(vmem_limit_bytes=LIMIT),
        cost_estimate=pl.CostEstimate(flops=10**6, bytes_accessed=20 * 10**6, transcendentals=0),
        name="zeros",
    )()


def finish(ids, layer, flats, tables):
    return pl.pallas_call(
        functools.partial(finish_kernel, len(flats) == 2),
        out_shape=[jax.ShapeDtypeStruct((2, 8) + shape, F32) for shape in TABLES],
        grid_spec=pltpu.PrefetchScalarGridSpec(
            num_scalar_prefetch=1,
            grid=(2,),
            in_specs=[VMEM] * len(flats) + [HBM] * len(tables),
            out_specs=[
                pl.BlockSpec((1, 1) + shape, lambda a, sc: (layer, sc[a], 0, 0))
                for shape in TABLES
            ],
            scratch_shapes=[
                pltpu.VMEM((2, 96, 1536), F32),
                pltpu.VMEM((96, 4608), F32),
                pltpu.VMEM((2, 48, 2048), F32),
            ],
        ),
        input_output_aliases={1 + len(flats) + i: i for i in range(len(tables))},
        compiler_params=pltpu.CompilerParams(vmem_limit_bytes=LIMIT),
        cost_estimate=pl.CostEstimate(flops=10**7, bytes_accessed=4 * 10**6, transcendentals=0),
        name="finish",
    )(ids, *flats, *tables)


def widen_kernel(v, out):
    out[...] = v[...].astype(F32)


def widen(v):
    rows, width = v.shape
    spec = pl.BlockSpec((BLOCK, width), lambda i: (i, 0))
    return pl.pallas_call(
        widen_kernel,
        out_shape=jax.ShapeDtypeStruct(v.shape, F32),
        grid=(rows // BLOCK,),
        in_specs=[spec],
        out_specs=spec,
        cost_estimate=pl.CostEstimate(flops=10**6, bytes_accessed=10**7, transcendentals=0),
        name="widen",
    )(v)


def other_core(z, c, y, x):
    return (z, 1 - c, y, x)


def other_half(z, c, y, x):
    return (z, c, y ^ 1, x)


def along_z(d):
    return lambda z, c, y, x: ((z + d) % 4, c, y, x)


def halves(value, index, move):
    count = value.shape[0] // 2
    mine = lax.dynamic_slice_in_dim(value, index * count, count, 0)
    theirs = lax.dynamic_slice_in_dim(value, (1 - index) * count, count, 0)
    return mine.astype(F32) + send(theirs, move).astype(F32)


def ring_scatter(value, index, moves, axis):
    count = value.shape[axis] // 4
    parts = [
        lax.dynamic_slice_in_dim(value, ((index - j) % 4) * count, count, axis) for j in range(4)
    ]
    return scatter4(parts, moves)


def sum_z(value):
    low = value.astype(BF)
    total = value
    for d in (1, 2, 3):
        total = total + send(low, along_z(d)).astype(F32)
    return total.astype(BF)


def blocks_of(v, rows):
    n, width = v.shape
    v = jnp.pad(v, ((0, rows - n), (0, -width % 128)))
    return jnp.concatenate([v[:, i : i + 128] for i in range(0, width, 128)], axis=0)


def reduce_shards(split):
    core, x, y = lax.axis_index("core"), lax.axis_index("x"), lax.axis_index("y")
    group = jnp.where(core == 0, y, x)
    shard = split.astype(BF).reshape(96, 4, 288).transpose(1, 0, 2)
    return ring_scatter(shard, group, ffn_shards, 0)[0]


def reduce_steps(mine, theirs):
    x, y = lax.axis_index("x"), lax.axis_index("y")
    part = mine + send(theirs, other_core).astype(F32)
    part = yield part
    split = jnp.concatenate([part[72:, i * 512 : i * 512 + 512] for i in range(3)], axis=0)
    whole = ring_scatter(part[:72].astype(BF), x, along_x, 1)
    whole, split = yield whole, split
    mix = jnp.concatenate([whole[48:], split], axis=1)
    pieces = []
    for q in range(4):
        here = jnp.where(y // 2 == q // 2, mix[(q % 2) * 12 : (q % 2) * 12 + 12], 0.0)
        pieces.append(jnp.concatenate([whole[q * 12 : q * 12 + 12], here], axis=1))
    part = ring_scatter(jnp.stack(pieces).astype(BF), y, along_y, 0)[0]
    yield blocks_of(part, 16)


def shards(
    tokens,
    cotangent,
    lengths,
    adapter_ids,
    mix_gain,
    ffn_gain,
    w_branch,
    input_weight,
    conv_weight,
    conv_bias,
    gate_a_weight,
    gate_a_bias,
    gate_i_weight,
    gate_i_bias,
    decay_param,
    w_out,
    w_gate,
    w_up,
    w_down,
    mix_down,
    mix_up,
    out_down,
    out_up,
    ffn_down,
    ffn_up,
    back_down,
    back_up,
):
    width = tokens.shape[2]
    z, core = lax.axis_index("z"), lax.axis_index("core")
    y, x = lax.axis_index("y"), lax.axis_index("x")
    seq, half = y // 2, y % 2
    w_back = lax.all_gather(w_out[0], "y")
    ids = adapter_ids
    ffn_group = jnp.where(core == 0, y, x)
    first = (z + core + half == 0).astype(jnp.int32)
    scalars = jnp.stack([x, first, y, ffn_group, core]).astype(jnp.int32)
    turned = lambda v: jnp.swapaxes(v, -1, -2)
    mix_down_t = turned(mix_down)
    mix_up_f = mix_up.reshape(2, 8, 32, 128)
    *local, normed_0, lat_b_0, lat_i_0 = head(
        jnp.stack([y, ids[0], ids[1]]),
        tokens,
        mix_down_t,
        mix_up_f,
        mix_gain,
        w_branch,
        input_weight,
    )
    mine = local[0]
    local = deal4(local, along_y)
    ffn_parts = [turned(w_gate), turned(w_up), w_down]
    gather_ffn = lambda v: lax.all_gather(v, ALL, axis=0, axis_index_groups=shard_groups())
    picked, mine = tie(ids, mine)
    prepared = prepare(
        jnp.concatenate([picked, lax.dynamic_index_in_dim(picked, seq, 0)]),
        [mix_down_t, out_up],
        [
            turned(ffn_down), back_up, mix_up_f, turned(out_down),
            ffn_up.reshape(2, 8, 32, 288), turned(back_down),
        ],
        [gate_a_weight, gate_i_weight, conv_weight],
        [conv_bias, gate_a_bias, gate_i_bias, decay_param],
    )
    mix_d, out_u, ffn_d, back_u = (prepared[i : i + 2] for i in (0, 2, 4, 6))
    small, ffn_small = prepared[8:]
    more, mine = tie(ffn_parts, mine)
    ffn_parts.append(ffn_small)
    packed, local = tie(pack(0, more + [ffn_small]), local)
    ffn_w = [gather_ffn(packed), None]
    arranged = call(
        arrange_kernel,
        "arrange",
        gather4(small, along_y),
        [((4, 128, 256), BF), ((32, 512), BF), ((16, 512), BF), ((8, 512), F32)] * 2,
        [pltpu.VMEM((4, 2, 400, 128), BF)],
        scalars,
    )
    w_mix = {}
    start = (seq, half * BLOCK + x * HOME, 0)
    residual = lax.dynamic_slice(tokens, start, (1, HOME, width))[0]
    position = (z * 2 + core) * 512 + half * BLOCK + x * HOME + jnp.arange(HOME)
    valid = (position < lengths[seq]).astype(F32)[:, None]
    of_rows = jnp.where(core == 0, y, (y - jnp.arange(4)) % 4) // 2
    of_rows = jnp.repeat(of_rows, HOME)[:, None]
    of_cols = jnp.arange(32) // RANK
    mask = (of_rows == of_cols[None, :]).astype(F32)
    rows_like = [((HOME, width), BF)] * 4
    group_sem = pltpu.SemaphoreType.DMA((2, 4))
    ffn_sem = pltpu.SemaphoreType.DMA((3, 4))
    ffn_buffers = [pltpu.VMEM((1152, width), BF)] * 3
    mix_buffer = pltpu.VMEM((512, width), BF)
    half_f = ((BLOCK, 512), F32)
    pair_f = ((2, BLOCK, 512), F32)
    half_b = ((BLOCK, 512), BF)
    low_b = ((BLOCK, RANK), BF)

    kept = []
    for l in range(2):
        k = {"residual": residual}
        down, up_out = mix_d[l], out_u[l]
        gw, up, down_out, params = arranged[l * 4 : l * 4 + 4]
        if l == 0:
            normed, lat_b, lat_i = normed_0, lat_b_0, lat_i_0
            inputs, last, act, pull = call(
                unpack_kernel,
                "unpack",
                local,
                [half_b, ((16, 512), BF), half_f, half_f],
                [pltpu.VMEM((4, BLOCK, 256), BF)],
                scalars,
            )
            halo = send(last, next_block(False))
        else:
            blocks = gather4(normed_low, along_x)
            packed, _ = tie(packed, (mine, blocks))
            ffn_w[1] = gather_ffn(packed)
            w_mix[1] = [mine, send(mine, other_core)]
            normed, inputs, last, lat_b, lat_i = mixer(
                inputs_kernel,
                "inputs",
                [*blocks, down, up],
                [((BLOCK, width), BF), half_b, ((16, 512), BF), low_b, low_b],
                [mix_buffer, group_sem],
                scalars,
                w_mix[l],
            )
            halo = send(last, next_block(False))
            act, pull = mixer(
                branch_kernel,
                "branch",
                [normed, lat_b, up],
                [half_f, half_f],
                [mix_buffer, group_sem],
                scalars,
                w_mix[l],
            )
        saved, decay, scan, ends = call(
            gates_kernel,
            "gates",
            [inputs, halo, params, gw],
            [((3, BLOCK, 512), F32), half_f, pair_f, ((2, 512), F32)],
            [pltpu.VMEM((BLOCK + 16, 512), F32), pltpu.VMEM((BLOCK, 512), F32)],
            scalars,
        )
        carry = entering(ends, core, half, False)
        w_back_l = [w_back] if l == 0 else w_mix[1]
        states, mixed, out_latent, *parts = mixer(
            mixed_kernel,
            "mixed",
            [carry, scan, act, down_out, up_out],
            [half_f, half_b, low_b] + rows_like,
            [mix_buffer, pltpu.VMEM((BLOCK, width), BF), group_sem],
            scalars,
            w_back_l,
        )
        if l == 0:
            (halves_of, more), _ = tie(((w_branch, input_weight, w_out), ffn_parts), parts[0])
            mine, packed = half_of(scalars, 1, *halves_of), pack(1, more)
        parts = deal4(parts, along_x)
        if l == 1:
            parts, w_pair = tie(parts, pair_of(0, w_branch, input_weight))
        residual, normed_low = call(
            functools.partial(add_norm_kernel, l),
            "add_norm",
            [*parts, residual, ffn_gain],
            [((HOME, width), F32), ((HOME, width), BF)],
        )
        k.update(
            down=down, up=up, down_out=down_out, up_out=up_out, gw=gw, params=params,
            normed=normed, lat_b=lat_b, lat_i=lat_i, act=act, pull=pull, saved=saved, decay=decay, ends=ends,
            carry=carry, states=states, mixed=mixed, out_latent=out_latent,
            residual_one=residual,
        )
        if l == 1:
            grad = lax.dynamic_slice(cotangent, start, (1, HOME, width))[0] * valid
            grad_low, _ = tie(grad.astype(BF), carry)
            grad_blocks = gather4(grad_low, ffn_rows)
        blocks = gather4(normed_low, ffn_rows)
        if l == 0:
            mine, _ = tie(mine, (ffn_w[0], blocks))
            mine = lax.all_gather(mine, "y")
        down, up_back = ffn_d[l], back_u[l]
        (ffn_a,) = call(
            join_kernel,
            "join",
            [],
            [((96, 1152), BF)],
            [
                pltpu.VMEM((4, 32, width), BF), pltpu.VMEM((96, 1152), F32),
                pltpu.SemaphoreType.DMA((4,)),
            ],

            far=[ffn_w[l]],
        )
        gate, ups = None, None
        if l == 0:
            gate, ups, hidden, latent, back_latent, *parts = call(
                ffn_kernel,
                "ffn",
                [*blocks, ffn_a, down, up_back, mask],
                [((BLOCK, 1152), F32)] * 2
                + [((BLOCK, 1152), BF), ((2, BLOCK, 32), BF), ((BLOCK, 32), BF)]
                + rows_like,
                [pltpu.VMEM((BLOCK, width), BF)] + ffn_buffers + [ffn_sem],
                far=[ffn_w[l]],
                mflops=2800,
                mbytes=15,
            )
        else:
            hidden, latent, back_latent, *turned_back = call(
                ffn_turn_kernel,
                "ffn_turn",
                [*blocks, *grad_blocks, ffn_a, down, up_back, mask],
                [((BLOCK, 1152), BF), ((2, BLOCK, 32), BF), ((BLOCK, 32), BF)]
                + [((BLOCK, 1152), BF)] * 2
                + [((BLOCK, 32), BF), ((2, BLOCK, 32), BF), ((BLOCK, width), BF)]
                + [((2 * HOME, width), BF)] * 4,
                [pltpu.VMEM((BLOCK, width), BF)] + ffn_buffers + [ffn_sem],
                far=[ffn_w[l]],
                mflops=5600,
                mbytes=15,
            )
            g_gate, g_up, g_back, g_latent, rows, *parts = turned_back
        k.update(
            ffn_a=ffn_a, down_two=down, up_back=up_back, blocks=blocks, gate=gate, ups=ups, hidden=hidden,
            latent=latent, back_latent=back_latent,
        )
        if l == 0:
            parts, tables = tie(deal4(parts, ffn_rows), empty_tables())
            residual, normed_low = call(
                functools.partial(add_norm_kernel, 1),
                "add_norm",
                [*parts, residual, mix_gain],
                [((HOME, width), F32), ((HOME, width), BF)],
            )
        kept.append(k)
    for l in (1, 0):
        k = kept[l]
        w_back_l, w_in_l = ([w_back], [w_in]) if l == 0 else (w_mix[1], w_mix[1])
        if l == 0:
            blocks = gather4(grad_low, ffn_rows)
            blocks, side = tie(blocks, side)
            side = steps.send(side)
            g_gate, g_up, g_back, g_latent, rows, *parts = call(
                ffn_back_kernel,
                "ffn_back",
                [*blocks, k["ffn_a"], k["down_two"], k["up_back"], mask, k["gate"], k["ups"]],
                [((BLOCK, 1152), BF)] * 2
                + [((BLOCK, 32), BF), ((2, BLOCK, 32), BF), ((BLOCK, width), BF)]
                + rows_like,
                ffn_buffers + [ffn_sem],
                far=[ffn_w[l]],
                mflops=2800,
                mbytes=15,
            )
        if l == 0:
            parts, side = tie(parts, side)
        parts = deal4(parts, ffn_rows)
        if l == 0:
            side, parts[1] = tie(side, parts[1])
            side = steps.send(side)
        ffn_whole, ffn_split = call(
            ffn_adapters_kernel,
            "ffn_adapters",
            [
                *k["blocks"], rows, k["latent"], k["back_latent"], k["hidden"], g_gate, g_up,
                g_back, g_latent,
            ],
            [((96, width), BF), ((96, 1152), BF)],
            [pltpu.VMEM((BLOCK, width), BF)],
            mflops=200,
        )
        parts, (ffn_whole, ffn_split) = tie(parts, (ffn_whole, ffn_split))
        out_parts = parts
        grad, grad_low = call(
            functools.partial(norm_back_kernel, l),
            "norm_back",
            [*parts, grad, k["residual_one"], ffn_gain],
            [((HOME, width), F32), ((HOME, width), BF)],
        )
        blocks = gather4(grad_low, along_x)
        if l == 1:
            (out_parts, shard_part), _ = tie((out_parts, ffn_split), grad_low)
            (output,) = call(
                output_kernel, "output", [*out_parts, residual, valid], [((HOME, width), BF)]
            )
            output = lax.all_gather(output, ("y", "x"), axis=0, tiled=True)
            shard_part = reduce_shards(shard_part)
        else:
            flat = jnp.concatenate([side[:48], shard_1, side[48:]], axis=0)
            flat, _ = tie(flat, grad_low)
            flat = sum_z(flat)
        rows, g_mixed, g_low, back, ends = mixer(
            states_back_kernel,
            "states_back",
            [*blocks, k["down_out"], k["up_out"], k["act"], k["decay"], k["ends"]],
            [((BLOCK, width), BF), half_b, low_b, pair_f, ((2, 512), F32)],
            [mix_buffer, pltpu.VMEM((BLOCK + 8, 512), F32), pltpu.VMEM((BLOCK, 512), F32)]
            + [group_sem],
            scalars,
            w_back_l,
        )
        if l == 1:
            ends, shard_part = tie(ends, shard_part)
        else:
            ends, (flat, output) = tie(ends, (flat, output))
            flat = lax.all_gather(flat, ("core", "y", "x")).reshape(2, 4, 4, 304, 128)
        if l == 1:
            w_pair, _ = tie(w_pair, ends)
            w_in = lax.all_gather(w_pair, "y")
        carry = entering(ends, core, half, True)
        part, g_up_out, g_down_out, g_up_b, g_low_b = mixer(
            branch_back_kernel,
            "branch_back",
            [
                rows, g_mixed, g_low, k["states"], k["pull"], k["mixed"], k["out_latent"],
                k["lat_b"], k["up"], k["down"],
            ],
            [((BLOCK, width), F32), ((RANK, width), F32), ((RANK, 512), F32), ((RANK, 512), F32)]
            + [low_b],
            [mix_buffer, group_sem],
            scalars,
            w_in_l,
        )
        carry, part = tie(carry, part)
        if l == 1:
            shard_part, _ = tie(shard_part, carry)
            shard_1 = halves(shard_part, core, other_core)

        g_conv, rim = call(
            gates_back_kernel,
            "gates_back",
            [
                carry, k["carry"], back, k["states"], k["saved"], k["decay"], k["params"],
                k["gw"],
            ],
            [half_f, ((8, 512), F32)],
            [pltpu.VMEM((BLOCK + 8, 512), F32)],
            scalars,
        )
        halo = send(rim, next_block(True))
        if l == 1:
            halo, shard_1 = tie(halo, shard_1)
            shard_1 = blocks_of(shard_1, 48)
        *parts, mine, theirs = mixer(
            inputs_back_kernel,
            "inputs_back",
            [
                g_conv, halo, k["params"], k["up"], k["down"], part, k["normed"], k["lat_i"],
                g_low_b, g_up_b, g_up_out, g_down_out, ffn_whole,
            ],
            rows_like + [((80, width), F32), ((80, width), BF)],
            [
                pltpu.VMEM((BLOCK + 8, 512), F32), mix_buffer, pltpu.VMEM((BLOCK, width), BF),
                pltpu.VMEM((48, width), F32), pltpu.VMEM((48, 512), F32),
                pltpu.VMEM((2, 80, width), F32), group_sem,
            ],
            scalars,
            w_in_l,
        )
        parts = deal4(parts, along_x)
        steps = reduce_steps(mine, theirs)
        side = next(steps)
        grad, grad_low = call(
            functools.partial(norm_back_kernel, l),
            "norm_back",
            [*parts, grad, k["residual"], mix_gain],
            [((HOME, width), F32), ((HOME, width), BF)],
        )
    grad_tokens = lax.all_gather(grad_low, ("y", "x"), axis=0, tiled=True)
    shard_0, _ = tie(ffn_split, grad_low)
    shard_0 = reduce_shards(shard_0)
    side, shard_0 = tie(steps.send(side), shard_0)
    shard_0 = blocks_of(halves(shard_0, core, other_core), 48)
    side = steps.send(side)
    last = jnp.concatenate([side[:48], shard_0, side[48:]], axis=0)
    last = sum_z(last)
    last, (tables, output) = tie(last, (finish(ids, 1, [flat], tables), widen(output)))
    last = lax.all_to_all(jnp.broadcast_to(last, (16, 304, 128)), ("y", "x"), 0, 0, tiled=True)
    grad_tokens, _ = tie(grad_tokens, last)
    other, grad_tokens = tie(send(last, other_core), widen(grad_tokens))
    last = last, other
    ids = jnp.concatenate([ids, core[None].astype(jnp.int32)])
    gmd, gmu, god, gou, gfd, gfu, gbd, gbu = finish(ids, 0, last, tables)
    return (
        output.reshape(tokens.shape),
        grad_tokens.reshape(tokens.shape),
        turned(gmd),
        gmu.reshape(2, 8, 2, RANK, 2048),
        turned(god),
        gou,
        turned(gfd),
        gfu.reshape(2, 8, 2, RANK, 4608),
        turned(gbd),
        gbu,
    )


def solution(mesh):
    grid = Mesh(mesh.devices.reshape(4, 2, 4, 4), ALL)
    sp, mp = ("z", "core"), ("y", "x")
    in_specs = (
        P(None, sp, None),
        P(None, sp, None),
        P(),
        P(),
        P(),
        P(),
        P(None, None, mp),
        P(None, None, mp),
        P(None, None, mp),
        P(None, mp),
        P(None, mp, None, None),
        P(None, mp),
        P(None, mp, None, None),
        P(None, mp),
        P(None, mp),
        P(None, mp, None),
        P(None, None, mp),
        P(None, None, mp),
        P(None, mp, None),
        P(),
        P(None, None, None, None, mp),
        P(None, None, mp, None),
        P(),
        P(),
        P(None, None, None, None, mp),
        P(None, None, mp, None),
        P(),
    )
    out_specs = (P(None, sp, None), P(None, sp, None)) + (P(),) * 8
    return jax.shard_map(shards, mesh=grid, in_specs=in_specs, out_specs=out_specs, check_vma=False)
```

```python
import functools

import jax
import jax.numpy as jnp
from jax import lax
from jax.experimental import pallas as pl
from jax.experimental.pallas import tpu as pltpu
from jax.sharding import Mesh
from jax.sharding import PartitionSpec as P

ALL = ("z", "core", "y", "x")
BF = jnp.bfloat16
F32 = jnp.float32
RANK = 16
HOME = 64
BLOCK = 256
LIMIT = 60 * 2**20
LARGE = 60 * 2**20
GELU_C = 0.7978845608028654


def device_pairs(move):
    pairs = []
    for z in range(4):
        for c in range(2):
            for y in range(4):
                for x in range(4):
                    to = move(z, c, y, x)
                    if to is not None:
                        a = ((z * 2 + c) * 4 + y) * 4 + x
                        b = ((to[0] * 2 + to[1]) * 4 + to[2]) * 4 + to[3]
                        pairs.append((a, b))
    return pairs


def send(value, move):
    return lax.ppermute(value, ALL, device_pairs(move))


def along_x(d):
    return lambda z, c, y, x: (z, c, y, (x + d) % 4)


def along_y(d):
    return lambda z, c, y, x: (z, c, (y + d) % 4, x)


def ffn_rows(d):
    return lambda z, c, y, x: (z, c, y, (x + d) % 4) if c == 0 else (z, c, (y + d) % 4, x)


def ffn_shards(d):
    return lambda z, c, y, x: (z, c, (y + d) % 4, x) if c == 0 else (z, c, y, (x + d) % 4)


def shard_groups():
    at = lambda z, c, y, x: ((z * 2 + c) * 4 + y) * 4 + x
    columns = [[at(z, 0, y, x) for y in range(4)] for z in range(4) for x in range(4)]
    rows = [[at(z, 1, y, x) for x in range(4)] for z in range(4) for y in range(4)]
    return columns + rows


def gather4(value, moves):
    return [value] + [send(value, moves(j)) for j in (1, 2, 3)]


def deal4(parts, moves):
    return [parts[0]] + [send(parts[j], moves(-j)) for j in (1, 2, 3)]


def scatter4(parts, moves):
    moved = deal4(parts, moves)[1:]
    total = parts[0].astype(F32)
    for part in moved:
        total = total + part.astype(F32)
    return total


def split3(v):
    high = v.astype(BF)
    rest = v - high.astype(F32)
    mid = rest.astype(BF)
    return high, mid, (rest - mid.astype(F32)).astype(BF)


def tie(first, second):
    return lax.optimization_barrier((first, second))


def combine(earlier, later):
    return (earlier[0] * later[0], later[0] * earlier[1] + later[1])


def next_block(reverse):
    def move(z, c, y, x):
        at = (z * 2 + c) * 2 + y % 2 + (-1 if reverse else 1)
        if not 0 <= at < 16:
            return None
        return (at // 4, (at // 2) % 2, (y // 2) * 2 + at % 2, x)

    return move


def entering(own, core, half, reverse):
    one = jnp.stack([jnp.ones_like(own[0]), jnp.zeros_like(own[0])])

    def step(own, other, later):
        pre = jnp.where(later, other, one)
        first, second = jnp.where(later, other, own), jnp.where(later, own, other)
        both = combine((first[0], first[1]), (second[0], second[1]))
        return pre, jnp.stack(both)

    other = send(own, lambda z, c, y, x: (z, c, y ^ 1, x))
    pre_h, own = step(own, other, half == (0 if reverse else 1))
    other = send(own, lambda z, c, y, x: (z, 1 - c, y, x))
    pre_c, own = step(own, other, core == (0 if reverse else 1))
    far = []
    for d in (1, 2, 3):
        e = -d if reverse else d
        far.append(
            send(own, lambda z, c, y, x, e=e: (z + e, c, y, x) if 0 <= z + e < 4 else None)
        )
    state = far[2][1]
    for part in (far[1], far[0], pre_c, pre_h):
        state = part[0] * state + part[1]
    return state[None]


def nn(a, b):
    return jnp.dot(a, b, preferred_element_type=F32)


def nt(a, b):
    return lax.dot_general(a, b, (((1,), (1,)), ((), ())), preferred_element_type=F32)


def tn(a, b):
    return lax.dot_general(a, b, (((0,), (0,)), ((), ())), preferred_element_type=F32)


def gelu_pair(v):
    t = jnp.tanh(GELU_C * (v + 0.044715 * v * v * v))
    act = 0.5 * v * (1.0 + t)
    pull = 0.5 * (1.0 + t) + 0.5 * v * (1.0 - t * t) * (GELU_C * (1.0 + 0.134145 * v * v))
    return act, pull


def inverse_rms(v):
    return lax.rsqrt(jnp.mean(v * v, axis=-1, keepdims=True) + 1e-06)


def rms_backward(v, inverse, gain, grad):
    scaled = grad * gain
    return inverse * scaled - v * inverse**3 * jnp.mean(v * scaled, axis=-1, keepdims=True)


VMEM = pl.BlockSpec(memory_space=pltpu.VMEM)
SMEM = pl.BlockSpec(memory_space=pltpu.SMEM)
HBM = pl.BlockSpec(memory_space=pl.ANY)


def grouped(kernel, n_in, n_far):
    def run(sc, *refs):
        kernel(sc, refs[n_in : n_in + n_far], *refs[:n_in], *refs[n_in + n_far :])

    return run


def mixer(kernel, name, ins, outs, scratch, scalars, far):
    return call(
        grouped(kernel, len(ins), len(far)), name, ins, outs, scratch, scalars, far, mflops=420
    )


def call(kernel, name, ins, outs, scratch=(), scalars=None, far=(), mflops=100, mbytes=4):
    specs = [VMEM] * len(ins) + [HBM] * len(far)
    arrays = list(ins) + list(far)
    if scalars is not None:
        specs, arrays = [SMEM] + specs, [scalars] + arrays
    return pl.pallas_call(
        kernel,
        out_shape=[jax.ShapeDtypeStruct(shape, dtype) for shape, dtype in outs],
        in_specs=specs,
        out_specs=[VMEM] * len(outs),
        scratch_shapes=list(scratch),
        compiler_params=pltpu.CompilerParams(
            vmem_limit_bytes=LARGE if mflops > 1000 else LIMIT
        ),
        cost_estimate=pl.CostEstimate(
            flops=mflops * 10**6, bytes_accessed=mbytes * 10**6, transcendentals=0
        ),
        name=name,
    )(*arrays)


def fetch(source, rows, target, sem):
    first, count = rows
    copies = []
    for j in range(4):
        copy = pltpu.make_async_copy(
            source.at[j, pl.ds(first, count)],
            target.at[pl.ds(j * count, count)],
            sem.at[j],
        )
        copy.start()
        copies.append(copy)
    return copies


def fetch_half(sc, mine, other, rows, target, sem):
    first, count = rows
    pieces = []
    for half in range(2):
        low, high = max(first, half * 192), min(first + count, half * 192 + 192)
        if low < high:
            pieces.append((half, low - half * 192, high - low, low - first))
    copies = []
    for core in range(2):

        @pl.when(sc[4] == core)
        def _():
            for i, (half, low, size, at) in enumerate(pieces):
                source = mine if half == core else other
                for j in range(4):
                    pltpu.make_async_copy(
                        source.at[j, pl.ds(low, size)],
                        target.at[pl.ds(j * count + at, size)],
                        sem.at[i, j],
                    ).start()

    for i, (half, low, size, at) in enumerate(pieces):
        for j in range(4):
            copies.append(
                pltpu.make_async_copy(
                    mine.at[j, pl.ds(low, size)],
                    target.at[pl.ds(j * count + at, size)],
                    sem.at[i, j],
                )
            )
    return copies


def weights(sc, w, rows, target, sem):
    if len(w) == 2 and w[0].shape[1] == 192:
        return fetch_half(sc, *w, rows, target, sem)
    if len(w) == 2:
        copies = []
        for i, source in enumerate(w):
            half = sc[4] if i == 0 else 1 - sc[4]
            for j in range(4):
                at = pl.multiple_of(j * 128 + half * 64, 64)
                copy = pltpu.make_async_copy(
                    source.at[j], target.at[pl.ds(at, 64)], sem.at[i, j]
                )
                copy.start()
                copies.append(copy)
        return copies
    return fetch(w[0], (rows[0] % w[0].shape[1], rows[1]), target, sem.at[0])


def wait_all(copies):
    for copy in copies:
        copy.wait()


def place(scalars, blocks, rows_ref):
    for j in range(4):
        at = pl.multiple_of(lax.rem(scalars[0] + 4 - j, 4) * HOME, HOME)
        rows_ref[pl.ds(at, HOME), :] = blocks[j][...]


def take(scalars, total_ref, parts):
    for j in range(4):
        at = pl.multiple_of(lax.rem(scalars[0] + 4 - j, 4) * HOME, HOME)
        parts[j][...] = total_ref[pl.ds(at, HOME), :]


def scan_rows(reverse, a_ref, b_ref, cum_ref, out_ref):
    rows, width = a_ref.shape
    row = lax.broadcasted_iota(jnp.int32, (8, width), 0)
    groups = rows // 8

    def body(i, carry):
        ca, cb = carry
        at = pl.multiple_of((groups - 1 - i if reverse else i) * 8, 8)
        a, b = a_ref[pl.ds(at, 8), :], b_ref[pl.ds(at, 8), :]
        for k in (1, 2, 4):
            seen = row < 8 - k if reverse else row >= k
            by = 8 - k if reverse else k
            pa = jnp.where(seen, pltpu.roll(a, by, 0), 1.0)
            pb = jnp.where(seen, pltpu.roll(b, by, 0), 0.0)
            b = a * pb + b
            a = a * pa
        b = a * cb + b
        a = a * ca
        cum_ref[pl.ds(at, 8), :] = a
        out_ref[pl.ds(at, 8), :] = b
        last = 0 if reverse else 7
        return (
            jnp.broadcast_to(a[last : last + 1], a.shape),
            jnp.broadcast_to(b[last : last + 1], b.shape),
        )

    start = (jnp.ones((8, width), F32), jnp.zeros((8, width), F32))
    lax.fori_loop(0, groups, body, start, unroll=4)


def add_norm_kernel(l, p0, p1, p2, p3, residual, gain, out, normed):
    total = p0[...].astype(F32) + p1[...].astype(F32) + p2[...].astype(F32)
    v = residual[...] + total + p3[...].astype(F32)
    out[...] = v
    normed[...] = (v * inverse_rms(v) * gain[l : l + 1]).astype(BF)


def output_kernel(p0, p1, p2, p3, residual, valid, out):
    total = p0[HOME:].astype(F32) + p1[HOME:].astype(F32) + p2[HOME:].astype(F32)
    out[...] = ((residual[...] + total + p3[HOME:].astype(F32)) * valid[...]).astype(BF)


def norm_back_kernel(l, p0, p1, p2, p3, grad, v_ref, gain, out, low):
    total = p0[:HOME].astype(F32) + p1[:HOME].astype(F32) + p2[:HOME].astype(F32)
    total = total + p3[:HOME].astype(F32)
    v = v_ref[...]
    g = grad[...] + rms_backward(v, inverse_rms(v), gain[l : l + 1], total)
    out[...] = g
    low[...] = g.astype(BF)


def inputs_kernel(
    sc, w, n0, n1, n2, n3, down, up, normed, inputs, last, lat_b, lat_i, wi, sem
):
    copies = weights(sc, w, (128, 128), wi, sem)
    place(sc, (n0, n1, n2, n3), normed)
    rows = normed[...]
    lat_b[...] = nt(rows, down[:RANK]).astype(BF)
    low = nt(rows, down[RANK:]).astype(BF)
    lat_i[...] = low
    wait_all(copies)
    inputs[...] = (nt(rows, wi[...]) + nn(low, up[RANK:])).astype(BF)
    last[...] = inputs[BLOCK - 16 :]


def branch_kernel(sc, w, normed, lat_b, up, act, pull, wb, sem):
    copies = weights(sc, w, (0, 128), wb, sem)
    wait_all(copies)
    branch = nt(normed[...], wb[...]) + nn(lat_b[...], up[:RANK])
    act[...], pull[...] = gelu_pair(branch)


def gates_kernel(
    sc, inputs, halo, params, gw, saved, decay, scan, ends, ext, driven
):
    conv, gate_a, gate_i = (saved.at[i] for i in range(3))
    cum, local = scan.at[0], scan.at[1]
    ext[:16] = halo[...].astype(F32)
    ext[16:] = inputs[...].astype(F32)
    value = params[4:5] + params[0:1] * ext[pl.ds(16, BLOCK)]
    for o in (1, 2, 3):
        value = value + params[o : o + 1] * ext[pl.ds(16 - o, BLOCK)]
    conv[...] = value
    row = lax.broadcasted_iota(jnp.int32, (BLOCK, 128), 0)
    first = (row == 0) & (sc[1] == 1)
    for h in range(4):
        at = slice(h * 128, h * 128 + 128)
        c = conv[:, at]
        pre = nn(c.astype(BF), gw[h])
        a = jax.nn.sigmoid(pre[:, :128] + params[5:6, at])
        i = jax.nn.sigmoid(pre[:, 128:] + params[6:7, at])
        d = jnp.exp(a * params[7:8, at])
        gate_a[:, at] = a
        gate_i[:, at] = i
        decay[:, at] = d
        driven[:, at] = c * i * jnp.where(first, 1.0, jnp.sqrt(1.0 - d * d + 0.01))
    scan_rows(False, decay, driven, cum, local)
    ends[0:1] = cum[BLOCK - 1 :]
    ends[1:2] = local[BLOCK - 1 :]


def mixed_kernel(
    sc, w, carry, scan, act, down_out, up_out, states, mixed, out_latent, q0, q1, q2, q3,
    wo, total, sem,
):
    copies = weights(sc, w, (256, 128), wo, sem)
    s = scan[1] + scan[0] * carry[...]
    states[...] = s
    m = (s * act[...]).astype(BF)
    mixed[...] = m
    low = nt(m, down_out[...]).astype(BF)
    out_latent[...] = low
    wait_all(copies)
    total[...] = (nn(m, wo[...]) + nn(low, up_out[...])).astype(BF)
    take(sc, total, (q0, q1, q2, q3))


def ffn_kernel(
    n0, n1, n2, n3, a, down, up_back, mask, w, gate, up, hidden, latent, back_latent,
    q0, q1, q2, q3, rows_ref, wg, wu, wd, sem,
):
    cg = fetch(w, (0, 288), wg, sem.at[0])
    cu = fetch(w, (288, 288), wu, sem.at[1])
    cd = fetch(w, (576, 288), wd, sem.at[2])
    for j, n in enumerate((n0, n1, n2, n3)):
        rows_ref[j * HOME : (j + 1) * HOME] = n[...]
    rows = rows_ref[...]
    lat_g = (nt(rows, down[:32]) * mask[...]).astype(BF)
    lat_u = (nt(rows, down[32:]) * mask[...]).astype(BF)
    latent[0] = lat_g
    latent[1] = lat_u
    wait_all(cg)
    g = nt(rows, wg[...]) + nn(lat_g, a[:32])
    gate[...] = g
    wait_all(cu)
    u = nt(rows, wu[...]) + nn(lat_u, a[32:64])
    up[...] = u
    hidden[...] = (gelu_pair(g)[0] * u).astype(BF)
    h = hidden[...]
    low = (nt(h, a[64:]) * mask[...]).astype(BF)
    back_latent[...] = low
    wait_all(cd)
    total = (nn(h, wd[...]) + nn(low, up_back[...])).astype(BF)
    for j, q in enumerate((q0, q1, q2, q3)):
        q[...] = total[j * HOME : (j + 1) * HOME]


def ffn_back_kernel(
    r0, r1, r2, r3, a, down, up_back, mask, gate, up, w, g_gate, g_up, g_back, g_latent, rows_ref,
    q0, q1, q2, q3, wg, wu, wd, sem,
):
    cd = fetch(w, (576, 288), wd, sem.at[2])
    cg = fetch(w, (0, 288), wg, sem.at[0])
    cu = fetch(w, (288, 288), wu, sem.at[1])
    for j, r in enumerate((r0, r1, r2, r3)):
        rows_ref[j * HOME : (j + 1) * HOME] = r[...]
    rows = rows_ref[...]
    low = (nt(rows, up_back[...]) * mask[...]).astype(BF)
    g_back[...] = low
    wait_all(cd)
    gh = (nt(rows, wd[...]) + nn(low, a[64:])).astype(BF).astype(F32)
    act, pull = gelu_pair(gate[...])
    g_up[...] = (gh * act).astype(BF)
    g_gate[...] = (gh * up[...] * pull).astype(BF)
    gg, gu = g_gate[...], g_up[...]
    lat_g = (nt(gg, a[:32]) * mask[...]).astype(BF)
    lat_u = (nt(gu, a[32:64]) * mask[...]).astype(BF)
    g_latent[0] = lat_g
    g_latent[1] = lat_u
    wait_all(cg)
    total = nn(gg, wg[...]) + nn(lat_g, down[:32]) + nn(lat_u, down[32:])
    wait_all(cu)
    total = (total + nn(gu, wu[...])).astype(BF)
    for j, q in enumerate((q0, q1, q2, q3)):
        q[...] = total[j * HOME : (j + 1) * HOME]


def ffn_turn_kernel(
    n0, n1, n2, n3, r0, r1, r2, r3, a, down, up_back, mask, w,
    hidden, latent, back_latent, g_gate, g_up, g_back, g_latent, rows_ref,
    q0, q1, q2, q3, normed_ref, wg, wu, wd, sem,
):
    cg = fetch(w, (0, 288), wg, sem.at[0])
    cu = fetch(w, (288, 288), wu, sem.at[1])
    cd = fetch(w, (576, 288), wd, sem.at[2])
    for j, (n, r) in enumerate(((n0, r0), (n1, r1), (n2, r2), (n3, r3))):
        normed_ref[j * HOME : (j + 1) * HOME] = n[...]
        rows_ref[j * HOME : (j + 1) * HOME] = r[...]
    normed, rows = normed_ref[...], rows_ref[...]
    lat_g = (nt(normed, down[:32]) * mask[...]).astype(BF)
    lat_u = (nt(normed, down[32:]) * mask[...]).astype(BF)
    latent[0] = lat_g
    latent[1] = lat_u
    low = (nt(rows, up_back[...]) * mask[...]).astype(BF)
    g_back[...] = low
    wait_all(cg)
    g = nt(normed, wg[...]) + nn(lat_g, a[:32])
    wait_all(cu)
    u = nt(normed, wu[...]) + nn(lat_u, a[32:64])
    act, pull = gelu_pair(g)
    hidden[...] = (act * u).astype(BF)
    wait_all(cd)
    gh = (nt(rows, wd[...]) + nn(low, a[64:])).astype(BF).astype(F32)
    g_up[...] = (gh * act).astype(BF)
    g_gate[...] = (gh * u * pull).astype(BF)
    gg, gu = g_gate[...], g_up[...]
    lat_g = (nt(gg, a[:32]) * mask[...]).astype(BF)
    lat_u = (nt(gu, a[32:64]) * mask[...]).astype(BF)
    g_latent[0] = lat_g
    g_latent[1] = lat_u
    total = nn(gg, wg[...]) + nn(lat_g, down[:32]) + nn(lat_u, down[32:])
    total = (total + nn(gu, wu[...])).astype(BF)
    for j, q in enumerate((q0, q1, q2, q3)):
        q[:HOME] = total[j * HOME : (j + 1) * HOME]
    h = hidden[...]
    low = (nt(h, a[64:]) * mask[...]).astype(BF)
    back_latent[...] = low
    total = (nn(h, wd[...]) + nn(low, up_back[...])).astype(BF)
    for j, q in enumerate((q0, q1, q2, q3)):
        q[HOME:] = total[j * HOME : (j + 1) * HOME]


def ffn_adapters_kernel(
    n0, n1, n2, n3, rows, latent, back_latent, hidden, g_gate, g_up, g_back, g_latent,
    whole, split, normed_ref,
):
    for j, n in enumerate((n0, n1, n2, n3)):
        normed_ref[j * HOME : (j + 1) * HOME] = n[...]
    normed = normed_ref[...]
    g_down = [tn(g_latent[0], normed), tn(g_latent[1], normed)]
    g_up_back = tn(back_latent[...], rows[...])
    for s in range(2):
        at = slice(s * RANK, s * RANK + RANK)
        whole[s * 48 : s * 48 + 16] = g_down[0][at].astype(BF)
        whole[s * 48 + 16 : s * 48 + 32] = g_down[1][at].astype(BF)
        whole[s * 48 + 32 : s * 48 + 48] = g_up_back[at].astype(BF)
    split[:32] = tn(latent[0], g_gate[...]).astype(BF)
    split[32:64] = tn(latent[1], g_up[...]).astype(BF)
    split[64:] = tn(g_back[...], hidden[...]).astype(BF)


def states_back_kernel(
    sc, w, r0, r1, r2, r3, down_out, up_out, act, decay, forward_ends,
    rows_ref, g_mixed, g_low, back, ends, wo, ext, g_states, sem,
):
    suffix, local = back.at[0], back.at[1]
    copies = weights(sc, w, (256, 128), wo, sem)
    place(sc, (r0, r1, r2, r3), rows_ref)
    rows = rows_ref[...]
    low = nt(rows, up_out[...]).astype(BF)
    g_low[...] = low
    ext[:BLOCK] = decay[...]
    ext[BLOCK:] = jnp.ones((8, 512), F32)
    ext[:BLOCK] = ext[pl.ds(1, BLOCK)]
    wait_all(copies)
    gm = (nt(rows, wo[...]) + nn(low, down_out[...])).astype(BF)
    g_mixed[...] = gm
    g_states[...] = gm.astype(F32) * act[...]
    scan_rows(True, ext.at[pl.ds(0, BLOCK)], g_states, suffix, local)
    ends[0:1] = forward_ends[0:1]
    ends[1:2] = decay[0:1] * local[0:1]


def branch_back_kernel(
    sc, w, rows, g_mixed, g_low, states, pull, mixed, out_latent, lat_b, up, down,
    part, g_up_out, g_down_out, g_up_b, g_branch_low, wb, sem,
):
    copies = weights(sc, w, (0, 128), wb, sem)
    gb = (g_mixed[...].astype(F32) * states[...] * pull[...]).astype(BF)
    low = nt(gb, up[:RANK]).astype(BF)
    g_branch_low[...] = low
    g_up_out[...] = tn(out_latent[...], rows[...])
    g_down_out[...] = tn(g_low[...], mixed[...])
    g_up_b[...] = tn(lat_b[...], gb)
    wait_all(copies)
    part[...] = nn(gb, wb[...]) + nn(low, down[:RANK])


def gates_back_kernel(
    sc, carry, carry_in, back, states, saved, decay, params, gw, g_conv, rim, ext
):
    conv, gate_a, gate_i = (saved.at[i] for i in range(3))
    suffix, local = back.at[0], back.at[1]
    ext[:8] = jnp.broadcast_to(carry_in[...], (8, 512))
    ext[8:] = states[...]
    row = lax.broadcasted_iota(jnp.int32, (BLOCK, 128), 0)
    first = (row == 0) & (sc[1] == 1)
    for h in range(4):
        at = slice(h * 128, h * 128 + 128)
        gd = local[:, at] + suffix[:, at] * carry[:, at]
        d, i, a, c = decay[:, at], gate_i[:, at], gate_a[:, at], conv[:, at]
        scale = jnp.where(first, 1.0, jnp.sqrt(1.0 - d * d + 0.01))
        g_scale = gd * c * i
        previous = ext[pl.ds(7, BLOCK), at]
        g_decay = gd * previous - jnp.where(first, 0.0, g_scale * (d / scale))
        ga = (g_decay * d * params[7:8, at] * a * (1.0 - a)).astype(BF)
        gi = (g_scale * scale * (1.0 - i)).astype(BF)
        g_conv[:, at] = gd * i * scale + nt(ga, gw[h, :, :128]) + nt(gi, gw[h, :, 128:])
    rim[...] = g_conv[:8]


def inputs_back_kernel(
    sc, w, g_conv, halo, params, up, down, part, normed, lat_i, g_low_b, g_up_b, g_up_out,
    g_down_out, ffn_whole, q0, q1, q2, q3, mine, theirs, ext, wi, total, whole, split, wide, sem,
):
    copies = weights(sc, w, (128, 128), wi, sem)
    ext[:BLOCK] = g_conv[...]
    ext[BLOCK:] = halo[...]
    value = params[0:1] * ext[:BLOCK]
    for o in (1, 2, 3):
        value = value + params[o : o + 1] * ext[pl.ds(o, BLOCK)]
    gi = value.astype(BF)
    low = nt(gi, up[RANK:]).astype(BF)
    whole[:RANK] = tn(g_low_b[...], normed[...])
    whole[RANK:32] = tn(low, normed[...])
    whole[32:] = g_up_out[...]
    split[:RANK] = g_up_b[...]
    split[RANK:32] = tn(lat_i[...], gi)
    split[32:] = g_down_out[...]
    for c in range(2):
        wide[c, :48] = ffn_whole[c * 48 : c * 48 + 48].astype(F32)
        wide[c, 48:72] = whole[c * 24 : c * 24 + 24]
        for i in range(3):
            at = c * 24 + i * 8
            wide[c, 72:, i * 512 : i * 512 + 512] = split[at : at + 8]
    mine[...] = wide[sc[4]]
    theirs[...] = wide[1 - sc[4]].astype(BF)
    wait_all(copies)
    total[...] = (part[...] + nn(gi, wi[...]) + nn(low, down[RANK:])).astype(BF)
    take(sc, total, (q0, q1, q2, q3))


def head_kernel(
    sc, tokens, down, up, gain, wb, wi, o0, o1, o2, o3, normed, lat_b, lat_i, w
):
    j = pl.program_id(0)

    @pl.when(j == 0)
    def _():
        w[:, :128] = wb[0]
        w[:, 128:] = wi[0]

    v = tokens[0]
    rows = (v * inverse_rms(v) * gain[0:1]).astype(BF)
    low_b = nt(rows, down[0, 0, :RANK]).astype(BF)
    low_i = nt(rows, down[0, 0, RANK:]).astype(BF)
    both = nn(rows, w[...])
    branch = (both[:, :128] + nn(low_b, up[0, 0, :RANK])).astype(BF)
    inputs = (both[:, 128:] + nn(low_i, up[0, 0, RANK:])).astype(BF)
    for i, out in enumerate((o0, o1, o2, o3)):

        @pl.when(j == i)
        def _():
            out[:, :128] = branch
            out[:, 128:] = inputs

    @pl.when(j == 0)
    def _():
        normed[...] = rows
        lat_b[...] = low_b
        lat_i[...] = low_i


def head(scalars, tokens, down, up, gain, wb, wi):
    at = lambda j, sc: lax.rem(sc[0] + 4 - j, 4)
    own = lambda j, sc: (0, sc[1 + at(j, sc) // 2], 0, 0)
    fixed = lambda j, sc: (0, 0)
    block = ((BLOCK, 256), BF)
    outs = [block] * 4 + [((BLOCK, 1536), BF), ((BLOCK, RANK), BF), ((BLOCK, RANK), BF)]
    return pl.pallas_call(
        head_kernel,
        out_shape=[jax.ShapeDtypeStruct(shape, dtype) for shape, dtype in outs],
        grid_spec=pltpu.PrefetchScalarGridSpec(
            num_scalar_prefetch=1,
            grid=(4,),
            in_specs=[
                pl.BlockSpec((1, BLOCK, 1536), lambda j, sc: (at(j, sc) // 2, at(j, sc) % 2, 0)),
                pl.BlockSpec((1, 1, 32, 1536), own),
                pl.BlockSpec((1, 1, 32, 128), own),
                pl.BlockSpec((2, 1536), fixed),
                pl.BlockSpec((1, 1536, 128), lambda j, sc: (0, 0, 0)),
                pl.BlockSpec((1, 1536, 128), lambda j, sc: (0, 0, 0)),
            ],
            out_specs=[pl.BlockSpec(shape, fixed) for shape, _ in outs],
            scratch_shapes=[pltpu.VMEM((1536, 256), BF)],
        ),
        compiler_params=pltpu.CompilerParams(vmem_limit_bytes=LIMIT),
        cost_estimate=pl.CostEstimate(
            flops=900 * 10**6, bytes_accessed=9 * 10**6, transcendentals=0
        ),
        name="head",
    )(scalars, tokens, down, up, gain, wb, wi)


def prepare_kernel(
    sc, md, ou, fd0, fd1, bu0, bu1, mu0, mu1, od0, od1, fu0, fu1, bd0, bd1,
    ga, gi, cw, cb, ab, ib, dp, mix_d0, mix_d1, out_u0, out_u1, ffn_d0, ffn_d1, back_u0, back_u1,
    small, ffn_small,
):
    l = pl.program_id(0)
    for i, (mix_d, out_u, ffn_d, back_u) in enumerate(
        ((mix_d0, out_u0, ffn_d0, back_u0), (mix_d1, out_u1, ffn_d1, back_u1))
    ):

        @pl.when(l == i)
        def _():
            mix_d[...] = md[0, 0]
            out_u[...] = ou[0, 0]
            for s, (fd, bu) in enumerate(((fd0, bu0), (fd1, bu1))):
                ffn_d[s * 16 : s * 16 + 16] = fd[0, 0, :16]
                ffn_d[32 + s * 16 : 48 + s * 16] = fd[0, 0, 16:]
                back_u[s * 16 : s * 16 + 16] = bu[0, 0]

    ffn_small[...] = jnp.zeros(ffn_small.shape, BF)
    small[0, :128] = ga[0, 0]
    small[0, 128:256] = gi[0, 0]
    for s, (mu, od, fu, bd) in enumerate(((mu0, od0, fu0, bd0), (mu1, od1, fu1, bd1))):
        small[0, 256 + s * 32 : 288 + s * 32] = mu[0, 0]
        small[0, 320 + s * 16 : 336 + s * 16] = od[0, 0]
        at = slice(s * 16, s * 16 + 16)
        ffn_small[0, at, :288] = fu[0, 0, :16]
        ffn_small[0, at, 384:672] = fu[0, 0, 16:]
        ffn_small[0, at, 768:1056] = bd[0, 0]
    vectors = [ref[pl.ds(l, 1), :] for ref in (cb, ab, ib, dp)]
    wide = jnp.concatenate([cw[0]] + vectors + [jnp.zeros((8, 128), F32)], axis=0)
    for i, part in enumerate(split3(wide)):
        small[0, 352 + 16 * i : 368 + 16 * i] = part


def prepare(picks, owned, tables, singles, vectors):
    specs, arrays = [], []
    for table, which in [(t, (2,)) for t in owned] + [(t, (0, 1)) for t in tables]:
        for s in which:
            specs.append(
                pl.BlockSpec((1, 1) + table.shape[2:], lambda l, sc, s=s: (l, sc[s], 0, 0))
            )
            arrays.append(table)
    for single in singles:
        dims = single.ndim - 1
        specs.append(
            pl.BlockSpec((1,) + single.shape[1:], lambda l, sc, dims=dims: (l,) + (0,) * dims)
        )
        arrays.append(single)
    for vector in vectors:
        specs.append(pl.BlockSpec(vector.shape, lambda l, sc: (0, 0)))
        arrays.append(vector)
    flat = [(32, 1536), (16, 1536), (64, 1536), (32, 1536)]
    flat = [shape for shape in flat for _ in range(2)]
    tall = [(400, 128), (32, 1536)]
    return pl.pallas_call(
        prepare_kernel,
        out_shape=[jax.ShapeDtypeStruct(shape, BF) for shape in flat]
        + [jax.ShapeDtypeStruct((2,) + shape, BF) for shape in tall],
        grid_spec=pltpu.PrefetchScalarGridSpec(
            num_scalar_prefetch=1,
            grid=(2,),
            in_specs=specs,
            out_specs=[pl.BlockSpec(shape, lambda l, sc: (0, 0)) for shape in flat]
            + [pl.BlockSpec((1,) + shape, lambda l, sc: (l, 0, 0)) for shape in tall],
        ),
        compiler_params=pltpu.CompilerParams(vmem_limit_bytes=LIMIT),
        cost_estimate=pl.CostEstimate(flops=10**6, bytes_accessed=4 * 10**6, transcendentals=0),
        name="prepare",
    )(picks, *arrays)


def arrange_kernel(sc, s0, s1, s2, s3, *refs):
    small = refs[-1]
    for j, block in enumerate((s0, s1, s2, s3)):
        small[lax.rem(sc[2] + 4 - j, 4)] = block[...]
    seq = sc[2] // 2
    for l in range(2):
        gw, up, down_out, params = refs[l * 4 : l * 4 + 4]
        for p in range(4):
            at = slice(p * 128, p * 128 + 128)
            gw[p, :, :128] = small[p, l, :128]
            gw[p, :, 128:] = small[p, l, 128:256]
            start = pl.multiple_of(256 + seq * 32, 32)
            up[:, at] = small[p, l, pl.ds(start, 32), :]
            start = pl.multiple_of(320 + seq * 16, 16)
            down_out[:, at] = small[p, l, pl.ds(start, 16), :]
            parts = [small[p, l, 352 + 16 * i : 368 + 16 * i].astype(F32) for i in range(3)]
            total = parts[0] + parts[1] + parts[2]
            params[:, at] = total[:8]
            params[7:8, at] = -8.0 * jax.nn.softplus(total[7:8])


def join_kernel(w, a, held, wide, sem):
    copies = []
    for j in range(4):
        copy = pltpu.make_async_copy(w.at[j, pl.ds(864, 32)], held.at[j], sem.at[j])
        copy.start()
        copies.append(copy)
    wait_all(copies)
    for j in range(4):
        for i in range(3):
            part = held[j, :, i * 384 : i * 384 + 288].astype(F32)
            wide[i * 32 : i * 32 + 32, j * 288 : j * 288 + 288] = part
    a[...] = wide[...].astype(BF)


def order_kernel(sc, b0, b1, b2, b3, out):
    for j, block in enumerate((b0, b1, b2, b3)):
        out[lax.rem(sc[2] + 4 - j, 4)] = block[...]


def order_x_kernel(sc, b0, b1, b2, b3, out):
    for j, block in enumerate((b0, b1, b2, b3)):
        out[lax.rem(sc[0] + 4 - j, 4)] = block[...]


def unpack_kernel(sc, b0, b1, b2, b3, inputs, last, act, pull, held):
    for j, block in enumerate((b0, b1, b2, b3)):
        held[lax.rem(sc[2] + j, 4)] = block[...]
    for p in range(4):
        at = slice(p * 128, p * 128 + 128)
        inputs[:, at] = held[p, :, 128:]
        act[:, at], pull[:, at] = gelu_pair(held[p, :, :128].astype(F32))
    last[...] = inputs[BLOCK - 16 :]


def pack_kernel(a_ref, b_ref, c_ref, d_ref, out):
    at = 0
    for ref in (a_ref, b_ref, c_ref, d_ref):
        count = ref.shape[1]
        out[at : at + count] = ref[0]
        at += count


def pack(l, parts):
    width = parts[0].shape[2]
    total = sum(part.shape[1] for part in parts)
    return pl.pallas_call(
        pack_kernel,
        out_shape=jax.ShapeDtypeStruct((total, width), BF),
        grid=(2,),
        in_specs=[pl.BlockSpec((1, p.shape[1], width // 2), lambda i: (l, 0, i)) for p in parts],
        out_specs=pl.BlockSpec((total, width // 2), lambda i: (0, i)),
        compiler_params=pltpu.CompilerParams(vmem_limit_bytes=LIMIT),
        cost_estimate=pl.CostEstimate(flops=0, bytes_accessed=5 * 10**6, transcendentals=0),
        name="pack",
    )(*parts)


def pair_kernel(a_ref, b_ref, out):
    out[:128] = a_ref[0].T
    out[128:] = b_ref[0].T


def pair_of(l, a, b):
    rows = a.shape[1] // 3
    piece = pl.BlockSpec((1, rows, 128), lambda i: (l, i, 0))
    return pl.pallas_call(
        pair_kernel,
        out_shape=jax.ShapeDtypeStruct((256, a.shape[1]), BF),
        grid=(3,),
        in_specs=[piece] * 2,
        out_specs=pl.BlockSpec((256, rows), lambda i: (0, i)),
        compiler_params=pltpu.CompilerParams(vmem_limit_bytes=LIMIT),
        cost_estimate=pl.CostEstimate(flops=0, bytes_accessed=2 * 10**6, transcendentals=0),
        name="pair",
    )(a, b)


def half_kernel(sc, a_ref, b_ref, c_ref, out):
    @pl.when(sc[4] == 0)
    def _():
        out[:128] = a_ref[0].T
        out[128:] = b_ref[0, :, :].T[:64]

    @pl.when(sc[4] == 1)
    def _():
        out[:64] = b_ref[0, :, :].T[64:]
        out[64:] = c_ref[0]


def half_of(scalars, l, a, b, c):
    rows = a.shape[1] // 3
    piece = pl.BlockSpec((1, rows, 128), lambda i, sc: (l, i, 0))
    return pl.pallas_call(
        half_kernel,
        out_shape=jax.ShapeDtypeStruct((192, a.shape[1]), BF),
        grid_spec=pltpu.PrefetchScalarGridSpec(
            num_scalar_prefetch=1,
            grid=(3,),
            in_specs=[piece] * 2 + [pl.BlockSpec((1, 128, rows), lambda i, sc: (l, 0, i))],
            out_specs=pl.BlockSpec((192, rows), lambda i, sc: (0, i)),
        ),
        compiler_params=pltpu.CompilerParams(vmem_limit_bytes=LIMIT),
        cost_estimate=pl.CostEstimate(flops=0, bytes_accessed=2 * 10**6, transcendentals=0),
        name="half",
    )(scalars, a, b, c)


def finish_kernel(ranked, sc, *refs):
    mix_d, mix_u, out_d, out_u, ffn_d, ffn_u, back_d, back_u, whole, shard, split = refs[-11:]
    a = pl.program_id(0)

    @pl.when(a == 0)
    def _():
        for c in range(2):
            for y in range(4):
                for x in range(4):
                    if ranked:
                        mine, other = (ref[y * 4 + x].astype(F32) for ref in refs[:2])
                        v = jnp.where(sc[2] == c, mine, other)
                    else:
                        v = refs[0][c, y, x].astype(F32)
                    row = c * 24 + (y % 2) * 12
                    for k in range(3):
                        lane = x * 384 + k * 128
                        whole[c, y * 12 : y * 12 + 12, lane : lane + 128] = v[
                            k * 16 : k * 16 + 12
                        ]
                        whole[y // 2, 48 + row : 60 + row, lane : lane + 128] = v[
                            192 + k * 16 : 204 + k * 16
                        ]
                        lane = (y * 4 + x) * 288 + k * 128
                        part = v[48 + k * 48 : 96 + k * 48]
                        wide = 32 if k == 2 else 128
                        shard[c * 48 : c * 48 + 48, lane : lane + wide] = part[:, :wide]
                    for p in range(4):
                        lane = (p * 4 + x) * 128
                        k = 192 + (3 + p) * 16
                        split[y // 2, row : row + 12, lane : lane + 128] = v[k : k + 12]

    w = [((sc[s] == sc[0]) == (sc[a] == sc[0])).astype(F32) for s in range(2)]
    both = lambda get: get(0) * w[0] + get(1) * w[1]
    ffn_d[0, 0] = both(lambda s: whole[s, :32])
    back_u[0, 0] = both(lambda s: whole[s, 32:48])
    mix_d[0, 0] = both(lambda s: whole[s, 48:80])
    out_u[0, 0] = both(lambda s: whole[s, 80:])
    ffn_u[0, 0, :16] = both(lambda s: shard[s * 16 : s * 16 + 16])
    ffn_u[0, 0, 16:] = both(lambda s: shard[32 + s * 16 : 48 + s * 16])
    back_d[0, 0] = both(lambda s: shard[64 + s * 16 : 80 + s * 16])
    mix_u[0, 0] = both(lambda s: split[s, :32])
    out_d[0, 0] = both(lambda s: split[s, 32:])


TABLES = [(32, 1536), (32, 2048), (16, 2048), (16, 1536), (32, 1536), (32, 4608), (16, 4608)]
TABLES.append((16, 1536))


def zeros_kernel(after, *refs):
    del after
    for ref in refs:
        ref[...] = jnp.zeros(ref.shape, F32)


def empty_tables(after):
    return pl.pallas_call(
        zeros_kernel,
        out_shape=[jax.ShapeDtypeStruct((2, 8) + shape, F32) for shape in TABLES],
        grid=(2, 4),
        in_specs=[SMEM],
        out_specs=[pl.BlockSpec((1, 2) + shape, lambda l, a: (l, a, 0, 0)) for shape in TABLES],
        compiler_params=pltpu.CompilerParams(vmem_limit_bytes=LIMIT),
        cost_estimate=pl.CostEstimate(flops=10**6, bytes_accessed=20 * 10**6, transcendentals=0),
        name="zeros",
    )(after)


def finish(ids, layer, flats, tables):
    return pl.pallas_call(
        functools.partial(finish_kernel, len(flats) == 2),
        out_shape=[jax.ShapeDtypeStruct((2, 8) + shape, F32) for shape in TABLES],
        grid_spec=pltpu.PrefetchScalarGridSpec(
            num_scalar_prefetch=1,
            grid=(2,),
            in_specs=[VMEM] * len(flats) + [HBM] * len(tables),
            out_specs=[
                pl.BlockSpec((1, 1) + shape, lambda a, sc: (layer, sc[a], 0, 0))
                for shape in TABLES
            ],
            scratch_shapes=[
                pltpu.VMEM((2, 96, 1536), F32),
                pltpu.VMEM((96, 4608), F32),
                pltpu.VMEM((2, 48, 2048), F32),
            ],
        ),
        input_output_aliases={1 + len(flats) + i: i for i in range(len(tables))},
        compiler_params=pltpu.CompilerParams(vmem_limit_bytes=LIMIT),
        cost_estimate=pl.CostEstimate(flops=10**7, bytes_accessed=4 * 10**6, transcendentals=0),
        name="finish",
    )(ids, *flats, *tables)


def widen_kernel(v, out):
    out[...] = v[...].astype(F32)


def widen(v):
    rows, width = v.shape
    spec = pl.BlockSpec((BLOCK, width), lambda i: (i, 0))
    return pl.pallas_call(
        widen_kernel,
        out_shape=jax.ShapeDtypeStruct(v.shape, F32),
        grid=(rows // BLOCK,),
        in_specs=[spec],
        out_specs=spec,
        cost_estimate=pl.CostEstimate(flops=10**6, bytes_accessed=10**7, transcendentals=0),
        name="widen",
    )(v)


def other_core(z, c, y, x):
    return (z, 1 - c, y, x)


def other_half(z, c, y, x):
    return (z, c, y ^ 1, x)


def along_z(d):
    return lambda z, c, y, x: ((z + d) % 4, c, y, x)


def halves(value, index, move):
    count = value.shape[0] // 2
    mine = lax.dynamic_slice_in_dim(value, index * count, count, 0)
    theirs = lax.dynamic_slice_in_dim(value, (1 - index) * count, count, 0)
    return mine.astype(F32) + send(theirs, move).astype(F32)


def ring_scatter(value, index, moves, axis):
    count = value.shape[axis] // 4
    parts = [
        lax.dynamic_slice_in_dim(value, ((index - j) % 4) * count, count, axis) for j in range(4)
    ]
    return scatter4(parts, moves)


def sum_z(value):
    low = value.astype(BF)
    total = value
    for d in (1, 2, 3):
        total = total + send(low, along_z(d)).astype(F32)
    return total.astype(BF)


def blocks_of(v, rows):
    n, width = v.shape
    v = jnp.pad(v, ((0, rows - n), (0, -width % 128)))
    return jnp.concatenate([v[:, i : i + 128] for i in range(0, width, 128)], axis=0)


def reduce_shards(split):
    core, x, y = lax.axis_index("core"), lax.axis_index("x"), lax.axis_index("y")
    group = jnp.where(core == 0, y, x)
    shard = split.astype(BF).reshape(96, 4, 288).transpose(1, 0, 2)
    return ring_scatter(shard, group, ffn_shards, 0)[0]


def reduce_steps(mine, theirs):
    x, y = lax.axis_index("x"), lax.axis_index("y")
    part = mine + send(theirs, other_core).astype(F32)
    part = yield part
    split = jnp.concatenate([part[72:, i * 512 : i * 512 + 512] for i in range(3)], axis=0)
    whole = ring_scatter(part[:72].astype(BF), x, along_x, 1)
    whole, split = yield whole, split
    mix = jnp.concatenate([whole[48:], split], axis=1)
    pieces = []
    for q in range(4):
        here = jnp.where(y // 2 == q // 2, mix[(q % 2) * 12 : (q % 2) * 12 + 12], 0.0)
        pieces.append(jnp.concatenate([whole[q * 12 : q * 12 + 12], here], axis=1))
    part = ring_scatter(jnp.stack(pieces).astype(BF), y, along_y, 0)[0]
    yield blocks_of(part, 16)


def shards(
    tokens,
    cotangent,
    lengths,
    adapter_ids,
    mix_gain,
    ffn_gain,
    w_branch,
    input_weight,
    conv_weight,
    conv_bias,
    gate_a_weight,
    gate_a_bias,
    gate_i_weight,
    gate_i_bias,
    decay_param,
    w_out,
    w_gate,
    w_up,
    w_down,
    mix_down,
    mix_up,
    out_down,
    out_up,
    ffn_down,
    ffn_up,
    back_down,
    back_up,
):
    width = tokens.shape[2]
    z, core = lax.axis_index("z"), lax.axis_index("core")
    y, x = lax.axis_index("y"), lax.axis_index("x")
    seq, half = y // 2, y % 2
    out = lax.dynamic_slice(w_out, (0, core * 64, 0), (1, 64, width))[0]
    w_back = lax.all_gather(out, "y")
    w_back = [w_back, send(w_back, other_core)]
    ids = adapter_ids
    ffn_group = jnp.where(core == 0, y, x)
    first = (z + core + half == 0).astype(jnp.int32)
    scalars = jnp.stack([x, first, y, ffn_group, core]).astype(jnp.int32)
    turned = lambda v: jnp.swapaxes(v, -1, -2)
    mix_down_t = turned(mix_down)
    mix_up_f = mix_up.reshape(2, 8, 32, 128)
    *local, normed_0, lat_b_0, lat_i_0 = head(
        jnp.stack([y, ids[0], ids[1]]),
        tokens,
        mix_down_t,
        mix_up_f,
        mix_gain,
        w_branch,
        input_weight,
    )
    mine = local[0]
    local = deal4(local, along_y)
    ffn_parts = [turned(w_gate), turned(w_up), w_down]
    gather_ffn = lambda v: lax.all_gather(v, ALL, axis=0, axis_index_groups=shard_groups())
    picked, mine = tie(ids, mine)
    prepared = prepare(
        jnp.concatenate([picked, lax.dynamic_index_in_dim(picked, seq, 0)]),
        [mix_down_t, out_up],
        [
            turned(ffn_down), back_up, mix_up_f, turned(out_down),
            ffn_up.reshape(2, 8, 32, 288), turned(back_down),
        ],
        [gate_a_weight, gate_i_weight, conv_weight],
        [conv_bias, gate_a_bias, gate_i_bias, decay_param],
    )
    mix_d, out_u, ffn_d, back_u = (prepared[i : i + 2] for i in (0, 2, 4, 6))
    small, ffn_small = prepared[8:]
    more, mine = tie(ffn_parts, mine)
    ffn_parts.append(ffn_small)
    packed, local = tie(pack(0, more + [ffn_small]), local)
    ffn_w = [gather_ffn(packed), None]
    arranged = call(
        arrange_kernel,
        "arrange",
        gather4(small, along_y),
        [((4, 128, 256), BF), ((32, 512), BF), ((16, 512), BF), ((8, 512), F32)] * 2,
        [pltpu.VMEM((4, 2, 400, 128), BF)],
        scalars,
    )
    w_mix = {}
    start = (seq, half * BLOCK + x * HOME, 0)
    residual = lax.dynamic_slice(tokens, start, (1, HOME, width))[0]
    position = (z * 2 + core) * 512 + half * BLOCK + x * HOME + jnp.arange(HOME)
    valid = (position < lengths[seq]).astype(F32)[:, None]
    of_rows = jnp.where(core == 0, y, (y - jnp.arange(4)) % 4) // 2
    of_rows = jnp.repeat(of_rows, HOME)[:, None]
    of_cols = jnp.arange(32) // RANK
    mask = (of_rows == of_cols[None, :]).astype(F32)
    rows_like = [((HOME, width), BF)] * 4
    group_sem = pltpu.SemaphoreType.DMA((2, 4))
    ffn_sem = pltpu.SemaphoreType.DMA((3, 4))
    ffn_buffers = [pltpu.VMEM((1152, width), BF)] * 3
    mix_buffer = pltpu.VMEM((512, width), BF)
    half_f = ((BLOCK, 512), F32)
    pair_f = ((2, BLOCK, 512), F32)
    half_b = ((BLOCK, 512), BF)
    low_b = ((BLOCK, RANK), BF)

    kept = []
    for l in range(2):
        k = {"residual": residual}
        down, up_out = mix_d[l], out_u[l]
        gw, up, down_out, params = arranged[l * 4 : l * 4 + 4]
        if l == 0:
            normed, lat_b, lat_i = normed_0, lat_b_0, lat_i_0
            inputs, last, act, pull = call(
                unpack_kernel,
                "unpack",
                local,
                [half_b, ((16, 512), BF), half_f, half_f],
                [pltpu.VMEM((4, BLOCK, 256), BF)],
                scalars,
            )
            halo = send(last, next_block(False))
        else:
            blocks = gather4(normed_low, along_x)
            packed, _ = tie(packed, (mine, blocks))
            ffn_w[1] = gather_ffn(packed)
            w_mix[1] = [mine, send(mine, other_core)]
            normed, inputs, last, lat_b, lat_i = mixer(
                inputs_kernel,
                "inputs",
                [*blocks, down, up],
                [((BLOCK, width), BF), half_b, ((16, 512), BF), low_b, low_b],
                [mix_buffer, group_sem],
                scalars,
                w_mix[l],
            )
            halo = send(last, next_block(False))
            act, pull = mixer(
                branch_kernel,
                "branch",
                [normed, lat_b, up],
                [half_f, half_f],
                [mix_buffer, group_sem],
                scalars,
                w_mix[l],
            )
        saved, decay, scan, ends = call(
            gates_kernel,
            "gates",
            [inputs, halo, params, gw],
            [((3, BLOCK, 512), F32), half_f, pair_f, ((2, 512), F32)],
            [pltpu.VMEM((BLOCK + 16, 512), F32), pltpu.VMEM((BLOCK, 512), F32)],
            scalars,
        )
        carry = entering(ends, core, half, False)
        w_back_l = w_back if l == 0 else w_mix[1]
        states, mixed, out_latent, *parts = mixer(
            mixed_kernel,
            "mixed",
            [carry, scan, act, down_out, up_out],
            [half_f, half_b, low_b] + rows_like,
            [mix_buffer, pltpu.VMEM((BLOCK, width), BF), group_sem],
            scalars,
            w_back_l,
        )
        if l == 0:
            (halves_of, more), _ = tie(((w_branch, input_weight, w_out), ffn_parts), parts[0])
            mine, packed = half_of(scalars, 1, *halves_of), pack(1, more)
        parts = deal4(parts, along_x)
        if l == 1:
            parts, w_pair = tie(parts, pair_of(0, w_branch, input_weight))
        residual, normed_low = call(
            functools.partial(add_norm_kernel, l),
            "add_norm",
            [*parts, residual, ffn_gain],
            [((HOME, width), F32), ((HOME, width), BF)],
        )
        k.update(
            down=down, up=up, down_out=down_out, up_out=up_out, gw=gw, params=params,
            normed=normed, lat_b=lat_b, lat_i=lat_i, act=act, pull=pull, saved=saved, decay=decay, ends=ends,
            carry=carry, states=states, mixed=mixed, out_latent=out_latent,
            residual_one=residual,
        )
        if l == 1:
            grad = lax.dynamic_slice(cotangent, start, (1, HOME, width))[0] * valid
            grad_low, _ = tie(grad.astype(BF), carry)
            grad_blocks = gather4(grad_low, ffn_rows)
        blocks = gather4(normed_low, ffn_rows)
        if l == 0:
            mine, _ = tie(mine, (ffn_w[0], normed_low))
            mine = lax.all_gather(mine, "y")
        down, up_back = ffn_d[l], back_u[l]
        (ffn_a,) = call(
            join_kernel,
            "join",
            [],
            [((96, 1152), BF)],
            [
                pltpu.VMEM((4, 32, width), BF), pltpu.VMEM((96, 1152), F32),
                pltpu.SemaphoreType.DMA((4,)),
            ],

            far=[ffn_w[l]],
        )
        gate, ups = None, None
        if l == 0:
            gate, ups, hidden, latent, back_latent, *parts = call(
                ffn_kernel,
                "ffn",
                [*blocks, ffn_a, down, up_back, mask],
                [((BLOCK, 1152), F32)] * 2
                + [((BLOCK, 1152), BF), ((2, BLOCK, 32), BF), ((BLOCK, 32), BF)]
                + rows_like,
                [pltpu.VMEM((BLOCK, width), BF)] + ffn_buffers + [ffn_sem],
                far=[ffn_w[l]],
                mflops=2800,
                mbytes=15,
            )
        else:
            hidden, latent, back_latent, *turned_back = call(
                ffn_turn_kernel,
                "ffn_turn",
                [*blocks, *grad_blocks, ffn_a, down, up_back, mask],
                [((BLOCK, 1152), BF), ((2, BLOCK, 32), BF), ((BLOCK, 32), BF)]
                + [((BLOCK, 1152), BF)] * 2
                + [((BLOCK, 32), BF), ((2, BLOCK, 32), BF), ((BLOCK, width), BF)]
                + [((2 * HOME, width), BF)] * 4,
                [pltpu.VMEM((BLOCK, width), BF)] + ffn_buffers + [ffn_sem],
                far=[ffn_w[l]],
                mflops=5600,
                mbytes=15,
            )
            g_gate, g_up, g_back, g_latent, rows, *parts = turned_back
        k.update(
            ffn_a=ffn_a, down_two=down, up_back=up_back, blocks=blocks, gate=gate, ups=ups, hidden=hidden,
            latent=latent, back_latent=back_latent,
        )
        if l == 0:
            after, _ = tie(scalars, parts[0])
            parts, tables = tie(deal4(parts, ffn_rows), empty_tables(after))
            residual, normed_low = call(
                functools.partial(add_norm_kernel, 1),
                "add_norm",
                [*parts, residual, mix_gain],
                [((HOME, width), F32), ((HOME, width), BF)],
            )
        kept.append(k)
    for l in (1, 0):
        k = kept[l]
        w_back_l, w_in_l = (w_back, [w_in]) if l == 0 else (w_mix[1], w_mix[1])
        if l == 0:
            blocks = gather4(grad_low, ffn_rows)
            blocks, side = tie(blocks, side)
            side = steps.send(side)
            g_gate, g_up, g_back, g_latent, rows, *parts = call(
                ffn_back_kernel,
                "ffn_back",
                [*blocks, k["ffn_a"], k["down_two"], k["up_back"], mask, k["gate"], k["ups"]],
                [((BLOCK, 1152), BF)] * 2
                + [((BLOCK, 32), BF), ((2, BLOCK, 32), BF), ((BLOCK, width), BF)]
                + rows_like,
                ffn_buffers + [ffn_sem],
                far=[ffn_w[l]],
                mflops=2800,
                mbytes=15,
            )
        if l == 0:
            parts, side = tie(parts, side)
        parts = deal4(parts, ffn_rows)
        if l == 0:
            side, parts[1] = tie(side, parts[1])
            side = steps.send(side)
        ffn_whole, ffn_split = call(
            ffn_adapters_kernel,
            "ffn_adapters",
            [
                *k["blocks"], rows, k["latent"], k["back_latent"], k["hidden"], g_gate, g_up,
                g_back, g_latent,
            ],
            [((96, width), BF), ((96, 1152), BF)],
            [pltpu.VMEM((BLOCK, width), BF)],
            mflops=200,
        )
        parts, (ffn_whole, ffn_split) = tie(parts, (ffn_whole, ffn_split))
        out_parts = parts
        grad, grad_low = call(
            functools.partial(norm_back_kernel, l),
            "norm_back",
            [*parts, grad, k["residual_one"], ffn_gain],
            [((HOME, width), F32), ((HOME, width), BF)],
        )
        blocks = gather4(grad_low, along_x)
        if l == 1:
            (out_parts, shard_part), _ = tie((out_parts, ffn_split), grad_low)
            (output,) = call(
                output_kernel, "output", [*out_parts, residual, valid], [((HOME, width), BF)]
            )
            output = lax.all_gather(output, ("y", "x"), axis=0, tiled=True)
            shard_part = reduce_shards(shard_part)
        else:
            flat = jnp.concatenate([side[:48], shard_1, side[48:]], axis=0)
            flat, _ = tie(flat, grad_low)
            flat = sum_z(flat)
        rows, g_mixed, g_low, back, ends = mixer(
            states_back_kernel,
            "states_back",
            [*blocks, k["down_out"], k["up_out"], k["act"], k["decay"], k["ends"]],
            [((BLOCK, width), BF), half_b, low_b, pair_f, ((2, 512), F32)],
            [mix_buffer, pltpu.VMEM((BLOCK + 8, 512), F32), pltpu.VMEM((BLOCK, 512), F32)]
            + [group_sem],
            scalars,
            w_back_l,
        )
        if l == 1:
            ends, shard_part = tie(ends, shard_part)
        else:
            ends, (flat, output) = tie(ends, (flat, output))
            flat = lax.all_gather(flat, ("core", "y", "x")).reshape(2, 4, 4, 304, 128)
        if l == 1:
            w_pair, _ = tie(w_pair, ends)
            w_in = lax.all_gather(w_pair, "y")
        carry = entering(ends, core, half, True)
        part, g_up_out, g_down_out, g_up_b, g_low_b = mixer(
            branch_back_kernel,
            "branch_back",
            [
                rows, g_mixed, g_low, k["states"], k["pull"], k["mixed"], k["out_latent"],
                k["lat_b"], k["up"], k["down"],
            ],
            [((BLOCK, width), F32), ((RANK, width), F32), ((RANK, 512), F32), ((RANK, 512), F32)]
            + [low_b],
            [mix_buffer, group_sem],
            scalars,
            w_in_l,
        )
        carry, part = tie(carry, part)
        if l == 1:
            shard_part, _ = tie(shard_part, carry)
            shard_1 = halves(shard_part, core, other_core)

        g_conv, rim = call(
            gates_back_kernel,
            "gates_back",
            [
                carry, k["carry"], back, k["states"], k["saved"], k["decay"], k["params"],
                k["gw"],
            ],
            [half_f, ((8, 512), F32)],
            [pltpu.VMEM((BLOCK + 8, 512), F32)],
            scalars,
        )
        halo = send(rim, next_block(True))
        if l == 1:
            halo, shard_1 = tie(halo, shard_1)
            shard_1 = blocks_of(shard_1, 48)
        *parts, mine, theirs = mixer(
            inputs_back_kernel,
            "inputs_back",
            [
                g_conv, halo, k["params"], k["up"], k["down"], part, k["normed"], k["lat_i"],
                g_low_b, g_up_b, g_up_out, g_down_out, ffn_whole,
            ],
            rows_like + [((80, width), F32), ((80, width), BF)],
            [
                pltpu.VMEM((BLOCK + 8, 512), F32), mix_buffer, pltpu.VMEM((BLOCK, width), BF),
                pltpu.VMEM((48, width), F32), pltpu.VMEM((48, 512), F32),
                pltpu.VMEM((2, 80, width), F32), group_sem,
            ],
            scalars,
            w_in_l,
        )
        parts = deal4(parts, along_x)
        steps = reduce_steps(mine, theirs)
        side = next(steps)
        grad, grad_low = call(
            functools.partial(norm_back_kernel, l),
            "norm_back",
            [*parts, grad, k["residual"], mix_gain],
            [((HOME, width), F32), ((HOME, width), BF)],
        )
    grad_tokens = lax.all_gather(grad_low, ("y", "x"), axis=0, tiled=True)
    shard_0, _ = tie(ffn_split, grad_low)
    shard_0 = reduce_shards(shard_0)
    side, shard_0 = tie(steps.send(side), shard_0)
    shard_0 = blocks_of(halves(shard_0, core, other_core), 48)
    side = steps.send(side)
    last = jnp.concatenate([side[:48], shard_0, side[48:]], axis=0)
    last = sum_z(last)
    last, (tables, output) = tie(last, (finish(ids, 1, [flat], tables), widen(output)))
    last = lax.all_to_all(jnp.broadcast_to(last, (16, 304, 128)), ("y", "x"), 0, 0, tiled=True)
    grad_tokens, _ = tie(grad_tokens, last)
    other, grad_tokens = tie(send(last, other_core), widen(grad_tokens))
    last = last, other
    ids = jnp.concatenate([ids, core[None].astype(jnp.int32)])
    gmd, gmu, god, gou, gfd, gfu, gbd, gbu = finish(ids, 0, last, tables)
    return (
        output.reshape(tokens.shape),
        grad_tokens.reshape(tokens.shape),
        turned(gmd),
        gmu.reshape(2, 8, 2, RANK, 2048),
        turned(god),
        gou,
        turned(gfd),
        gfu.reshape(2, 8, 2, RANK, 4608),
        turned(gbd),
        gbu,
    )


def solution(mesh):
    grid = Mesh(mesh.devices.reshape(4, 2, 4, 4), ALL)
    sp, mp = ("z", "core"), ("y", "x")
    in_specs = (
        P(None, sp, None),
        P(None, sp, None),
        P(),
        P(),
        P(),
        P(),
        P(None, None, mp),
        P(None, None, mp),
        P(None, None, mp),
        P(None, mp),
        P(None, mp, None, None),
        P(None, mp),
        P(None, mp, None, None),
        P(None, mp),
        P(None, mp),
        P(None, mp, None),
        P(None, None, mp),
        P(None, None, mp),
        P(None, mp, None),
        P(),
        P(None, None, None, None, mp),
        P(None, None, mp, None),
        P(),
        P(),
        P(None, None, None, None, mp),
        P(None, None, mp, None),
        P(),
    )
    out_specs = (P(None, sp, None), P(None, sp, None)) + (P(),) * 8
    return jax.shard_map(shards, mesh=grid, in_specs=in_specs, out_specs=out_specs, check_vma=False)
```

```python
import functools

import jax
import jax.numpy as jnp
from jax import lax
from jax.experimental import pallas as pl
from jax.experimental.pallas import tpu as pltpu
from jax.sharding import Mesh
from jax.sharding import PartitionSpec as P

ALL = ("z", "core", "y", "x")
BF = jnp.bfloat16
F32 = jnp.float32
RANK = 16
HOME = 64
BLOCK = 256
LIMIT = 60 * 2**20
LARGE = 60 * 2**20
GELU_C = 0.7978845608028654


def device_pairs(move):
    pairs = []
    for z in range(4):
        for c in range(2):
            for y in range(4):
                for x in range(4):
                    to = move(z, c, y, x)
                    if to is not None:
                        a = ((z * 2 + c) * 4 + y) * 4 + x
                        b = ((to[0] * 2 + to[1]) * 4 + to[2]) * 4 + to[3]
                        pairs.append((a, b))
    return pairs


def send(value, move):
    return lax.ppermute(value, ALL, device_pairs(move))


def along_x(d):
    return lambda z, c, y, x: (z, c, y, (x + d) % 4)


def along_y(d):
    return lambda z, c, y, x: (z, c, (y + d) % 4, x)


def ffn_rows(d):
    return lambda z, c, y, x: (z, c, y, (x + d) % 4) if c == 0 else (z, c, (y + d) % 4, x)


def ffn_shards(d):
    return lambda z, c, y, x: (z, c, (y + d) % 4, x) if c == 0 else (z, c, y, (x + d) % 4)


def shard_groups():
    at = lambda z, c, y, x: ((z * 2 + c) * 4 + y) * 4 + x
    columns = [[at(z, 0, y, x) for y in range(4)] for z in range(4) for x in range(4)]
    rows = [[at(z, 1, y, x) for x in range(4)] for z in range(4) for y in range(4)]
    return columns + rows


def gather4(value, moves):
    return [value] + [send(value, moves(j)) for j in (1, 2, 3)]


def deal4(parts, moves):
    return [parts[0]] + [send(parts[j], moves(-j)) for j in (1, 2, 3)]


def scatter4(parts, moves):
    moved = deal4(parts, moves)[1:]
    total = parts[0].astype(F32)
    for part in moved:
        total = total + part.astype(F32)
    return total


def split3(v):
    high = v.astype(BF)
    rest = v - high.astype(F32)
    mid = rest.astype(BF)
    return high, mid, (rest - mid.astype(F32)).astype(BF)


def tie(first, second):
    return lax.optimization_barrier((first, second))


def combine(earlier, later):
    return (earlier[0] * later[0], later[0] * earlier[1] + later[1])


def next_block(reverse):
    def move(z, c, y, x):
        at = (z * 2 + c) * 2 + y % 2 + (-1 if reverse else 1)
        if not 0 <= at < 16:
            return None
        return (at // 4, (at // 2) % 2, (y // 2) * 2 + at % 2, x)

    return move


def entering(own, core, half, reverse):
    one = jnp.stack([jnp.ones_like(own[0]), jnp.zeros_like(own[0])])

    def step(own, other, later):
        pre = jnp.where(later, other, one)
        first, second = jnp.where(later, other, own), jnp.where(later, own, other)
        both = combine((first[0], first[1]), (second[0], second[1]))
        return pre, jnp.stack(both)

    other = send(own, lambda z, c, y, x: (z, c, y ^ 1, x))
    pre_h, own = step(own, other, half == (0 if reverse else 1))
    other = send(own, lambda z, c, y, x: (z, 1 - c, y, x))
    pre_c, own = step(own, other, core == (0 if reverse else 1))
    far = []
    for d in (1, 2, 3):
        e = -d if reverse else d
        far.append(
            send(own, lambda z, c, y, x, e=e: (z + e, c, y, x) if 0 <= z + e < 4 else None)
        )
    state = far[2][1]
    for part in (far[1], far[0], pre_c, pre_h):
        state = part[0] * state + part[1]
    return state[None]


def nn(a, b):
    return jnp.dot(a, b, preferred_element_type=F32)


def nt(a, b):
    return lax.dot_general(a, b, (((1,), (1,)), ((), ())), preferred_element_type=F32)


def tn(a, b):
    return lax.dot_general(a, b, (((0,), (0,)), ((), ())), preferred_element_type=F32)


def gelu_pair(v):
    t = jnp.tanh(GELU_C * (v + 0.044715 * v * v * v))
    act = 0.5 * v * (1.0 + t)
    pull = 0.5 * (1.0 + t) + 0.5 * v * (1.0 - t * t) * (GELU_C * (1.0 + 0.134145 * v * v))
    return act, pull


def inverse_rms(v):
    return lax.rsqrt(jnp.mean(v * v, axis=-1, keepdims=True) + 1e-06)


def rms_backward(v, inverse, gain, grad):
    scaled = grad * gain
    return inverse * scaled - v * inverse**3 * jnp.mean(v * scaled, axis=-1, keepdims=True)


VMEM = pl.BlockSpec(memory_space=pltpu.VMEM)
SMEM = pl.BlockSpec(memory_space=pltpu.SMEM)
HBM = pl.BlockSpec(memory_space=pl.ANY)


def grouped(kernel, n_in, n_far):
    def run(sc, *refs):
        kernel(sc, refs[n_in : n_in + n_far], *refs[:n_in], *refs[n_in + n_far :])

    return run


def mixer(kernel, name, ins, outs, scratch, scalars, far):
    return call(
        grouped(kernel, len(ins), len(far)), name, ins, outs, scratch, scalars, far, mflops=420
    )


def call(kernel, name, ins, outs, scratch=(), scalars=None, far=(), mflops=100, mbytes=4):
    specs = [VMEM] * len(ins) + [HBM] * len(far)
    arrays = list(ins) + list(far)
    if scalars is not None:
        specs, arrays = [SMEM] + specs, [scalars] + arrays
    return pl.pallas_call(
        kernel,
        out_shape=[jax.ShapeDtypeStruct(shape, dtype) for shape, dtype in outs],
        in_specs=specs,
        out_specs=[VMEM] * len(outs),
        scratch_shapes=list(scratch),
        compiler_params=pltpu.CompilerParams(
            vmem_limit_bytes=LARGE if mflops > 1000 else LIMIT
        ),
        cost_estimate=pl.CostEstimate(
            flops=mflops * 10**6, bytes_accessed=mbytes * 10**6, transcendentals=0
        ),
        name=name,
    )(*arrays)


def fetch(source, rows, target, sem):
    first, count = rows
    copies = []
    for j in range(4):
        copy = pltpu.make_async_copy(
            source.at[j, pl.ds(first, count)],
            target.at[pl.ds(j * count, count)],
            sem.at[j],
        )
        copy.start()
        copies.append(copy)
    return copies


def fetch_half(sc, mine, other, rows, target, sem):
    first, count = rows
    pieces = []
    for half in range(2):
        low, high = max(first, half * 192), min(first + count, half * 192 + 192)
        if low < high:
            pieces.append((half, low - half * 192, high - low, low - first))
    copies = []
    for core in range(2):

        @pl.when(sc[4] == core)
        def _():
            for i, (half, low, size, at) in enumerate(pieces):
                source = mine if half == core else other
                for j in range(4):
                    pltpu.make_async_copy(
                        source.at[j, pl.ds(low, size)],
                        target.at[pl.ds(j * count + at, size)],
                        sem.at[i, j],
                    ).start()

    for i, (half, low, size, at) in enumerate(pieces):
        for j in range(4):
            copies.append(
                pltpu.make_async_copy(
                    mine.at[j, pl.ds(low, size)],
                    target.at[pl.ds(j * count + at, size)],
                    sem.at[i, j],
                )
            )
    return copies


def weights(sc, w, rows, target, sem):
    if len(w) == 2 and w[0].shape[1] == 192:
        return fetch_half(sc, *w, rows, target, sem)
    if len(w) == 2:
        copies = []
        for i, source in enumerate(w):
            half = sc[4] if i == 0 else 1 - sc[4]
            for j in range(4):
                at = pl.multiple_of(j * 128 + half * 64, 64)
                copy = pltpu.make_async_copy(
                    source.at[j], target.at[pl.ds(at, 64)], sem.at[i, j]
                )
                copy.start()
                copies.append(copy)
        return copies
    return fetch(w[0], (rows[0] % w[0].shape[1], rows[1]), target, sem.at[0])


def wait_all(copies):
    for copy in copies:
        copy.wait()


def place(scalars, blocks, rows_ref):
    for j in range(4):
        at = pl.multiple_of(lax.rem(scalars[0] + 4 - j, 4) * HOME, HOME)
        rows_ref[pl.ds(at, HOME), :] = blocks[j][...]


def take(scalars, total_ref, parts):
    for j in range(4):
        at = pl.multiple_of(lax.rem(scalars[0] + 4 - j, 4) * HOME, HOME)
        parts[j][...] = total_ref[pl.ds(at, HOME), :]


def scan_rows(reverse, a_ref, b_ref, cum_ref, out_ref):
    rows, width = a_ref.shape
    row = lax.broadcasted_iota(jnp.int32, (8, width), 0)
    groups = rows // 8

    def body(i, carry):
        ca, cb = carry
        at = pl.multiple_of((groups - 1 - i if reverse else i) * 8, 8)
        a, b = a_ref[pl.ds(at, 8), :], b_ref[pl.ds(at, 8), :]
        for k in (1, 2, 4):
            seen = row < 8 - k if reverse else row >= k
            by = 8 - k if reverse else k
            pa = jnp.where(seen, pltpu.roll(a, by, 0), 1.0)
            pb = jnp.where(seen, pltpu.roll(b, by, 0), 0.0)
            b = a * pb + b
            a = a * pa
        b = a * cb + b
        a = a * ca
        cum_ref[pl.ds(at, 8), :] = a
        out_ref[pl.ds(at, 8), :] = b
        last = 0 if reverse else 7
        return (
            jnp.broadcast_to(a[last : last + 1], a.shape),
            jnp.broadcast_to(b[last : last + 1], b.shape),
        )

    start = (jnp.ones((8, width), F32), jnp.zeros((8, width), F32))
    lax.fori_loop(0, groups, body, start, unroll=4)


def add_norm_kernel(l, p0, p1, p2, p3, residual, gain, out, normed):
    total = p0[...].astype(F32) + p1[...].astype(F32) + p2[...].astype(F32)
    v = residual[...] + total + p3[...].astype(F32)
    out[...] = v
    normed[...] = (v * inverse_rms(v) * gain[l : l + 1]).astype(BF)


def output_kernel(p0, p1, p2, p3, residual, valid, out):
    total = p0[HOME:].astype(F32) + p1[HOME:].astype(F32) + p2[HOME:].astype(F32)
    out[...] = ((residual[...] + total + p3[HOME:].astype(F32)) * valid[...]).astype(BF)


def norm_back_kernel(l, p0, p1, p2, p3, grad, v_ref, gain, out, low):
    total = p0[:HOME].astype(F32) + p1[:HOME].astype(F32) + p2[:HOME].astype(F32)
    total = total + p3[:HOME].astype(F32)
    v = v_ref[...]
    g = grad[...] + rms_backward(v, inverse_rms(v), gain[l : l + 1], total)
    out[...] = g
    low[...] = g.astype(BF)


def inputs_kernel(
    sc, w, n0, n1, n2, n3, down, up, normed, inputs, last, lat_b, lat_i, wi, sem
):
    copies = weights(sc, w, (128, 128), wi, sem)
    place(sc, (n0, n1, n2, n3), normed)
    rows = normed[...]
    lat_b[...] = nt(rows, down[:RANK]).astype(BF)
    low = nt(rows, down[RANK:]).astype(BF)
    lat_i[...] = low
    wait_all(copies)
    inputs[...] = (nt(rows, wi[...]) + nn(low, up[RANK:])).astype(BF)
    last[...] = inputs[BLOCK - 16 :]


def branch_kernel(sc, w, normed, lat_b, up, act, pull, wb, sem):
    copies = weights(sc, w, (0, 128), wb, sem)
    wait_all(copies)
    branch = nt(normed[...], wb[...]) + nn(lat_b[...], up[:RANK])
    act[...], pull[...] = gelu_pair(branch)


def gates_kernel(
    sc, inputs, halo, params, gw, saved, decay, scan, ends, ext, driven
):
    conv, gate_a, gate_i = (saved.at[i] for i in range(3))
    cum, local = scan.at[0], scan.at[1]
    ext[:16] = halo[...].astype(F32)
    ext[16:] = inputs[...].astype(F32)
    value = params[4:5] + params[0:1] * ext[pl.ds(16, BLOCK)]
    for o in (1, 2, 3):
        value = value + params[o : o + 1] * ext[pl.ds(16 - o, BLOCK)]
    conv[...] = value
    row = lax.broadcasted_iota(jnp.int32, (BLOCK, 128), 0)
    first = (row == 0) & (sc[1] == 1)
    for h in range(4):
        at = slice(h * 128, h * 128 + 128)
        c = conv[:, at]
        pre = nn(c.astype(BF), gw[h])
        a = jax.nn.sigmoid(pre[:, :128] + params[5:6, at])
        i = jax.nn.sigmoid(pre[:, 128:] + params[6:7, at])
        d = jnp.exp(a * params[7:8, at])
        gate_a[:, at] = a
        gate_i[:, at] = i
        decay[:, at] = d
        driven[:, at] = c * i * jnp.where(first, 1.0, jnp.sqrt(1.0 - d * d + 0.01))
    scan_rows(False, decay, driven, cum, local)
    ends[0:1] = cum[BLOCK - 1 :]
    ends[1:2] = local[BLOCK - 1 :]


def mixed_kernel(
    sc, w, carry, scan, act, down_out, up_out, states, mixed, out_latent, q0, q1, q2, q3,
    wo, total, sem,
):
    copies = weights(sc, w, (256, 128), wo, sem)
    s = scan[1] + scan[0] * carry[...]
    states[...] = s
    m = (s * act[...]).astype(BF)
    mixed[...] = m
    low = nt(m, down_out[...]).astype(BF)
    out_latent[...] = low
    wait_all(copies)
    total[...] = (nn(m, wo[...]) + nn(low, up_out[...])).astype(BF)
    take(sc, total, (q0, q1, q2, q3))


def ffn_kernel(
    n0, n1, n2, n3, a, down, up_back, mask, w, gate, up, hidden, latent, back_latent,
    q0, q1, q2, q3, rows_ref, wg, wu, wd, sem,
):
    cg = fetch(w, (0, 288), wg, sem.at[0])
    cu = fetch(w, (288, 288), wu, sem.at[1])
    cd = fetch(w, (576, 288), wd, sem.at[2])
    for j, n in enumerate((n0, n1, n2, n3)):
        rows_ref[j * HOME : (j + 1) * HOME] = n[...]
    rows = rows_ref[...]
    lat_g = (nt(rows, down[:32]) * mask[...]).astype(BF)
    lat_u = (nt(rows, down[32:]) * mask[...]).astype(BF)
    latent[0] = lat_g
    latent[1] = lat_u
    wait_all(cg)
    g = nt(rows, wg[...]) + nn(lat_g, a[:32])
    gate[...] = g
    wait_all(cu)
    u = nt(rows, wu[...]) + nn(lat_u, a[32:64])
    up[...] = u
    hidden[...] = (gelu_pair(g)[0] * u).astype(BF)
    h = hidden[...]
    low = (nt(h, a[64:]) * mask[...]).astype(BF)
    back_latent[...] = low
    wait_all(cd)
    total = (nn(h, wd[...]) + nn(low, up_back[...])).astype(BF)
    for j, q in enumerate((q0, q1, q2, q3)):
        q[...] = total[j * HOME : (j + 1) * HOME]


def ffn_back_kernel(
    r0, r1, r2, r3, a, down, up_back, mask, gate, up, w, g_gate, g_up, g_back, g_latent, rows_ref,
    q0, q1, q2, q3, wg, wu, wd, sem,
):
    cd = fetch(w, (576, 288), wd, sem.at[2])
    cg = fetch(w, (0, 288), wg, sem.at[0])
    cu = fetch(w, (288, 288), wu, sem.at[1])
    for j, r in enumerate((r0, r1, r2, r3)):
        rows_ref[j * HOME : (j + 1) * HOME] = r[...]
    rows = rows_ref[...]
    low = (nt(rows, up_back[...]) * mask[...]).astype(BF)
    g_back[...] = low
    wait_all(cd)
    gh = (nt(rows, wd[...]) + nn(low, a[64:])).astype(BF).astype(F32)
    act, pull = gelu_pair(gate[...])
    g_up[...] = (gh * act).astype(BF)
    g_gate[...] = (gh * up[...] * pull).astype(BF)
    gg, gu = g_gate[...], g_up[...]
    lat_g = (nt(gg, a[:32]) * mask[...]).astype(BF)
    lat_u = (nt(gu, a[32:64]) * mask[...]).astype(BF)
    g_latent[0] = lat_g
    g_latent[1] = lat_u
    wait_all(cg)
    total = nn(gg, wg[...]) + nn(lat_g, down[:32]) + nn(lat_u, down[32:])
    wait_all(cu)
    total = (total + nn(gu, wu[...])).astype(BF)
    for j, q in enumerate((q0, q1, q2, q3)):
        q[...] = total[j * HOME : (j + 1) * HOME]


def ffn_turn_kernel(
    n0, n1, n2, n3, r0, r1, r2, r3, a, down, up_back, mask, w,
    hidden, latent, back_latent, g_gate, g_up, g_back, g_latent, rows_ref,
    q0, q1, q2, q3, normed_ref, wg, wu, wd, sem,
):
    cg = fetch(w, (0, 288), wg, sem.at[0])
    cu = fetch(w, (288, 288), wu, sem.at[1])
    cd = fetch(w, (576, 288), wd, sem.at[2])
    for j, (n, r) in enumerate(((n0, r0), (n1, r1), (n2, r2), (n3, r3))):
        normed_ref[j * HOME : (j + 1) * HOME] = n[...]
        rows_ref[j * HOME : (j + 1) * HOME] = r[...]
    normed, rows = normed_ref[...], rows_ref[...]
    lat_g = (nt(normed, down[:32]) * mask[...]).astype(BF)
    lat_u = (nt(normed, down[32:]) * mask[...]).astype(BF)
    latent[0] = lat_g
    latent[1] = lat_u
    low = (nt(rows, up_back[...]) * mask[...]).astype(BF)
    g_back[...] = low
    wait_all(cg)
    g = nt(normed, wg[...]) + nn(lat_g, a[:32])
    wait_all(cu)
    u = nt(normed, wu[...]) + nn(lat_u, a[32:64])
    act, pull = gelu_pair(g)
    hidden[...] = (act * u).astype(BF)
    wait_all(cd)
    gh = (nt(rows, wd[...]) + nn(low, a[64:])).astype(BF).astype(F32)
    g_up[...] = (gh * act).astype(BF)
    g_gate[...] = (gh * u * pull).astype(BF)
    gg, gu = g_gate[...], g_up[...]
    lat_g = (nt(gg, a[:32]) * mask[...]).astype(BF)
    lat_u = (nt(gu, a[32:64]) * mask[...]).astype(BF)
    g_latent[0] = lat_g
    g_latent[1] = lat_u
    total = nn(gg, wg[...]) + nn(lat_g, down[:32]) + nn(lat_u, down[32:])
    total = (total + nn(gu, wu[...])).astype(BF)
    for j, q in enumerate((q0, q1, q2, q3)):
        q[:HOME] = total[j * HOME : (j + 1) * HOME]
    h = hidden[...]
    low = (nt(h, a[64:]) * mask[...]).astype(BF)
    back_latent[...] = low
    total = (nn(h, wd[...]) + nn(low, up_back[...])).astype(BF)
    for j, q in enumerate((q0, q1, q2, q3)):
        q[HOME:] = total[j * HOME : (j + 1) * HOME]


def ffn_adapters_kernel(
    n0, n1, n2, n3, rows, latent, back_latent, hidden, g_gate, g_up, g_back, g_latent,
    whole, split, normed_ref,
):
    for j, n in enumerate((n0, n1, n2, n3)):
        normed_ref[j * HOME : (j + 1) * HOME] = n[...]
    normed = normed_ref[...]
    g_down = [tn(g_latent[0], normed), tn(g_latent[1], normed)]
    g_up_back = tn(back_latent[...], rows[...])
    for s in range(2):
        at = slice(s * RANK, s * RANK + RANK)
        whole[s * 48 : s * 48 + 16] = g_down[0][at].astype(BF)
        whole[s * 48 + 16 : s * 48 + 32] = g_down[1][at].astype(BF)
        whole[s * 48 + 32 : s * 48 + 48] = g_up_back[at].astype(BF)
    split[:32] = tn(latent[0], g_gate[...]).astype(BF)
    split[32:64] = tn(latent[1], g_up[...]).astype(BF)
    split[64:] = tn(g_back[...], hidden[...]).astype(BF)


def states_back_kernel(
    sc, w, r0, r1, r2, r3, down_out, up_out, act, decay, forward_ends,
    rows_ref, g_mixed, g_low, back, ends, wo, ext, g_states, sem,
):
    suffix, local = back.at[0], back.at[1]
    copies = weights(sc, w, (256, 128), wo, sem)
    place(sc, (r0, r1, r2, r3), rows_ref)
    rows = rows_ref[...]
    low = nt(rows, up_out[...]).astype(BF)
    g_low[...] = low
    ext[:BLOCK] = decay[...]
    ext[BLOCK:] = jnp.ones((8, 512), F32)
    ext[:BLOCK] = ext[pl.ds(1, BLOCK)]
    wait_all(copies)
    gm = (nt(rows, wo[...]) + nn(low, down_out[...])).astype(BF)
    g_mixed[...] = gm
    g_states[...] = gm.astype(F32) * act[...]
    scan_rows(True, ext.at[pl.ds(0, BLOCK)], g_states, suffix, local)
    ends[0:1] = forward_ends[0:1]
    ends[1:2] = decay[0:1] * local[0:1]


def branch_back_kernel(
    sc, w, rows, g_mixed, g_low, states, pull, mixed, out_latent, lat_b, up, down,
    part, g_up_out, g_down_out, g_up_b, g_branch_low, wb, sem,
):
    copies = weights(sc, w, (0, 128), wb, sem)
    gb = (g_mixed[...].astype(F32) * states[...] * pull[...]).astype(BF)
    low = nt(gb, up[:RANK]).astype(BF)
    g_branch_low[...] = low
    g_up_out[...] = tn(out_latent[...], rows[...])
    g_down_out[...] = tn(g_low[...], mixed[...])
    g_up_b[...] = tn(lat_b[...], gb)
    wait_all(copies)
    part[...] = nn(gb, wb[...]) + nn(low, down[:RANK])


def gates_back_kernel(
    sc, carry, carry_in, back, states, saved, decay, params, gw, g_conv, rim, ext
):
    conv, gate_a, gate_i = (saved.at[i] for i in range(3))
    suffix, local = back.at[0], back.at[1]
    ext[:8] = jnp.broadcast_to(carry_in[...], (8, 512))
    ext[8:] = states[...]
    row = lax.broadcasted_iota(jnp.int32, (BLOCK, 128), 0)
    first = (row == 0) & (sc[1] == 1)
    for h in range(4):
        at = slice(h * 128, h * 128 + 128)
        gd = local[:, at] + suffix[:, at] * carry[:, at]
        d, i, a, c = decay[:, at], gate_i[:, at], gate_a[:, at], conv[:, at]
        scale = jnp.where(first, 1.0, jnp.sqrt(1.0 - d * d + 0.01))
        g_scale = gd * c * i
        previous = ext[pl.ds(7, BLOCK), at]
        g_decay = gd * previous - jnp.where(first, 0.0, g_scale * (d / scale))
        ga = (g_decay * d * params[7:8, at] * a * (1.0 - a)).astype(BF)
        gi = (g_scale * scale * (1.0 - i)).astype(BF)
        g_conv[:, at] = gd * i * scale + nt(ga, gw[h, :, :128]) + nt(gi, gw[h, :, 128:])
    rim[...] = g_conv[:8]


def inputs_back_kernel(
    sc, w, g_conv, halo, params, up, down, part, normed, lat_i, g_low_b, g_up_b, g_up_out,
    g_down_out, ffn_whole, q0, q1, q2, q3, mine, theirs, ext, wi, total, whole, split, wide, sem,
):
    copies = weights(sc, w, (128, 128), wi, sem)
    ext[:BLOCK] = g_conv[...]
    ext[BLOCK:] = halo[...]
    value = params[0:1] * ext[:BLOCK]
    for o in (1, 2, 3):
        value = value + params[o : o + 1] * ext[pl.ds(o, BLOCK)]
    gi = value.astype(BF)
    low = nt(gi, up[RANK:]).astype(BF)
    whole[:RANK] = tn(g_low_b[...], normed[...])
    whole[RANK:32] = tn(low, normed[...])
    whole[32:] = g_up_out[...]
    split[:RANK] = g_up_b[...]
    split[RANK:32] = tn(lat_i[...], gi)
    split[32:] = g_down_out[...]
    for c in range(2):
        wide[c, :48] = ffn_whole[c * 48 : c * 48 + 48].astype(F32)
        wide[c, 48:72] = whole[c * 24 : c * 24 + 24]
        for i in range(3):
            at = c * 24 + i * 8
            wide[c, 72:, i * 512 : i * 512 + 512] = split[at : at + 8]
    mine[...] = wide[sc[4]]
    theirs[...] = wide[1 - sc[4]].astype(BF)
    wait_all(copies)
    total[...] = (part[...] + nn(gi, wi[...]) + nn(low, down[RANK:])).astype(BF)
    take(sc, total, (q0, q1, q2, q3))


def head_kernel(
    sc, tokens, down, up, gain, wb, wi, o0, o1, o2, o3, normed, lat_b, lat_i, w
):
    j = pl.program_id(0)

    @pl.when(j == 0)
    def _():
        w[:, :128] = wb[0]
        w[:, 128:] = wi[0]

    v = tokens[0]
    rows = (v * inverse_rms(v) * gain[0:1]).astype(BF)
    low_b = nt(rows, down[0, 0, :RANK]).astype(BF)
    low_i = nt(rows, down[0, 0, RANK:]).astype(BF)
    both = nn(rows, w[...])
    branch = (both[:, :128] + nn(low_b, up[0, 0, :RANK])).astype(BF)
    inputs = (both[:, 128:] + nn(low_i, up[0, 0, RANK:])).astype(BF)
    for i, out in enumerate((o0, o1, o2, o3)):

        @pl.when(j == i)
        def _():
            out[:, :128] = branch
            out[:, 128:] = inputs

    @pl.when(j == 0)
    def _():
        normed[...] = rows
        lat_b[...] = low_b
        lat_i[...] = low_i


def head(scalars, tokens, down, up, gain, wb, wi):
    at = lambda j, sc: lax.rem(sc[0] + 4 - j, 4)
    own = lambda j, sc: (0, sc[1 + at(j, sc) // 2], 0, 0)
    fixed = lambda j, sc: (0, 0)
    block = ((BLOCK, 256), BF)
    outs = [block] * 4 + [((BLOCK, 1536), BF), ((BLOCK, RANK), BF), ((BLOCK, RANK), BF)]
    return pl.pallas_call(
        head_kernel,
        out_shape=[jax.ShapeDtypeStruct(shape, dtype) for shape, dtype in outs],
        grid_spec=pltpu.PrefetchScalarGridSpec(
            num_scalar_prefetch=1,
            grid=(4,),
            in_specs=[
                pl.BlockSpec((1, BLOCK, 1536), lambda j, sc: (at(j, sc) // 2, at(j, sc) % 2, 0)),
                pl.BlockSpec((1, 1, 32, 1536), own),
                pl.BlockSpec((1, 1, 32, 128), own),
                pl.BlockSpec((2, 1536), fixed),
                pl.BlockSpec((1, 1536, 128), lambda j, sc: (0, 0, 0)),
                pl.BlockSpec((1, 1536, 128), lambda j, sc: (0, 0, 0)),
            ],
            out_specs=[pl.BlockSpec(shape, fixed) for shape, _ in outs],
            scratch_shapes=[pltpu.VMEM((1536, 256), BF)],
        ),
        compiler_params=pltpu.CompilerParams(vmem_limit_bytes=LIMIT),
        cost_estimate=pl.CostEstimate(
            flops=900 * 10**6, bytes_accessed=9 * 10**6, transcendentals=0
        ),
        name="head",
    )(scalars, tokens, down, up, gain, wb, wi)


def prepare_kernel(
    sc, md, ou, fd0, fd1, bu0, bu1, mu0, mu1, od0, od1, fu0, fu1, bd0, bd1,
    ga, gi, cw, cb, ab, ib, dp, mix_d0, mix_d1, out_u0, out_u1, ffn_d0, ffn_d1, back_u0, back_u1,
    small, ffn_small,
):
    l = pl.program_id(0)
    for i, (mix_d, out_u, ffn_d, back_u) in enumerate(
        ((mix_d0, out_u0, ffn_d0, back_u0), (mix_d1, out_u1, ffn_d1, back_u1))
    ):

        @pl.when(l == i)
        def _():
            mix_d[...] = md[0, 0]
            out_u[...] = ou[0, 0]
            for s, (fd, bu) in enumerate(((fd0, bu0), (fd1, bu1))):
                ffn_d[s * 16 : s * 16 + 16] = fd[0, 0, :16]
                ffn_d[32 + s * 16 : 48 + s * 16] = fd[0, 0, 16:]
                back_u[s * 16 : s * 16 + 16] = bu[0, 0]

    ffn_small[...] = jnp.zeros(ffn_small.shape, BF)
    small[0, :128] = ga[0, 0]
    small[0, 128:256] = gi[0, 0]
    for s, (mu, od, fu, bd) in enumerate(((mu0, od0, fu0, bd0), (mu1, od1, fu1, bd1))):
        small[0, 256 + s * 32 : 288 + s * 32] = mu[0, 0]
        small[0, 320 + s * 16 : 336 + s * 16] = od[0, 0]
        at = slice(s * 16, s * 16 + 16)
        ffn_small[0, at, :288] = fu[0, 0, :16]
        ffn_small[0, at, 384:672] = fu[0, 0, 16:]
        ffn_small[0, at, 768:1056] = bd[0, 0]
    vectors = [ref[pl.ds(l, 1), :] for ref in (cb, ab, ib, dp)]
    wide = jnp.concatenate([cw[0]] + vectors + [jnp.zeros((8, 128), F32)], axis=0)
    for i, part in enumerate(split3(wide)):
        small[0, 352 + 16 * i : 368 + 16 * i] = part


def prepare(picks, owned, tables, singles, vectors):
    specs, arrays = [], []
    for table, which in [(t, (2,)) for t in owned] + [(t, (0, 1)) for t in tables]:
        for s in which:
            specs.append(
                pl.BlockSpec((1, 1) + table.shape[2:], lambda l, sc, s=s: (l, sc[s], 0, 0))
            )
            arrays.append(table)
    for single in singles:
        dims = single.ndim - 1
        specs.append(
            pl.BlockSpec((1,) + single.shape[1:], lambda l, sc, dims=dims: (l,) + (0,) * dims)
        )
        arrays.append(single)
    for vector in vectors:
        specs.append(pl.BlockSpec(vector.shape, lambda l, sc: (0, 0)))
        arrays.append(vector)
    flat = [(32, 1536), (16, 1536), (64, 1536), (32, 1536)]
    flat = [shape for shape in flat for _ in range(2)]
    tall = [(400, 128), (32, 1536)]
    return pl.pallas_call(
        prepare_kernel,
        out_shape=[jax.ShapeDtypeStruct(shape, BF) for shape in flat]
        + [jax.ShapeDtypeStruct((2,) + shape, BF) for shape in tall],
        grid_spec=pltpu.PrefetchScalarGridSpec(
            num_scalar_prefetch=1,
            grid=(2,),
            in_specs=specs,
            out_specs=[pl.BlockSpec(shape, lambda l, sc: (0, 0)) for shape in flat]
            + [pl.BlockSpec((1,) + shape, lambda l, sc: (l, 0, 0)) for shape in tall],
        ),
        compiler_params=pltpu.CompilerParams(vmem_limit_bytes=LIMIT),
        cost_estimate=pl.CostEstimate(flops=10**6, bytes_accessed=4 * 10**6, transcendentals=0),
        name="prepare",
    )(picks, *arrays)


def arrange_kernel(sc, s0, s1, s2, s3, *refs):
    small = refs[-1]
    for j, block in enumerate((s0, s1, s2, s3)):
        small[lax.rem(sc[2] + 4 - j, 4)] = block[...]
    seq = sc[2] // 2
    for l in range(2):
        gw, up, down_out, params = refs[l * 4 : l * 4 + 4]
        for p in range(4):
            at = slice(p * 128, p * 128 + 128)
            gw[p, :, :128] = small[p, l, :128]
            gw[p, :, 128:] = small[p, l, 128:256]
            start = pl.multiple_of(256 + seq * 32, 32)
            up[:, at] = small[p, l, pl.ds(start, 32), :]
            start = pl.multiple_of(320 + seq * 16, 16)
            down_out[:, at] = small[p, l, pl.ds(start, 16), :]
            parts = [small[p, l, 352 + 16 * i : 368 + 16 * i].astype(F32) for i in range(3)]
            total = parts[0] + parts[1] + parts[2]
            params[:, at] = total[:8]
            params[7:8, at] = -8.0 * jax.nn.softplus(total[7:8])


def join_kernel(w, a, held, wide, sem):
    copies = []
    for j in range(4):
        copy = pltpu.make_async_copy(w.at[j, pl.ds(864, 32)], held.at[j], sem.at[j])
        copy.start()
        copies.append(copy)
    wait_all(copies)
    for j in range(4):
        for i in range(3):
            part = held[j, :, i * 384 : i * 384 + 288].astype(F32)
            wide[i * 32 : i * 32 + 32, j * 288 : j * 288 + 288] = part
    a[...] = wide[...].astype(BF)


def order_kernel(sc, b0, b1, b2, b3, out):
    for j, block in enumerate((b0, b1, b2, b3)):
        out[lax.rem(sc[2] + 4 - j, 4)] = block[...]


def order_x_kernel(sc, b0, b1, b2, b3, out):
    for j, block in enumerate((b0, b1, b2, b3)):
        out[lax.rem(sc[0] + 4 - j, 4)] = block[...]


def unpack_kernel(sc, b0, b1, b2, b3, inputs, last, act, pull, held):
    for j, block in enumerate((b0, b1, b2, b3)):
        held[lax.rem(sc[2] + j, 4)] = block[...]
    for p in range(4):
        at = slice(p * 128, p * 128 + 128)
        inputs[:, at] = held[p, :, 128:]
        act[:, at], pull[:, at] = gelu_pair(held[p, :, :128].astype(F32))
    last[...] = inputs[BLOCK - 16 :]


def pack_kernel(a_ref, b_ref, c_ref, d_ref, out):
    at = 0
    for ref in (a_ref, b_ref, c_ref, d_ref):
        count = ref.shape[1]
        out[at : at + count] = ref[0]
        at += count


def pack(l, parts):
    width = parts[0].shape[2]
    total = sum(part.shape[1] for part in parts)
    return pl.pallas_call(
        pack_kernel,
        out_shape=jax.ShapeDtypeStruct((total, width), BF),
        grid=(2,),
        in_specs=[pl.BlockSpec((1, p.shape[1], width // 2), lambda i: (l, 0, i)) for p in parts],
        out_specs=pl.BlockSpec((total, width // 2), lambda i: (0, i)),
        compiler_params=pltpu.CompilerParams(vmem_limit_bytes=LIMIT),
        cost_estimate=pl.CostEstimate(flops=0, bytes_accessed=5 * 10**6, transcendentals=0),
        name="pack",
    )(*parts)


def pair_kernel(a_ref, b_ref, out):
    out[:128] = a_ref[0].T
    out[128:] = b_ref[0].T


def pair_of(l, a, b):
    rows = a.shape[1] // 3
    piece = pl.BlockSpec((1, rows, 128), lambda i: (l, i, 0))
    return pl.pallas_call(
        pair_kernel,
        out_shape=jax.ShapeDtypeStruct((256, a.shape[1]), BF),
        grid=(3,),
        in_specs=[piece] * 2,
        out_specs=pl.BlockSpec((256, rows), lambda i: (0, i)),
        compiler_params=pltpu.CompilerParams(vmem_limit_bytes=LIMIT),
        cost_estimate=pl.CostEstimate(flops=0, bytes_accessed=2 * 10**6, transcendentals=0),
        name="pair",
    )(a, b)


def half_kernel(sc, a_ref, b_ref, c_ref, out):
    @pl.when(sc[4] == 0)
    def _():
        out[:128] = a_ref[0].T
        out[128:] = b_ref[0, :, :].T[:64]

    @pl.when(sc[4] == 1)
    def _():
        out[:64] = b_ref[0, :, :].T[64:]
        out[64:] = c_ref[0]


def half_of(scalars, l, a, b, c):
    rows = a.shape[1] // 3
    piece = pl.BlockSpec((1, rows, 128), lambda i, sc: (l, i, 0))
    return pl.pallas_call(
        half_kernel,
        out_shape=jax.ShapeDtypeStruct((192, a.shape[1]), BF),
        grid_spec=pltpu.PrefetchScalarGridSpec(
            num_scalar_prefetch=1,
            grid=(3,),
            in_specs=[piece] * 2 + [pl.BlockSpec((1, 128, rows), lambda i, sc: (l, 0, i))],
            out_specs=pl.BlockSpec((192, rows), lambda i, sc: (0, i)),
        ),
        compiler_params=pltpu.CompilerParams(vmem_limit_bytes=LIMIT),
        cost_estimate=pl.CostEstimate(flops=0, bytes_accessed=2 * 10**6, transcendentals=0),
        name="half",
    )(scalars, a, b, c)


def finish_kernel(ranked, sc, *refs):
    mix_d, mix_u, out_d, out_u, ffn_d, ffn_u, back_d, back_u, whole, shard, split = refs[-11:]
    a = pl.program_id(0)

    @pl.when(a == 0)
    def _():
        for c in range(2):
            for y in range(4):
                for x in range(4):
                    if ranked:
                        mine, other = (ref[y * 4 + x].astype(F32) for ref in refs[:2])
                        v = jnp.where(sc[2] == c, mine, other)
                    else:
                        v = refs[0][c, y, x].astype(F32)
                    row = c * 24 + (y % 2) * 12
                    for k in range(3):
                        lane = x * 384 + k * 128
                        whole[c, y * 12 : y * 12 + 12, lane : lane + 128] = v[
                            k * 12 : k * 12 + 12
                        ]
                        whole[y // 2, 48 + row : 60 + row, lane : lane + 128] = v[
                            144 + k * 12 : 156 + k * 12
                        ]
                    lane = (y * 4 + x) * 288
                    for k in range(2):
                        shard[c * 48 : c * 48 + 48, lane + k * 128 : lane + k * 128 + 128] = v[
                            36 + k * 48 : 84 + k * 48
                        ]
                    for k in range(4):
                        at = c * 48 + k * 12
                        shard[at : at + 12, lane + 256 : lane + 288] = v[
                            132:144, k * 32 : k * 32 + 32
                        ]
                    for p in range(4):
                        lane = (p * 4 + x) * 128
                        k = 144 + (3 + p) * 12
                        split[y // 2, row : row + 12, lane : lane + 128] = v[k : k + 12]

    w = [((sc[s] == sc[0]) == (sc[a] == sc[0])).astype(F32) for s in range(2)]
    both = lambda get: get(0) * w[0] + get(1) * w[1]
    ffn_d[0, 0] = both(lambda s: whole[s, :32])
    back_u[0, 0] = both(lambda s: whole[s, 32:48])
    mix_d[0, 0] = both(lambda s: whole[s, 48:80])
    out_u[0, 0] = both(lambda s: whole[s, 80:])
    ffn_u[0, 0, :16] = both(lambda s: shard[s * 16 : s * 16 + 16])
    ffn_u[0, 0, 16:] = both(lambda s: shard[32 + s * 16 : 48 + s * 16])
    back_d[0, 0] = both(lambda s: shard[64 + s * 16 : 80 + s * 16])
    mix_u[0, 0] = both(lambda s: split[s, :32])
    out_d[0, 0] = both(lambda s: split[s, 32:])


TABLES = [(32, 1536), (32, 2048), (16, 2048), (16, 1536), (32, 1536), (32, 4608), (16, 4608)]
TABLES.append((16, 1536))


def zeros_kernel(after, *refs):
    del after
    for ref in refs:
        ref[...] = jnp.zeros(ref.shape, F32)


def empty_tables(after):
    return pl.pallas_call(
        zeros_kernel,
        out_shape=[jax.ShapeDtypeStruct((2, 8) + shape, F32) for shape in TABLES],
        grid=(2, 4),
        in_specs=[SMEM],
        out_specs=[pl.BlockSpec((1, 2) + shape, lambda l, a: (l, a, 0, 0)) for shape in TABLES],
        compiler_params=pltpu.CompilerParams(vmem_limit_bytes=LIMIT),
        cost_estimate=pl.CostEstimate(flops=10**6, bytes_accessed=20 * 10**6, transcendentals=0),
        name="zeros",
    )(after)


def finish(ids, layer, flats, tables):
    return pl.pallas_call(
        functools.partial(finish_kernel, len(flats) == 2),
        out_shape=[jax.ShapeDtypeStruct((2, 8) + shape, F32) for shape in TABLES],
        grid_spec=pltpu.PrefetchScalarGridSpec(
            num_scalar_prefetch=1,
            grid=(2,),
            in_specs=[VMEM] * len(flats) + [HBM] * len(tables),
            out_specs=[
                pl.BlockSpec((1, 1) + shape, lambda a, sc: (layer, sc[a], 0, 0))
                for shape in TABLES
            ],
            scratch_shapes=[
                pltpu.VMEM((2, 96, 1536), F32),
                pltpu.VMEM((96, 4608), F32),
                pltpu.VMEM((2, 48, 2048), F32),
            ],
        ),
        input_output_aliases={1 + len(flats) + i: i for i in range(len(tables))},
        compiler_params=pltpu.CompilerParams(vmem_limit_bytes=LIMIT),
        cost_estimate=pl.CostEstimate(flops=10**7, bytes_accessed=4 * 10**6, transcendentals=0),
        name="finish",
    )(ids, *flats, *tables)


def widen_kernel(v, out):
    out[...] = v[...].astype(F32)


def widen(v):
    rows, width = v.shape
    spec = pl.BlockSpec((BLOCK, width), lambda i: (i, 0))
    return pl.pallas_call(
        widen_kernel,
        out_shape=jax.ShapeDtypeStruct(v.shape, F32),
        grid=(rows // BLOCK,),
        in_specs=[spec],
        out_specs=spec,
        cost_estimate=pl.CostEstimate(flops=10**6, bytes_accessed=10**7, transcendentals=0),
        name="widen",
    )(v)


def other_core(z, c, y, x):
    return (z, 1 - c, y, x)


def other_half(z, c, y, x):
    return (z, c, y ^ 1, x)


def along_z(d):
    return lambda z, c, y, x: ((z + d) % 4, c, y, x)


def halves(value, index, move):
    count = value.shape[0] // 2
    mine = lax.dynamic_slice_in_dim(value, index * count, count, 0)
    theirs = lax.dynamic_slice_in_dim(value, (1 - index) * count, count, 0)
    return mine.astype(F32) + send(theirs, move).astype(F32)


def ring_scatter(value, index, moves, axis):
    count = value.shape[axis] // 4
    parts = [
        lax.dynamic_slice_in_dim(value, ((index - j) % 4) * count, count, axis) for j in range(4)
    ]
    return scatter4(parts, moves)


def sum_z(value):
    low = value.astype(BF)
    total = value
    for d in (1, 2, 3):
        total = total + send(low, along_z(d)).astype(F32)
    return total.astype(BF)


def blocks_of(v, rows):
    n, width = v.shape
    v = jnp.pad(v, ((0, rows - n), (0, -width % 128)))
    return jnp.concatenate([v[:, i : i + 128] for i in range(0, width, 128)], axis=0)


def shard_rows(v):
    rest = jnp.concatenate([v[i * 12 : i * 12 + 12, 256:] for i in range(4)], axis=1)
    return jnp.concatenate([v[:, :128], v[:, 128:256], rest], axis=0)


def reduce_shards(split):
    core, x, y = lax.axis_index("core"), lax.axis_index("x"), lax.axis_index("y")
    group = jnp.where(core == 0, y, x)
    shard = split.astype(BF).reshape(96, 4, 288).transpose(1, 0, 2)
    return ring_scatter(shard, group, ffn_shards, 0)[0]


def reduce_steps(mine, theirs):
    x, y = lax.axis_index("x"), lax.axis_index("y")
    part = mine + send(theirs, other_core).astype(F32)
    part = yield part
    split = jnp.concatenate([part[72:, i * 512 : i * 512 + 512] for i in range(3)], axis=0)
    whole = ring_scatter(part[:72].astype(BF), x, along_x, 1)
    whole, split = yield whole, split
    mix = jnp.concatenate([whole[48:], split], axis=1)
    pieces = []
    for q in range(4):
        here = jnp.where(y // 2 == q // 2, mix[(q % 2) * 12 : (q % 2) * 12 + 12], 0.0)
        pieces.append(jnp.concatenate([whole[q * 12 : q * 12 + 12], here], axis=1))
    part = ring_scatter(jnp.stack(pieces).astype(BF), y, along_y, 0)[0]
    yield blocks_of(part, 12)


def shards(
    tokens,
    cotangent,
    lengths,
    adapter_ids,
    mix_gain,
    ffn_gain,
    w_branch,
    input_weight,
    conv_weight,
    conv_bias,
    gate_a_weight,
    gate_a_bias,
    gate_i_weight,
    gate_i_bias,
    decay_param,
    w_out,
    w_gate,
    w_up,
    w_down,
    mix_down,
    mix_up,
    out_down,
    out_up,
    ffn_down,
    ffn_up,
    back_down,
    back_up,
):
    width = tokens.shape[2]
    z, core = lax.axis_index("z"), lax.axis_index("core")
    y, x = lax.axis_index("y"), lax.axis_index("x")
    seq, half = y // 2, y % 2
    out = lax.dynamic_slice(w_out, (0, core * 64, 0), (1, 64, width))[0]
    w_back = lax.all_gather(out, "y")
    w_back = [w_back, send(w_back, other_core)]
    ids = adapter_ids
    ffn_group = jnp.where(core == 0, y, x)
    first = (z + core + half == 0).astype(jnp.int32)
    scalars = jnp.stack([x, first, y, ffn_group, core]).astype(jnp.int32)
    turned = lambda v: jnp.swapaxes(v, -1, -2)
    mix_down_t = turned(mix_down)
    mix_up_f = mix_up.reshape(2, 8, 32, 128)
    *local, normed_0, lat_b_0, lat_i_0 = head(
        jnp.stack([y, ids[0], ids[1]]),
        tokens,
        mix_down_t,
        mix_up_f,
        mix_gain,
        w_branch,
        input_weight,
    )
    mine = local[0]
    local = deal4(local, along_y)
    ffn_parts = [turned(w_gate), turned(w_up), w_down]
    gather_ffn = lambda v: lax.all_gather(v, ALL, axis=0, axis_index_groups=shard_groups())
    picked, mine = tie(ids, mine)
    prepared = prepare(
        jnp.concatenate([picked, lax.dynamic_index_in_dim(picked, seq, 0)]),
        [mix_down_t, out_up],
        [
            turned(ffn_down), back_up, mix_up_f, turned(out_down),
            ffn_up.reshape(2, 8, 32, 288), turned(back_down),
        ],
        [gate_a_weight, gate_i_weight, conv_weight],
        [conv_bias, gate_a_bias, gate_i_bias, decay_param],
    )
    mix_d, out_u, ffn_d, back_u = (prepared[i : i + 2] for i in (0, 2, 4, 6))
    small, ffn_small = prepared[8:]
    more, mine = tie(ffn_parts, mine)
    ffn_parts.append(ffn_small)
    packed, local = tie(pack(0, more + [ffn_small]), local)
    ffn_w = [gather_ffn(packed), None]
    arranged = call(
        arrange_kernel,
        "arrange",
        gather4(small, along_y),
        [((4, 128, 256), BF), ((32, 512), BF), ((16, 512), BF), ((8, 512), F32)] * 2,
        [pltpu.VMEM((4, 2, 400, 128), BF)],
        scalars,
    )
    w_mix = {}
    start = (seq, half * BLOCK + x * HOME, 0)
    residual = lax.dynamic_slice(tokens, start, (1, HOME, width))[0]
    position = (z * 2 + core) * 512 + half * BLOCK + x * HOME + jnp.arange(HOME)
    valid = (position < lengths[seq]).astype(F32)[:, None]
    of_rows = jnp.where(core == 0, y, (y - jnp.arange(4)) % 4) // 2
    of_rows = jnp.repeat(of_rows, HOME)[:, None]
    of_cols = jnp.arange(32) // RANK
    mask = (of_rows == of_cols[None, :]).astype(F32)
    rows_like = [((HOME, width), BF)] * 4
    group_sem = pltpu.SemaphoreType.DMA((2, 4))
    ffn_sem = pltpu.SemaphoreType.DMA((3, 4))
    ffn_buffers = [pltpu.VMEM((1152, width), BF)] * 3
    mix_buffer = pltpu.VMEM((512, width), BF)
    half_f = ((BLOCK, 512), F32)
    pair_f = ((2, BLOCK, 512), F32)
    half_b = ((BLOCK, 512), BF)
    low_b = ((BLOCK, RANK), BF)

    kept = []
    for l in range(2):
        k = {"residual": residual}
        down, up_out = mix_d[l], out_u[l]
        gw, up, down_out, params = arranged[l * 4 : l * 4 + 4]
        if l == 0:
            normed, lat_b, lat_i = normed_0, lat_b_0, lat_i_0
            inputs, last, act, pull = call(
                unpack_kernel,
                "unpack",
                local,
                [half_b, ((16, 512), BF), half_f, half_f],
                [pltpu.VMEM((4, BLOCK, 256), BF)],
                scalars,
            )
            halo = send(last, next_block(False))
        else:
            blocks = gather4(normed_low, along_x)
            packed, _ = tie(packed, (mine, blocks))
            ffn_w[1] = gather_ffn(packed)
            w_mix[1] = [mine, send(mine, other_core)]
            normed, inputs, last, lat_b, lat_i = mixer(
                inputs_kernel,
                "inputs",
                [*blocks, down, up],
                [((BLOCK, width), BF), half_b, ((16, 512), BF), low_b, low_b],
                [mix_buffer, group_sem],
                scalars,
                w_mix[l],
            )
            halo = send(last, next_block(False))
            act, pull = mixer(
                branch_kernel,
                "branch",
                [normed, lat_b, up],
                [half_f, half_f],
                [mix_buffer, group_sem],
                scalars,
                w_mix[l],
            )
        saved, decay, scan, ends = call(
            gates_kernel,
            "gates",
            [inputs, halo, params, gw],
            [((3, BLOCK, 512), F32), half_f, pair_f, ((2, 512), F32)],
            [pltpu.VMEM((BLOCK + 16, 512), F32), pltpu.VMEM((BLOCK, 512), F32)],
            scalars,
        )
        carry = entering(ends, core, half, False)
        w_back_l = w_back if l == 0 else w_mix[1]
        states, mixed, out_latent, *parts = mixer(
            mixed_kernel,
            "mixed",
            [carry, scan, act, down_out, up_out],
            [half_f, half_b, low_b] + rows_like,
            [mix_buffer, pltpu.VMEM((BLOCK, width), BF), group_sem],
            scalars,
            w_back_l,
        )
        if l == 0:
            (halves_of, more), _ = tie(((w_branch, input_weight, w_out), ffn_parts), parts[0])
            mine, packed = half_of(scalars, 1, *halves_of), pack(1, more)
        parts = deal4(parts, along_x)
        if l == 1:
            parts, w_pair = tie(parts, pair_of(0, w_branch, input_weight))
        residual, normed_low = call(
            functools.partial(add_norm_kernel, l),
            "add_norm",
            [*parts, residual, ffn_gain],
            [((HOME, width), F32), ((HOME, width), BF)],
        )
        k.update(
            down=down, up=up, down_out=down_out, up_out=up_out, gw=gw, params=params,
            normed=normed, lat_b=lat_b, lat_i=lat_i, act=act, pull=pull, saved=saved, decay=decay, ends=ends,
            carry=carry, states=states, mixed=mixed, out_latent=out_latent,
            residual_one=residual,
        )
        if l == 1:
            grad = lax.dynamic_slice(cotangent, start, (1, HOME, width))[0] * valid
            grad_low, _ = tie(grad.astype(BF), carry)
            grad_blocks = gather4(grad_low, ffn_rows)
        blocks = gather4(normed_low, ffn_rows)
        if l == 0:
            mine, _ = tie(mine, (ffn_w[0], normed_low))
            mine = lax.all_gather(mine, "y")
        down, up_back = ffn_d[l], back_u[l]
        (ffn_a,) = call(
            join_kernel,
            "join",
            [],
            [((96, 1152), BF)],
            [
                pltpu.VMEM((4, 32, width), BF), pltpu.VMEM((96, 1152), F32),
                pltpu.SemaphoreType.DMA((4,)),
            ],

            far=[ffn_w[l]],
        )
        gate, ups = None, None
        if l == 0:
            gate, ups, hidden, latent, back_latent, *parts = call(
                ffn_kernel,
                "ffn",
                [*blocks, ffn_a, down, up_back, mask],
                [((BLOCK, 1152), F32)] * 2
                + [((BLOCK, 1152), BF), ((2, BLOCK, 32), BF), ((BLOCK, 32), BF)]
                + rows_like,
                [pltpu.VMEM((BLOCK, width), BF)] + ffn_buffers + [ffn_sem],
                far=[ffn_w[l]],
                mflops=2800,
                mbytes=15,
            )
        else:
            hidden, latent, back_latent, *turned_back = call(
                ffn_turn_kernel,
                "ffn_turn",
                [*blocks, *grad_blocks, ffn_a, down, up_back, mask],
                [((BLOCK, 1152), BF), ((2, BLOCK, 32), BF), ((BLOCK, 32), BF)]
                + [((BLOCK, 1152), BF)] * 2
                + [((BLOCK, 32), BF), ((2, BLOCK, 32), BF), ((BLOCK, width), BF)]
                + [((2 * HOME, width), BF)] * 4,
                [pltpu.VMEM((BLOCK, width), BF)] + ffn_buffers + [ffn_sem],
                far=[ffn_w[l]],
                mflops=5600,
                mbytes=15,
            )
            g_gate, g_up, g_back, g_latent, rows, *parts = turned_back
        k.update(
            ffn_a=ffn_a, down_two=down, up_back=up_back, blocks=blocks, gate=gate, ups=ups, hidden=hidden,
            latent=latent, back_latent=back_latent,
        )
        if l == 0:
            after, _ = tie(scalars, parts[0])
            parts, tables = tie(deal4(parts, ffn_rows), empty_tables(after))
            residual, normed_low = call(
                functools.partial(add_norm_kernel, 1),
                "add_norm",
                [*parts, residual, mix_gain],
                [((HOME, width), F32), ((HOME, width), BF)],
            )
        kept.append(k)
    for l in (1, 0):
        k = kept[l]
        w_back_l, w_in_l = (w_back, [w_in]) if l == 0 else (w_mix[1], w_mix[1])
        if l == 0:
            blocks = gather4(grad_low, ffn_rows)
            blocks, side = tie(blocks, side)
            side = steps.send(side)
            g_gate, g_up, g_back, g_latent, rows, *parts = call(
                ffn_back_kernel,
                "ffn_back",
                [*blocks, k["ffn_a"], k["down_two"], k["up_back"], mask, k["gate"], k["ups"]],
                [((BLOCK, 1152), BF)] * 2
                + [((BLOCK, 32), BF), ((2, BLOCK, 32), BF), ((BLOCK, width), BF)]
                + rows_like,
                ffn_buffers + [ffn_sem],
                far=[ffn_w[l]],
                mflops=2800,
                mbytes=15,
            )
        if l == 0:
            parts, side = tie(parts, side)
        parts = deal4(parts, ffn_rows)
        if l == 0:
            side, parts[1] = tie(side, parts[1])
            side = steps.send(side)
        ffn_whole, ffn_split = call(
            ffn_adapters_kernel,
            "ffn_adapters",
            [
                *k["blocks"], rows, k["latent"], k["back_latent"], k["hidden"], g_gate, g_up,
                g_back, g_latent,
            ],
            [((96, width), BF), ((96, 1152), BF)],
            [pltpu.VMEM((BLOCK, width), BF)],
            mflops=200,
        )
        parts, (ffn_whole, ffn_split) = tie(parts, (ffn_whole, ffn_split))
        out_parts = parts
        grad, grad_low = call(
            functools.partial(norm_back_kernel, l),
            "norm_back",
            [*parts, grad, k["residual_one"], ffn_gain],
            [((HOME, width), F32), ((HOME, width), BF)],
        )
        blocks = gather4(grad_low, along_x)
        if l == 1:
            (out_parts, shard_part), _ = tie((out_parts, ffn_split), grad_low)
            (output,) = call(
                output_kernel, "output", [*out_parts, residual, valid], [((HOME, width), BF)]
            )
            output = lax.all_gather(output, ("y", "x"), axis=0, tiled=True)
            shard_part = reduce_shards(shard_part)
        else:
            flat = jnp.concatenate([side[:36], shard_1, side[36:]], axis=0)
            flat, _ = tie(flat, grad_low)
            flat = sum_z(flat)
        rows, g_mixed, g_low, back, ends = mixer(
            states_back_kernel,
            "states_back",
            [*blocks, k["down_out"], k["up_out"], k["act"], k["decay"], k["ends"]],
            [((BLOCK, width), BF), half_b, low_b, pair_f, ((2, 512), F32)],
            [mix_buffer, pltpu.VMEM((BLOCK + 8, 512), F32), pltpu.VMEM((BLOCK, 512), F32)]
            + [group_sem],
            scalars,
            w_back_l,
        )
        if l == 1:
            ends, shard_part = tie(ends, shard_part)
        else:
            ends, (flat, output) = tie(ends, (flat, output))
            flat = lax.all_gather(flat, ("core", "y", "x")).reshape(2, 4, 4, 228, 128)
        if l == 1:
            w_pair, _ = tie(w_pair, ends)
            w_in = lax.all_gather(w_pair, "y")
        carry = entering(ends, core, half, True)
        part, g_up_out, g_down_out, g_up_b, g_low_b = mixer(
            branch_back_kernel,
            "branch_back",
            [
                rows, g_mixed, g_low, k["states"], k["pull"], k["mixed"], k["out_latent"],
                k["lat_b"], k["up"], k["down"],
            ],
            [((BLOCK, width), F32), ((RANK, width), F32), ((RANK, 512), F32), ((RANK, 512), F32)]
            + [low_b],
            [mix_buffer, group_sem],
            scalars,
            w_in_l,
        )
        carry, part = tie(carry, part)
        if l == 1:
            shard_part, _ = tie(shard_part, carry)
            shard_1 = halves(shard_part, core, other_core)

        g_conv, rim = call(
            gates_back_kernel,
            "gates_back",
            [
                carry, k["carry"], back, k["states"], k["saved"], k["decay"], k["params"],
                k["gw"],
            ],
            [half_f, ((8, 512), F32)],
            [pltpu.VMEM((BLOCK + 8, 512), F32)],
            scalars,
        )
        halo = send(rim, next_block(True))
        if l == 1:
            halo, shard_1 = tie(halo, shard_1)
            shard_1 = shard_rows(shard_1)
        *parts, mine, theirs = mixer(
            inputs_back_kernel,
            "inputs_back",
            [
                g_conv, halo, k["params"], k["up"], k["down"], part, k["normed"], k["lat_i"],
                g_low_b, g_up_b, g_up_out, g_down_out, ffn_whole,
            ],
            rows_like + [((80, width), F32), ((80, width), BF)],
            [
                pltpu.VMEM((BLOCK + 8, 512), F32), mix_buffer, pltpu.VMEM((BLOCK, width), BF),
                pltpu.VMEM((48, width), F32), pltpu.VMEM((48, 512), F32),
                pltpu.VMEM((2, 80, width), F32), group_sem,
            ],
            scalars,
            w_in_l,
        )
        parts = deal4(parts, along_x)
        steps = reduce_steps(mine, theirs)
        side = next(steps)
        if l == 0:
            parts, output = tie(parts, widen(output))
        grad, grad_low = call(
            functools.partial(norm_back_kernel, l),
            "norm_back",
            [*parts, grad, k["residual"], mix_gain],
            [((HOME, width), F32), ((HOME, width), BF)],
        )
    grad_tokens = lax.all_gather(grad_low, ("y", "x"), axis=0, tiled=True)
    shard_0, _ = tie(ffn_split, grad_low)
    shard_0 = reduce_shards(shard_0)
    side, shard_0 = tie(steps.send(side), shard_0)
    shard_0 = shard_rows(halves(shard_0, core, other_core))
    side = steps.send(side)
    last = jnp.concatenate([side[:36], shard_0, side[36:]], axis=0)
    last = sum_z(last)
    last, (tables, output) = tie(last, (finish(ids, 1, [flat], tables), output))
    last = lax.all_to_all(jnp.broadcast_to(last, (16, 228, 128)), ("y", "x"), 0, 0, tiled=True)
    grad_tokens, _ = tie(grad_tokens, last)
    other, grad_tokens = tie(send(last, other_core), widen(grad_tokens))
    last = last, other
    ids = jnp.concatenate([ids, core[None].astype(jnp.int32)])
    gmd, gmu, god, gou, gfd, gfu, gbd, gbu = finish(ids, 0, last, tables)
    return (
        output.reshape(tokens.shape),
        grad_tokens.reshape(tokens.shape),
        turned(gmd),
        gmu.reshape(2, 8, 2, RANK, 2048),
        turned(god),
        gou,
        turned(gfd),
        gfu.reshape(2, 8, 2, RANK, 4608),
        turned(gbd),
        gbu,
    )


def solution(mesh):
    grid = Mesh(mesh.devices.reshape(4, 2, 4, 4), ALL)
    sp, mp = ("z", "core"), ("y", "x")
    in_specs = (
        P(None, sp, None),
        P(None, sp, None),
        P(),
        P(),
        P(),
        P(),
        P(None, None, mp),
        P(None, None, mp),
        P(None, None, mp),
        P(None, mp),
        P(None, mp, None, None),
        P(None, mp),
        P(None, mp, None, None),
        P(None, mp),
        P(None, mp),
        P(None, mp, None),
        P(None, None, mp),
        P(None, None, mp),
        P(None, mp, None),
        P(),
        P(None, None, None, None, mp),
        P(None, None, mp, None),
        P(),
        P(),
        P(None, None, None, None, mp),
        P(None, None, mp, None),
        P(),
    )
    out_specs = (P(None, sp, None), P(None, sp, None)) + (P(),) * 8
    return jax.shard_map(shards, mesh=grid, in_specs=in_specs, out_specs=out_specs, check_vma=False)
```
